32 devices in a mesh: side: 2 (over core), dev: 16 (over z, y, x).
Axes of the slice: x: 2, y: 2, z: 4, core: 2. Of those that a mesh axis runs over, the one named last changes fastest.
Arguments:
- queries: bfloat16 [256, 64, 576], P('dev'), may hold values from -18 to 18
- latent_cache: bfloat16 [256, 768, 576], P('dev', 'side'), may hold values from -18 to 18
- lengths: int32 [256], P('dev'), may hold values from 64 to 768, as said below
- value_lift: bfloat16 [64, 512, 128], P('side'), may hold values from -0.25 to 0.25
- output_map: bfloat16 [8192, 7168], P('side', 'dev'), may hold values from -0.5 to 0.5
- residual: bfloat16 [256, 7168], P(('side', 'dev')), may hold values from -6 to 6
- norm_gain: bfloat16 [7168], replicated, may hold values from 0.099609375 to 1.8984375
- expert_ids: int32 [256, 8], P(('side', 'dev')), may hold values from 0 to 7, all different within a row; in each aligned block of 8 rows (0 to 7, 8 to 15, ...) at most 8 rows name the same one
- gate_values: float32 [256, 8], P(('side', 'dev')), may hold values from 0.1 to 0.8
- expert_in: bfloat16 [16, 7168, 2, 512], P('dev', None, None, 'side'), may hold values from -0.0625 to 0.0625
- expert_down: bfloat16 [16, 512, 7168], P('dev', 'side'), may hold values from -0.1875 to 0.1875
Outputs:
- layer_out: bfloat16 [256, 7168], P(('side', 'dev'))
The draws below stay inside these ranges and needn't reach their ends.
Inputs may be any that keep to these rules, and one draw needn't show every extreme that they name: `lengths`: request 0 has all 768 slots live. `expert_ids`: within the rows of one device (aligned blocks of 8 rows) no expert is chosen by more than 8 rows, and some expert is chosen by exactly 8 rows in some blocks.
All inputs are finite; a program needn't handle non-finite values.
Results may differ from the reference program's by a relative error of at most 0.02.
Values may be sent and summed in bfloat16 or wider, within the bound.
No kernel may reach another device: no remote copies, remote signals or barrier semaphores. Data moves between devices by JAX's collectives and lax.ppermute only.
A program may use at most 128 MiB of HBM per device.

```python
import math
import jax
import jax.numpy as jnp
import numpy as np
from jax import lax

D = 7168
H = 64
LAT = 512
ROPE = 64
VH = 128
QKD = 192
FFW = 1024
TOP = 8
LEN = 768
REQS = 256
TOK_DEV = 8
EXPERTS = 8
CAP = 8


def draw_queries(key, part):
    values = jax.random.normal(jax.random.fold_in(key, 1), (REQS, H, LAT + ROPE), jnp.float32)
    return jnp.clip(values, -18.0, 18.0).astype(jnp.bfloat16)


def draw_latent_cache(key, part):
    values = jax.random.normal(jax.random.fold_in(key, 2), (REQS, LEN, LAT + ROPE), jnp.float32)
    return jnp.clip(values, -18.0, 18.0).astype(jnp.bfloat16)


def draw_lengths(key, part):
    lowest = max(6, LEN // 12)
    drawn = jax.random.randint(jax.random.fold_in(key, 3), (REQS,), lowest, LEN + 1, dtype=jnp.int32)
    return drawn.at[0].set(LEN)


def levels(own_key, extent, shards, smallest, largest):
    loudness = 1.0
    for axis_at, shards_of in shards:
        heights = jax.random.uniform(jax.random.fold_in(jax.random.fold_in(own_key, 6), axis_at), (shards_of,), jnp.float32, smallest / len(shards), largest / len(shards))
        loudness = loudness * jnp.repeat(jnp.exp(heights), extent[axis_at] // shards_of).reshape((-1,) + (1,) * (len(extent) - 1 - axis_at))
    return loudness


def assign_block(stream_key, own, number, rows, count, top, reach, lean):
    order = jax.random.permutation(stream_key, count)
    heavy_load, ordinary = shares(count, rows * top, reach, lean, True), shares(count, rows * top, reach, lean, False)
    places = jnp.arange(count)

    def named(tallies, rotation):
        used = int((tallies > 0).sum())
        fixed = max(1, used // 4)
        passed = fixed + (places - fixed + rotation * (used - fixed)) % max(1, count - fixed)
        return jnp.zeros((count,), jnp.int32).at[order[jnp.where(places < fixed, places, passed)]].set(jnp.asarray(tallies, jnp.int32))

    tallies = jnp.where(number % 4 == 0, named(heavy_load, number // 4), named(ordinary, number - number // 4 - 1))
    mixed = jax.random.permutation(jax.random.fold_in(own, 3), count)
    donor, receiver = mixed[0:count // 2 * 2:2], mixed[1:count // 2 * 2:2]
    room = jnp.minimum(tallies[donor] - 1, reach - tallies[receiver]) // 2
    room = jnp.where((donor == order[0]) | (receiver == order[0]) | (tallies[receiver] == 0), 0, jnp.maximum(room, 0))
    passed = jax.random.randint(jax.random.fold_in(own, 4), (count // 2,), 0, 1 << 20) % (room + 1)
    tallies = tallies.at[donor].add(-passed).at[receiver].add(passed)
    labels = jnp.searchsorted(jnp.cumsum(tallies), jnp.arange(rows * top), side="right").astype(jnp.int32)
    table = labels.reshape(top, rows).T
    table = table[jax.random.permutation(jax.random.fold_in(own, 1), rows)]
    rotation = jax.random.randint(jax.random.fold_in(own, 2), (rows, 1), 0, top)
    return jnp.take_along_axis(table, (jnp.arange(top)[None, :] + rotation) % top, axis=1)


def shares(number_of, total, bound, lean, full):
    loads = [(1 << 20) // math.isqrt(grade ** lean) + 1 for grade in range(1, number_of + 1)]
    largest = bound if full else min(bound, max(-(-total // number_of), total * loads[0] // sum(loads)))
    least = 1 if total - largest >= number_of - 1 else 0
    holding, surplus = [largest] + [least] * (number_of - 1), total - largest - least * (number_of - 1)
    while surplus > 0:
        candidates = [i for i in range(1, number_of) if holding[i] < largest] or [i for i in range(1, number_of) if holding[i] < bound]
        whole, left = sum([loads[i] for i in candidates]), surplus
        for i in candidates:
            addition = min(bound - holding[i], max(1, left * loads[i] // whole), surplus)
            holding[i] = holding[i] + addition
            surplus = surplus - addition
    return np.array(holding)


def gaussian(stream_key, dims, spread, reach, cuts=(), kind=jnp.bfloat16):
    factor_of = levels(stream_key, dims, cuts, -0.22, 0.18) if cuts else 1.0
    values = jax.random.normal(stream_key, dims, jnp.float32) * spread * factor_of
    return jnp.minimum(jnp.maximum(values, -reach), reach).astype(kind)


def setup_inputs(seed: int = 0) -> dict:
    splits = jax.random.split(jax.random.key(seed), 12)
    queries = draw_queries(jax.random.fold_in(splits[11], 71), 0)
    latent_cache = draw_latent_cache(jax.random.fold_in(splits[11], 71), 0)
    lengths = draw_lengths(jax.random.fold_in(splits[11], 71), 0)
    value_lift = gaussian(splits[3], (H, LAT, VH), LAT ** -0.5, 0.25, ((0, 2),))
    output_map = gaussian(splits[4], (H * VH, D), (H * 2) ** -0.5, 0.5, ((0, 2), (1, 16)))
    residual = gaussian(splits[5], (REQS, D), 1.0, 6.0, ((0, 32),))
    norm_gain = jnp.clip(1.0 + 0.18 * jax.random.normal(splits[6], (D,), jnp.float32), 0.099609375, 1.8984375).astype(jnp.bfloat16)
    expert_ids_keys = jax.random.split(jax.random.fold_in(splits[7], 1), REQS // TOK_DEV)
    expert_ids_turns = jax.random.permutation(jax.random.fold_in(splits[7], 3), REQS // TOK_DEV)
    expert_ids = jax.vmap(lambda own, number: assign_block(jax.random.fold_in(splits[7], 2), own, number, TOK_DEV, EXPERTS, TOP, CAP, 2))(expert_ids_keys, expert_ids_turns).reshape((REQS, TOP))
    gate_values = jnp.clip(jnp.exp(math.log(0.8) - 2.0794415 * jax.random.uniform(splits[8], (REQS, TOP), jnp.float32) ** levels(splits[8], (REQS, TOP), ((0, 32),), -0.2, 0.2)), 0.1, 0.8)
    expert_in = gaussian(splits[9], (2 * EXPERTS, D, 2, FFW // 2), D ** -0.5, 0.0625, ((0, 16), (3, 2)))
    expert_down = gaussian(splits[10], (2 * EXPERTS, FFW // 2, D), FFW ** -0.5, 0.1875, ((0, 16), (1, 2)))
    return {"queries": queries, "latent_cache": latent_cache, "lengths": lengths, "value_lift": value_lift, "output_map": output_map, "residual": residual, "norm_gain": norm_gain, "expert_ids": expert_ids, "gate_values": gate_values, "expert_in": expert_in, "expert_down": expert_down}


def attend(block):
    query_block, cache_block, length_block = block
    score_scale = QKD ** (-0.5)
    scores = jnp.einsum('rhc,rpc->rhp', query_block.astype(jnp.float32), cache_block.astype(jnp.float32)) * score_scale
    positions = jnp.arange(LEN, dtype=jnp.int32)
    usable = (positions[None, :] < length_block[:, None])[:, None, :]
    masked = jnp.where(usable, scores, -1e+30)
    row_top = lax.optimization_barrier(jnp.max(masked, axis=2, keepdims=True))
    raised = jnp.where(usable, jnp.exp(masked - row_top), 0.0)
    row_total = lax.optimization_barrier(jnp.sum(raised, axis=2))
    probabilities = lax.optimization_barrier(raised.astype(jnp.bfloat16)).astype(jnp.float32)
    latent_sum = jnp.einsum('rhp,rpc->rhc', probabilities, cache_block[:, :, :LAT].astype(jnp.float32))
    return (latent_sum / row_total[:, :, None]).astype(jnp.bfloat16)

def expert_apply(inputs):
    rows_in, gate_up, down_rows = inputs
    wide_rows = rows_in.astype(jnp.float32)
    gate_part = jnp.einsum('rd,jdh->rjh', wide_rows, gate_up[:, :, 0, :].astype(jnp.float32))
    up_part = jnp.einsum('rd,jdh->rjh', wide_rows, gate_up[:, :, 1, :].astype(jnp.float32))
    activated = (jax.nn.silu(gate_part) * up_part).astype(jnp.bfloat16)
    return jnp.einsum('rjh,jhd->rd', activated.astype(jnp.float32), down_rows.astype(jnp.float32)).astype(jnp.bfloat16)

def reference(queries, latent_cache, lengths, value_lift, output_map, residual, norm_gain, expert_ids, gate_values, expert_in, expert_down):
    blocks = REQS // 8
    latent_out = lax.map(attend, (queries.reshape(blocks, 8, H, LAT + ROPE), latent_cache.reshape(blocks, 8, LEN, LAT + ROPE), lengths.reshape(blocks, 8)))
    latent_out = latent_out.reshape(REQS, H, LAT)
    head_values = jnp.einsum('rhc,hcv->rhv', latent_out.astype(jnp.float32), value_lift.astype(jnp.float32))
    head_values = head_values.astype(jnp.bfloat16).reshape(REQS, H * VH)
    attention = jnp.dot(head_values, output_map, preferred_element_type=jnp.float32)
    hidden = (residual.astype(jnp.float32) + attention).astype(jnp.bfloat16)
    hidden_wide = hidden.astype(jnp.float32)
    normed = hidden_wide * lax.rsqrt(lax.optimization_barrier(jnp.mean(hidden_wide * hidden_wide, axis=1, keepdims=True)) + 1e-06)
    normed = (normed * norm_gain.astype(jnp.float32)[None, :]).astype(jnp.bfloat16)
    source_count = REQS // TOK_DEV
    pair_ids = expert_ids.reshape(source_count, TOK_DEV * TOP)
    expert_hits = (pair_ids[:, :, None] == jnp.arange(EXPERTS, dtype=jnp.int32)[None, None, :]).astype(jnp.int32)
    before = jnp.cumsum(expert_hits, axis=1) - expert_hits
    slot_index = lax.optimization_barrier(jnp.sum(before * expert_hits, axis=2)).astype(jnp.int32)
    token_of = jnp.repeat(jnp.arange(TOK_DEV, dtype=jnp.int32), TOP)
    pair_rows = normed.reshape(source_count, TOK_DEV, D)[:, token_of, :]
    source_index = jnp.broadcast_to(jnp.arange(source_count, dtype=jnp.int32)[:, None], pair_ids.shape)
    sectioning = jnp.zeros((EXPERTS, source_count, CAP, D), jnp.bfloat16)
    sectioning = sectioning.at[pair_ids, source_index, slot_index].set(pair_rows)
    expert_out = lax.map(expert_apply, (sectioning.reshape(EXPERTS, source_count * CAP, D), expert_in.reshape(EXPERTS, 2, D, 2, FFW // 2), expert_down.reshape(EXPERTS, 2, FFW // 2, D)))
    expert_out = expert_out.reshape(EXPERTS, source_count, CAP, D)
    pair_out = expert_out[pair_ids, source_index, slot_index].astype(jnp.float32)
    weighted = pair_out * gate_values.reshape(source_count, TOK_DEV * TOP)[:, :, None]
    routed_sum = lax.optimization_barrier(jnp.sum(weighted.reshape(REQS, TOP, D), axis=1))
    return (hidden.astype(jnp.float32) + routed_sum).astype(jnp.bfloat16)
```

```python
import functools

import jax
import jax.numpy as jnp
from jax import lax
from jax.experimental import pallas as pl
from jax.experimental.pallas import tpu as pltpu
from jax.sharding import PartitionSpec as P

QKD = 192
F32 = jnp.float32
BF16 = jnp.bfloat16


def hop(value, axis, size, mask):
    return lax.ppermute(value, axis, [(i, i ^ mask) for i in range(size)])


def plane_of(count):
    return 4 if count % 4 == 0 else count


def project_kernel(place_ref, *refs, groups, rows, steps):
    parts, (map_ref, own_ref, send_ref, total, ordered) = refs[:groups], refs[groups:]
    step = pl.program_id(0)
    left = jnp.concatenate([part[...] for part in parts], axis=0)
    term = jnp.dot(left, map_ref[...], preferred_element_type=F32)

    @pl.when(step == 0)
    def _():
        total[...] = term

    @pl.when(step > 0)
    def _():
        total[...] += term

    @pl.when(step == steps - 1)
    def _():
        count = total.shape[0] // rows
        half = total.shape[0] // 2
        for block in range(count):
            target = pl.multiple_of(place_ref[block] * rows, rows)
            ordered[pl.ds(target, rows), :] = total[block * rows : (block + 1) * rows, :]
        side = place_ref[count]
        own_ref[...] = ordered[pl.ds(pl.multiple_of(side * half, half), half), :]
        send_ref[...] = ordered[pl.ds(pl.multiple_of((1 - side) * half, half), half), :].astype(BF16)


def project(parts, output_map, place, rows):
    groups = len(parts)
    depth, width = output_map.shape
    part_rows = parts[0].shape[0]
    total_rows = part_rows * groups
    steps = 8
    tile = depth // steps
    return pl.pallas_call(
        functools.partial(project_kernel, groups=groups, rows=rows, steps=steps),
        grid_spec=pltpu.PrefetchScalarGridSpec(
            num_scalar_prefetch=1,
            grid=(steps,),
            in_specs=[pl.BlockSpec((part_rows, tile), lambda k, place: (0, k))] * groups
            + [pl.BlockSpec((tile, width), lambda k, place: (k, 0))],
            out_specs=[pl.BlockSpec((total_rows // 2, width), lambda k, place: (0, 0))] * 2,
            scratch_shapes=[pltpu.VMEM((total_rows, width), F32)] * 2,
        ),
        out_shape=[
            jax.ShapeDtypeStruct((total_rows // 2, width), F32),
            jax.ShapeDtypeStruct((total_rows // 2, width), BF16),
        ],
        compiler_params=pltpu.CompilerParams(vmem_limit_bytes=24 * 2**20),
        cost_estimate=pl.CostEstimate(
            flops=2 * total_rows * depth * width,
            bytes_accessed=2 * (total_rows * depth + depth * width),
            transcendentals=0,
        ),
    )(place, *parts, output_map)


def expert_kernel(place_ref, *refs, groups, blocks, width):
    parts = refs[:groups]
    gain_ref, in_ref, gate_ref, down_ref, out_ref, total, squares, activated = refs[groups:]
    step = pl.program_id(0)
    line = blocks // groups
    hidden_units = down_ref.shape[0]

    @pl.when(step == 0)
    def _():
        total[...] = jnp.zeros_like(total)
        squares[...] = jnp.zeros_like(squares)

    for group, part in enumerate(parts):

        @pl.when((step >= group * line) & (step < (group + 1) * line))
        def _(part=part):
            wide = part[0].astype(F32)
            squares[...] += jnp.sum(wide * wide, axis=1, keepdims=True)
            scaled = (wide * gain_ref[0].astype(F32)).astype(BF16)
            total[...] += jnp.dot(scaled, in_ref[0], preferred_element_type=F32)

    @pl.when(step == blocks)
    def _():
        level = lax.rsqrt(squares[...] / width + 1e-06)
        gate_part = total[:, :hidden_units] * level
        up_part = total[:, hidden_units:] * level
        raised = gate_part / (1.0 + jnp.exp(-gate_part))
        activated[...] = (raised * up_part * gate_ref[...]).astype(BF16)

    @pl.when(step >= blocks)
    def _():
        out_ref[...] = jnp.dot(
            activated[...], down_ref[...], preferred_element_type=F32
        ).astype(BF16)


def expert_part(parts, gain, expert_rows, gates, down, place):
    groups = len(parts)
    line, tokens, columns = parts[0].shape
    blocks = groups * line
    units, width = down.shape
    tile = 1024 if width % 1024 == 0 else width
    out_steps = width // tile

    def part_spec(group):
        return pl.BlockSpec(
            (1, tokens, columns),
            lambda b, place: (jnp.clip(b - group * line, 0, line - 1), 0, 0),
        )

    def placed(b, place):
        return (place[jnp.minimum(b, blocks - 1)], 0, 0)

    return pl.pallas_call(
        functools.partial(expert_kernel, groups=groups, blocks=blocks, width=float(width)),
        grid_spec=pltpu.PrefetchScalarGridSpec(
            num_scalar_prefetch=1,
            grid=(blocks + out_steps,),
            in_specs=[part_spec(group) for group in range(groups)]
            + [
                pl.BlockSpec((1, 1, columns), placed),
                pl.BlockSpec((1, columns, 2 * units), placed),
                pl.BlockSpec((tokens, 1), lambda b, place: (0, 0)),
                pl.BlockSpec((units, tile), lambda b, place: (0, jnp.maximum(b - blocks, 0))),
            ],
            out_specs=pl.BlockSpec((tokens, tile), lambda b, place: (0, jnp.maximum(b - blocks, 0))),
            scratch_shapes=[
                pltpu.VMEM((tokens, 2 * units), F32),
                pltpu.VMEM((tokens, 1), F32),
                pltpu.VMEM((tokens, units), BF16),
            ],
        ),
        out_shape=jax.ShapeDtypeStruct((tokens, width), BF16),
        compiler_params=pltpu.CompilerParams(vmem_limit_bytes=24 * 2**20),
        cost_estimate=pl.CostEstimate(
            flops=6 * tokens * width * units,
            bytes_accessed=6 * width * units + 4 * tokens * width,
            transcendentals=tokens * units,
        ),
    )(place, *parts, gain, expert_rows, gates, down)


def on_device(
    queries,
    latent_cache,
    lengths,
    value_lift,
    output_map,
    residual,
    norm_gain,
    expert_ids,
    gate_values,
    expert_in,
    expert_down,
):
    request_count = queries.shape[0]
    latent_width = value_lift.shape[1]
    half_heads = value_lift.shape[0]
    value_width = value_lift.shape[2]
    half_slots = latent_cache.shape[1]
    token_count, model_width = residual.shape
    chips = lax.axis_size("dev")
    plane = plane_of(chips)
    line = chips // plane
    columns = output_map.shape[1]
    experts = chips // 2
    units = expert_down.shape[1]
    side = lax.axis_index("side")
    chip = lax.axis_index("dev")
    line_at, plane_at = chip // plane, chip % plane
    half_tokens = token_count * chips

    def line_hop(value, k):
        return hop(value, "dev", chips, k * plane)

    def plane_hop(value, k):
        return hop(value, "dev", chips, k)

    def swap(value):
        return hop(value, "side", 2, 1)

    chosen = expert_ids[:, :, None] == jnp.arange(experts, dtype=jnp.int32)[None, None, :]
    weights = jnp.sum(jnp.where(chosen, gate_values[:, :, None], 0.0), axis=1)
    all_weights = lax.all_gather(weights, ("side", "dev"), axis=0, tiled=True)
    own_weights = lax.dynamic_slice_in_dim(all_weights, chip // 2, 1, 1)
    gates_own = lax.dynamic_slice_in_dim(own_weights, side * half_tokens, half_tokens, 0)
    gates_other = lax.dynamic_slice_in_dim(own_weights, (1 - side) * half_tokens, half_tokens, 0)

    residual_blocks = residual.reshape(token_count, chips, columns).swapaxes(0, 1)
    residual_columns = lax.all_to_all(
        residual_blocks, "dev", split_axis=0, concat_axis=0, tiled=True
    ).reshape(half_tokens, columns)

    score_scale = QKD ** (-0.5)
    scores = (
        jnp.einsum("rhc,rpc->rhp", queries, latent_cache, preferred_element_type=F32) * score_scale
    )
    positions = side * half_slots + jnp.arange(half_slots, dtype=jnp.int32)
    usable = (positions[None, :] < lengths[:, None])[:, None, :]
    masked = jnp.where(usable, scores, -1e30)
    local_top = jnp.max(masked, axis=2)
    raised = jnp.where(usable, jnp.exp(masked - local_top[:, :, None]), 0.0)
    local_total = jnp.sum(raised, axis=2)
    local_latent = jnp.einsum(
        "rhp,rpc->rhc",
        raised.astype(BF16),
        latent_cache[:, :, :latent_width],
        preferred_element_type=F32,
    )
    local_latent = (local_latent / jnp.maximum(local_total, 1e-30)[:, :, None]).astype(BF16)

    def heads_of(value, which):
        return lax.dynamic_slice_in_dim(value, which * half_heads, half_heads, 1)

    stats = jnp.stack([local_top, local_total], axis=2)
    other_latent = swap(heads_of(local_latent, 1 - side))
    other_stats = swap(heads_of(stats, 1 - side))
    own_latent = heads_of(local_latent, side)
    own_stats = heads_of(stats, side)
    top = jnp.maximum(own_stats[:, :, 0], other_stats[:, :, 0])
    own_share = own_stats[:, :, 1] * jnp.exp(own_stats[:, :, 0] - top)
    other_share = other_stats[:, :, 1] * jnp.exp(other_stats[:, :, 0] - top)
    share_sum = own_share + other_share
    latent_out = (
        own_latent.astype(F32) * (own_share / share_sum)[:, :, None]
        + other_latent.astype(F32) * (other_share / share_sum)[:, :, None]
    ).astype(BF16)
    head_values = jnp.einsum("rhc,hcv->rhv", latent_out, value_lift, preferred_element_type=F32)
    head_values = head_values.astype(BF16).reshape(request_count, half_heads * value_width)

    def gather(block):
        stacked = jnp.stack([block] + [line_hop(block, k) for k in range(1, line)])
        return [stacked] + [plane_hop(stacked, k) for k in range(1, plane)]

    places = [
        (line_at ^ k_line) * plane + (plane_at ^ k_plane)
        for k_plane in range(plane)
        for k_line in range(line)
    ]
    place = jnp.stack(places + [side]).astype(jnp.int32)
    gathered = [
        part.reshape(line * request_count, half_heads * value_width) for part in gather(head_values)
    ]
    own_columns, sent_columns = project(gathered, output_map, place, request_count)
    attention = own_columns + swap(sent_columns).astype(F32)
    hidden = (residual_columns.astype(F32) + attention).astype(BF16)

    hidden_own = gather(hidden)
    hidden_other = [swap(part) for part in hidden_own]
    gain = norm_gain.reshape(chips, 1, columns)
    expert_rows = expert_in.reshape(chips, columns, 2 * units)
    down = expert_down[0]
    partial_own = expert_part(hidden_own, gain, expert_rows, gates_own, down, place)
    partial_other = expert_part(hidden_other, gain, expert_rows, gates_other, down, place)
    partial = (partial_own.astype(F32) + swap(partial_other).astype(F32)).astype(BF16)

    partial = partial.reshape(line, plane, token_count, model_width)

    def to_plane(k):
        return lax.dynamic_index_in_dim(partial, plane_at ^ k, 1, keepdims=False)

    plane_sum = to_plane(0).astype(F32)
    for k in range(1, plane):
        plane_sum = plane_sum + plane_hop(to_plane(k), k).astype(F32)
    plane_sum = plane_sum.astype(BF16)

    def to_line(k):
        return lax.dynamic_index_in_dim(plane_sum, line_at ^ k, 0, keepdims=False)

    routed_sum = to_line(0).astype(F32)
    for k in range(1, line):
        routed_sum = routed_sum + line_hop(to_line(k), k).astype(F32)

    stacked = jnp.concatenate(
        [lax.dynamic_slice_in_dim(part, chip * token_count, token_count, 1) for part in hidden_own]
    )
    order = jnp.stack(
        [
            ((plane_at ^ (at % plane)) * line + (line_at ^ (at // plane)))
            for at in range(chips)
        ]
    )
    own_hidden = jnp.take(stacked, order, axis=0).swapaxes(0, 1).reshape(token_count, model_width)
    return (own_hidden.astype(F32) + routed_sum).astype(BF16)


def solution(mesh):
    in_specs = (
        P("dev", None, None),
        P("dev", "side", None),
        P("dev"),
        P("side", None, None),
        P("side", "dev"),
        P(("side", "dev"), None),
        P(),
        P(("side", "dev"), None),
        P(("side", "dev"), None),
        P("dev", None, None, "side"),
        P("dev", "side", None),
    )
    out_specs = P(("side", "dev"), None)
    return jax.shard_map(
        on_device, mesh=mesh, in_specs=in_specs, out_specs=out_specs, check_vma=False
    )
```

```python
import functools

import jax
import jax.numpy as jnp
from jax import lax
from jax.experimental import pallas as pl
from jax.experimental.pallas import tpu as pltpu
from jax.sharding import PartitionSpec as P

QKD = 192
F32 = jnp.float32
BF16 = jnp.bfloat16


def hop(value, axis, size, mask):
    return lax.ppermute(value, axis, [(i, i ^ mask) for i in range(size)])


def budget(*arrays):
    count = sum(2 * a.size * a.dtype.itemsize for a in arrays)
    return 8 * 2**20 + count


def gather(first, second, line, line_hop, plane_hop):
    both = jnp.concatenate([first.reshape(-1), second.reshape(-1)]) if first.shape != second.shape else None
    if both is None:
        sent = jnp.stack([first, second])
        arrived = [line_hop(sent, k) for k in range(1, line)]
        far = [jnp.stack([a[h] for a in arrived]) for h in (0, 1)]
    else:
        far = [jnp.stack([line_hop(part, k) for k in range(1, line)]) for part in (first, second)]
    near = [first[None], second[None]]
    far_at = list(range(1, line))
    halves = []
    near_one = [plane_hop(near[h], 1 + h) for h in (0, 1)]
    near_two = [plane_hop(jnp.concatenate([near[h], near_one[h]]), 2 - h) for h in (0, 1)]
    far_one = [plane_hop(far[h], 1 + h) for h in (0, 1)]
    far_two = [plane_hop(jnp.concatenate([far[h], far_one[h]]), 2 - h) for h in (0, 1)]
    for h in (0, 1):
        one, two = 1 + h, 2 - h
        halves.append(
            [
                (near[h], [(0, 0)]),
                (near_one[h], [(one, 0)]),
                (near_two[h], [(two, 0), (3, 0)]),
                (far[h], [(0, k) for k in far_at]),
                (far_one[h], [(one, k) for k in far_at]),
                (far_two[h], [(p, k) for p in (two, 3) for k in far_at]),
            ]
        )
    return halves


def project_kernel(place_ref, *refs, groups, rows, steps):
    first, second = refs[:groups], refs[groups : 2 * groups]
    map_ref, own_ref, send_ref, totals, ordered = refs[2 * groups :]
    step = pl.program_id(0)
    blocks = totals.shape[1] // rows

    def add(parts, half):
        left = jnp.concatenate([part[...] for part in parts], axis=0)
        term = lax.dot_general(
            left, map_ref[...], (((1,), (1,)), ((), ())), preferred_element_type=F32
        )

        @pl.when(step == half * steps)
        def _():
            totals[half] = term

        @pl.when(step != half * steps)
        def _():
            totals[half] += term

    @pl.when(step < steps)
    def _():
        add(first, 0)

    @pl.when(step >= steps)
    def _():
        add(second, 1)

    @pl.when(step == 2 * steps - 1)
    def _():
        half_rows = totals.shape[1] // 2
        for block in range(blocks):
            target = pl.multiple_of(place_ref[block] * rows, rows)
            ordered[pl.ds(target, rows), :] = totals[0, block * rows : (block + 1) * rows, :]
        for block in range(blocks):
            target = pl.multiple_of(place_ref[blocks + block] * rows, rows)
            ordered[pl.ds(target, rows), :] += totals[1, block * rows : (block + 1) * rows, :]
        side = place_ref[2 * blocks]
        own_ref[...] = ordered[pl.ds(pl.multiple_of(side * half_rows, half_rows), half_rows), :]
        send_ref[...] = ordered[
            pl.ds(pl.multiple_of((1 - side) * half_rows, half_rows), half_rows), :
        ].astype(BF16)


def project(first, second, columns_map, place, rows):
    groups = len(first)
    width, depth = columns_map.shape
    total_rows = sum(part.shape[0] for part in first)
    steps = 4
    tile = depth // (2 * steps)
    return pl.pallas_call(
        functools.partial(project_kernel, groups=groups, rows=rows, steps=steps),
        grid_spec=pltpu.PrefetchScalarGridSpec(
            num_scalar_prefetch=1,
            grid=(2 * steps,),
            in_specs=[
                pl.BlockSpec((p.shape[0], tile), lambda k, place: (0, jnp.minimum(k, steps - 1)))
                for p in first
            ]
            + [
                pl.BlockSpec((p.shape[0], tile), lambda k, place: (0, jnp.maximum(k - steps, 0)))
                for p in second
            ]
            + [pl.BlockSpec((width, tile), lambda k, place: (0, k))],
            out_specs=[pl.BlockSpec((total_rows // 2, width), lambda k, place: (0, 0))] * 2,
            scratch_shapes=[
                pltpu.VMEM((2, total_rows, width), F32),
                pltpu.VMEM((total_rows, width), F32),
            ],
        ),
        out_shape=[
            jax.ShapeDtypeStruct((total_rows // 2, width), F32),
            jax.ShapeDtypeStruct((total_rows // 2, width), BF16),
        ],
        compiler_params=pltpu.CompilerParams(vmem_limit_bytes=24 * 2**20),
        cost_estimate=pl.CostEstimate(
            flops=2 * total_rows * depth * width,
            bytes_accessed=2 * (total_rows * depth + depth * width),
            transcendentals=0,
        ),
    )(place, *first, *second, columns_map)


def expert_kernel(place_ref, *refs, sources, plan, last, line, model_width, owner_rows):
    count = len(sources)
    own, other = refs[:count], refs[count : 2 * count]
    refs = refs[2 * count :]
    if last:
        gain_ref, in_ref, sums_in, squares_in, rows_in, gate_ref = refs[:6]
        out_ref, rows_out, weights, wide, total, squares, arrived = refs[6:]
    else:
        gain_ref, in_ref, total, squares, rows_out, weights, wide, arrived = refs
    blocks = sum(steps for steps, _, _ in plan)
    offsets = []
    for steps, _, _ in plan:
        offsets.append(sum(p[0] for p in plan[: len(offsets)]))

    def load(at):
        return pltpu.make_async_copy(in_ref.at[place_ref[at]], weights.at[at], arrived.at[at])

    def start(at, carry):
        load(at).start()
        return carry

    lax.fori_loop(0, blocks, start, 0)
    if last:
        total[...] = sums_in[...]
        squares[...] = squares_in[...]
        rows_out[...] = rows_in[...]
    else:
        total[...] = jnp.zeros_like(total)
        squares[...] = jnp.zeros_like(squares)
        rows_out[...] = jnp.zeros_like(rows_out)
    half = wide.shape[0] // 4
    owner = place_ref[blocks]

    def work(at, first, second):
        source, index = first
        wide[0:half] = own[source][index].astype(F32)
        wide[2 * half : 3 * half] = other[source][index].astype(F32)
        source, index = second
        wide[half : 2 * half] = own[source][index].astype(F32)
        wide[3 * half : 4 * half] = other[source][index].astype(F32)
        chip = place_ref[at]
        rows_out[chip] = wide[pl.ds(pl.multiple_of(owner * owner_rows, owner_rows), owner_rows), :]
        values = wide[...]
        squares[...] += jnp.sum(values * values, axis=1, keepdims=True)
        scaled = (values * gain_ref[chip].astype(F32)).astype(BF16)
        load(at).wait()
        total[...] += jnp.dot(scaled, weights[at], preferred_element_type=F32)

    for offset, (steps, (first, first_at), (second, second_at)) in zip(offsets, plan):
        if steps == 1:
            work(offset, (first, first_at), (second, second_at))
        else:

            def step(k, carry):
                work(offset + k, (first, first_at + k), (second, second_at + k))
                return carry

            lax.fori_loop(0, steps, step, 0)

    if last:
        units = total.shape[1] // 2
        level = lax.rsqrt(squares[...] / model_width + 1e-06)
        gate_part = total[:, :units] * level
        up_part = total[:, units:] * level
        raised = gate_part / (1.0 + jnp.exp(-gate_part))
        total[:, :units] = raised * up_part * gate_ref[...]
        chips = rows_out.shape[0]
        side_rows = total.shape[0] // 2
        for first_row in (0, side_rows):
            for pair in range(chips // 2):
                pieces = [
                    total[
                        pl.ds(
                            pl.multiple_of(
                                first_row + place_ref[blocks + 1 + 2 * pair + j] * owner_rows,
                                owner_rows,
                            ),
                            owner_rows,
                        ),
                        :units,
                    ]
                    for j in (0, 1)
                ]
                row = first_row + 2 * pair * owner_rows
                out_ref[row : row + 2 * owner_rows, :] = jnp.concatenate(pieces).astype(BF16)


def expert_rows(sources, other_sources, plan, gain, weights, place, owner_rows, carried=None, gates=None):
    last = carried is not None
    chips, columns, double = weights.shape
    half = sources[0].shape[1]
    tokens = 4 * half
    blocks = sum(steps for steps, _, _ in plan)
    model_width = chips * columns
    whole = pl.BlockSpec(memory_space=pltpu.VMEM)
    operands = [*sources, *other_sources, gain]
    extra = [*carried, gates] if last else []
    sums = [
        jax.ShapeDtypeStruct((tokens, double), F32),
        jax.ShapeDtypeStruct((tokens, 1), F32),
        jax.ShapeDtypeStruct((chips, owner_rows, columns), F32),
    ]
    scratch = [
        pltpu.VMEM((blocks, columns, double), BF16),
        pltpu.VMEM((tokens, columns), F32),
    ]
    if last:
        out_shape = [jax.ShapeDtypeStruct((tokens, double // 2), BF16), sums[2]]
        scratch += [pltpu.VMEM((tokens, double), F32), pltpu.VMEM((tokens, 1), F32)]
    else:
        out_shape = sums
    scratch += [pltpu.SemaphoreType.DMA((blocks,))]
    return pl.pallas_call(
        functools.partial(
            expert_kernel,
            sources=sources,
            plan=plan,
            last=last,
            line=0,
            model_width=float(model_width),
            owner_rows=owner_rows,
        ),
        in_specs=[pl.BlockSpec(memory_space=pltpu.SMEM)]
        + [whole] * len(operands)
        + [pl.BlockSpec(memory_space=pl.ANY)]
        + [whole] * len(extra),
        out_specs=[whole] * len(out_shape),
        out_shape=out_shape,
        scratch_shapes=scratch,
        compiler_params=pltpu.CompilerParams(
            vmem_limit_bytes=budget(*operands, *extra, weights, *out_shape, *sums)
        ),
        cost_estimate=pl.CostEstimate(
            flops=2 * tokens * blocks * columns * double,
            bytes_accessed=2 * blocks * columns * (double + tokens),
            transcendentals=tokens * double,
        ),
    )(place, *operands, weights, *extra)


def down_kernel(rows_ref, down_ref, *outs, order):
    rows = rows_ref.shape[0] // 8
    product = jnp.dot(rows_ref[...], down_ref[...], preferred_element_type=F32).astype(BF16)
    for at, groups in enumerate(order):
        for j, group in enumerate(groups):
            outs[at][j * rows : (j + 1) * rows, :] = product[group * rows : (group + 1) * rows, :]


def lower(rows, down, half, order):
    units, width = down.shape
    steps = 4
    tile = width // (2 * steps)
    count = rows.shape[0] // 4
    return pl.pallas_call(
        functools.partial(down_kernel, order=order),
        grid=(steps,),
        in_specs=[
            pl.BlockSpec(rows.shape, lambda k: (0, 0)),
            pl.BlockSpec((units, tile), lambda k: (0, half * steps + k)),
        ],
        out_specs=[pl.BlockSpec((count, tile), lambda k: (0, k))] * 4,
        out_shape=[jax.ShapeDtypeStruct((count, width // 2), BF16)] * 4,
        compiler_params=pltpu.CompilerParams(vmem_limit_bytes=24 * 2**20),
        cost_estimate=pl.CostEstimate(
            flops=rows.shape[0] * units * width,
            bytes_accessed=(units + rows.shape[0]) * width,
            transcendentals=0,
        ),
    )(rows, down)


def on_device(
    queries,
    latent_cache,
    lengths,
    value_lift,
    output_map,
    residual,
    norm_gain,
    expert_ids,
    gate_values,
    expert_in,
    expert_down,
):
    request_count = queries.shape[0]
    latent_width = value_lift.shape[1]
    half_heads = value_lift.shape[0]
    value_width = value_lift.shape[2]
    half_slots = latent_cache.shape[1]
    token_count, model_width = residual.shape
    chips = lax.axis_size("dev")
    plane = 4
    line = chips // plane
    columns = output_map.shape[1]
    experts = chips // 2
    units = expert_down.shape[1]
    side = lax.axis_index("side")
    chip = lax.axis_index("dev")
    line_at, plane_at = chip // plane, chip % plane
    half_tokens = token_count * chips

    def line_hop(value, k):
        return hop(value, "dev", chips, k * plane)

    def plane_hop(value, k):
        return hop(value, "dev", chips, k)

    def swap(value):
        return hop(value, "side", 2, 1)

    def placed(offsets):
        return [(line_at ^ k_line) * plane + (plane_at ^ k_plane) for k_plane, k_line in offsets]

    chosen = expert_ids[:, :, None] == jnp.arange(experts, dtype=jnp.int32)[None, None, :]
    weights = jnp.sum(jnp.where(chosen, gate_values[:, :, None], 0.0), axis=1)
    weights_high = lax.reduce_precision(weights, 8, 7)
    weight_terms = jnp.concatenate([weights_high, weights - weights_high], axis=1).astype(BF16)
    weight_width = -(-token_count * 2 * experts // (request_count * 128)) * 128
    weight_block = jnp.pad(
        weight_terms.reshape(-1), (0, request_count * weight_width - weight_terms.size)
    ).reshape(request_count, weight_width)

    residual_blocks = residual.reshape(token_count, chips, columns).swapaxes(0, 1)
    residual_columns = lax.all_to_all(
        residual_blocks, "dev", split_axis=0, concat_axis=0, tiled=True
    ).reshape(half_tokens, columns)

    score_scale = QKD ** (-0.5)
    scores = (
        jnp.einsum("rhc,rpc->rhp", queries, latent_cache, preferred_element_type=F32) * score_scale
    )
    positions = side * half_slots + jnp.arange(half_slots, dtype=jnp.int32)
    usable = (positions[None, :] < lengths[:, None])[:, None, :]
    masked = jnp.where(usable, scores, -1e30)
    local_top = jnp.max(masked, axis=2)
    raised = jnp.where(usable, jnp.exp(masked - local_top[:, :, None]), 0.0)
    local_total = jnp.sum(raised, axis=2)
    local_latent = jnp.einsum(
        "rhp,rpc->rhc",
        raised.astype(BF16),
        latent_cache[:, :, :latent_width],
        preferred_element_type=F32,
    )
    local_latent = (local_latent / jnp.maximum(local_total, 1e-30)[:, :, None]).astype(BF16)

    def heads_of(value, which):
        return lax.dynamic_slice_in_dim(value, which * half_heads, half_heads, 1)

    stats = jnp.stack([local_top, local_total], axis=2)
    other_latent = swap(heads_of(local_latent, 1 - side))
    other_stats = swap(heads_of(stats, 1 - side))
    own_latent = heads_of(local_latent, side)
    own_stats = heads_of(stats, side)
    top = jnp.maximum(own_stats[:, :, 0], other_stats[:, :, 0])
    own_share = own_stats[:, :, 1] * jnp.exp(own_stats[:, :, 0] - top)
    other_share = other_stats[:, :, 1] * jnp.exp(other_stats[:, :, 0] - top)
    share_sum = own_share + other_share
    latent_out = (
        own_latent.astype(F32) * (own_share / share_sum)[:, :, None]
        + other_latent.astype(F32) * (other_share / share_sum)[:, :, None]
    ).astype(BF16)
    head_values = jnp.einsum("rhc,hcv->rhv", latent_out, value_lift, preferred_element_type=F32)
    head_values = head_values.astype(BF16).reshape(request_count, half_heads * value_width)

    half_depth = half_heads * value_width // 2
    first, second = gather(
        jnp.concatenate([head_values[:, :half_depth], weight_block], axis=1),
        jnp.concatenate([head_values[:, half_depth:], jnp.zeros_like(weight_block)], axis=1),
        line,
        line_hop,
        plane_hop,
    )
    place = jnp.stack(
        [at for half in (first, second) for _, offsets in half for at in placed(offsets)] + [side]
    ).astype(jnp.int32)
    first_parts, second_parts = [
        [part.reshape(-1, part.shape[-1]) for part, _ in half] for half in (first, second)
    ]
    own_columns, sent_columns = project(
        first_parts, second_parts, output_map.T, place, request_count
    )
    attention = own_columns + swap(sent_columns).astype(F32)
    hidden = (residual_columns.astype(F32) + attention).astype(BF16)

    gathered = jnp.concatenate([part[:, :, half_depth:] for part, _ in first])
    gathered = gathered.reshape(chips, -1)[:, : token_count * 2 * experts]
    gathered = gathered.reshape(chips, token_count, 2, experts).astype(F32)
    gathered = lax.dynamic_index_in_dim(gathered, chip // 2, 3, keepdims=False).sum(axis=2)
    order = [offsets for _, part_offsets in first for offsets in part_offsets]
    spots = jnp.stack(placed(order))
    own_gates = jnp.zeros((chips, token_count), F32).at[spots].set(gathered).reshape(-1, 1)
    gates = jnp.concatenate([own_gates, swap(own_gates)])

    half_rows = half_tokens // 2
    first, second = gather(hidden[:half_rows], hidden[half_rows:], line, line_hop, plane_hop)
    (near_a, near_one_a, near_two_a, far_a, far_one_a, far_two_a) = [part for part, _ in first]
    (near_b, near_one_b, near_two_b, far_b, far_one_b, far_two_b) = [part for part, _ in second]
    early = [near_a, near_b, near_one_a, near_one_b, near_two_a, near_two_b, far_a, far_b]
    late = [far_one_a, far_one_b, far_two_a, far_two_b]
    steps = line - 1
    early_plan = [
        (1, (0, 0), (1, 0)),
        (1, (2, 0), (5, 0)),
        (1, (4, 0), (3, 0)),
        (1, (4, 1), (5, 1)),
        (steps, (6, 0), (7, 0)),
    ]
    late_plan = [
        (steps, (0, 0), (3, 0)),
        (steps, (2, 0), (1, 0)),
        (steps, (2, steps), (3, steps)),
    ]
    early_at = [(0, 0), (1, 0), (2, 0), (3, 0)] + [(0, k) for k in range(1, line)]
    late_at = [(p, k) for p in (1, 2, 3) for k in range(1, line)]
    out_at = [(p, k) for p in range(plane) for k in range(line)]
    early_place = jnp.stack(placed(early_at) + [chip]).astype(jnp.int32)
    late_place = jnp.stack(placed(late_at) + [chip] + placed(out_at)).astype(jnp.int32)
    gain = norm_gain.reshape(chips, 1, columns)
    in_rows = expert_in.reshape(chips, columns, 2 * units)
    down = expert_down[0]
    carried = expert_rows(
        early, [swap(part) for part in early], early_plan, gain, in_rows, early_place, token_count
    )
    activated, own_hidden = expert_rows(
        late,
        [swap(part) for part in late],
        late_plan,
        gain,
        in_rows,
        late_place,
        token_count,
        carried,
        gates,
    )

    sums = []
    for half in (0, 1):
        one, two = 1 + half, 2 - half
        kept, moved = [0, two], [one, 3]
        own_moved, own_kept, other_moved, other_kept = lower(
            activated, down, half, [moved, kept, [4 + g for g in moved], [4 + g for g in kept]]
        )
        moved_sum = (own_moved.astype(F32) + swap(other_moved).astype(F32)).astype(BF16)
        kept_sum = own_kept.astype(F32) + swap(other_kept).astype(F32)
        kept_sum = kept_sum + plane_hop(moved_sum, one).astype(F32)
        rows = kept_sum.shape[0] // 2
        arrived = plane_hop(kept_sum[rows:].astype(BF16), two).astype(F32)
        sums.append(kept_sum[:rows] + arrived)
    plane_sum = jnp.concatenate(sums, axis=1).reshape(line, token_count, model_width)
    routed_sum = plane_sum[0]
    for k in range(1, line):
        routed_sum = routed_sum + line_hop(plane_sum[k].astype(BF16), k).astype(F32)
    own_hidden = own_hidden.swapaxes(0, 1).reshape(token_count, model_width)
    return (own_hidden + routed_sum).astype(BF16)


def solution(mesh):
    in_specs = (
        P("dev", None, None),
        P("dev", "side", None),
        P("dev"),
        P("side", None, None),
        P("side", "dev"),
        P(("side", "dev"), None),
        P(),
        P(("side", "dev"), None),
        P(("side", "dev"), None),
        P("dev", None, None, "side"),
        P("dev", "side", None),
    )
    out_specs = P(("side", "dev"), None)
    return jax.shard_map(
        on_device, mesh=mesh, in_specs=in_specs, out_specs=out_specs, check_vma=False
    )
```

```python
import functools

import jax
import jax.numpy as jnp
from jax import lax
from jax.experimental import pallas as pl
from jax.experimental.pallas import tpu as pltpu
from jax.sharding import PartitionSpec as P

QKD = 192
F32 = jnp.float32
BF16 = jnp.bfloat16
VMEM_LIMIT = 48 * 2**20


def hop(value, axis, size, mask):
    return lax.ppermute(value, axis, [(i, i ^ mask) for i in range(size)])


def gather(block, split, groups, line_hop, plane_hop, beside):
    arrived = {0: block}
    for group in groups:
        for k in group:
            if k:
                arrived[k] = line_hop(block, k)
    halves = ([], [])
    for at, group in enumerate(groups):
        column = jnp.stack([arrived[k] for k in group])
        if at == len(groups) - 1:
            column, beside = lax.optimization_barrier((column, beside))
        for parts, half, (one, two) in zip(halves, split(column), ((1, 2), (2, 1))):
            near = plane_hop(half, one)
            rest = plane_hop(jnp.concatenate([half, near]), two)
            parts.append((half, [(0, k) for k in group]))
            parts.append((near, [(one, k) for k in group]))
            parts.append((rest, [(p, k) for p in (two, 3) for k in group]))
    return halves, beside


def attend_kernel(length_ref, query_ref, cache_ref, own_ref, other_ref, stats_ref, latents, *, scale):
    group, heads, _ = query_ref.shape
    latent_width = own_ref.shape[2]
    slots = cache_ref.shape[2]
    half = heads // 2
    first = pl.program_id(0) * group
    side = length_ref[length_ref.shape[0] - 1]
    positions = side * slots + lax.broadcasted_iota(jnp.int32, (heads, slots), 1)
    lanes = lax.broadcasted_iota(jnp.int32, (heads, stats_ref.shape[2]), 1)
    for at in range(group):
        usable = positions < length_ref[first + at]
        scores = jnp.dot(query_ref[at], cache_ref[at], preferred_element_type=F32) * scale
        masked = jnp.where(usable, scores, -1e30)
        top = jnp.max(masked, axis=1, keepdims=True)
        raised = jnp.where(usable, jnp.exp(masked - top), 0.0)
        total = jnp.sum(raised, axis=1, keepdims=True)
        latent = lax.dot_general(
            raised.astype(BF16),
            cache_ref[at, :latent_width, :],
            (((1,), (1,)), ((), ())),
            preferred_element_type=F32,
        )
        latents[at] = latent / jnp.maximum(total, 1e-30)
        stats_ref[at] = jnp.where(lanes == 0, top, total)
    for at in range(group):
        own_ref[at] = latents[at, pl.ds(pl.multiple_of(side * half, half), half), :].astype(BF16)
        other_ref[at] = latents[
            at, pl.ds(pl.multiple_of((1 - side) * half, half), half), :
        ].astype(BF16)


def attend(queries, cache_columns, lengths, side, latent_width):
    requests, heads, width = queries.shape
    slots = cache_columns.shape[2]
    group = 4
    table = jnp.concatenate([lengths, side.reshape(1)]).astype(jnp.int32)
    return pl.pallas_call(
        functools.partial(attend_kernel, scale=QKD ** (-0.5)),
        grid_spec=pltpu.PrefetchScalarGridSpec(
            num_scalar_prefetch=1,
            grid=(requests // group,),
            in_specs=[
                pl.BlockSpec((group, heads, width), lambda r, table: (r, 0, 0)),
                pl.BlockSpec((group, width, slots), lambda r, table: (r, 0, 0)),
            ],
            out_specs=[
                pl.BlockSpec((group, heads // 2, latent_width), lambda r, table: (r, 0, 0)),
                pl.BlockSpec((group, heads // 2, latent_width), lambda r, table: (r, 0, 0)),
                pl.BlockSpec((group, heads, 128), lambda r, table: (r, 0, 0)),
            ],
            scratch_shapes=[pltpu.VMEM((group, heads, latent_width), F32)],
        ),
        out_shape=[
            jax.ShapeDtypeStruct((requests, heads // 2, latent_width), BF16),
            jax.ShapeDtypeStruct((requests, heads // 2, latent_width), BF16),
            jax.ShapeDtypeStruct((requests, heads, 128), F32),
        ],
        compiler_params=pltpu.CompilerParams(vmem_limit_bytes=48 * 2**20),
        cost_estimate=pl.CostEstimate(
            flops=4 * requests * heads * width * slots,
            bytes_accessed=2 * requests * width * (heads + slots),
            transcendentals=requests * heads * slots,
        ),
    )(table, queries, cache_columns)


def project_kernel(place_ref, *refs, counts, rows, depths, steps):
    groups = len(counts)
    parts = (refs[:groups], refs[groups : 2 * groups])
    map_ref, own_ref, send_ref, first, second, mapping, total, arrived, map_arrived = refs[2 * groups :]
    blocks = sum(counts)
    copies, map_copies = [], []
    for half, left in enumerate((first, second)):
        at = half * blocks
        for part, count in zip(parts[half], counts):
            for k in range(count):
                row = pl.multiple_of(place_ref[at] * rows, rows)
                copies.append(
                    pltpu.make_async_copy(part.at[k], left.at[pl.ds(row, rows)], arrived.at[at])
                )
                at += 1
    tile = mapping.shape[1] // steps
    for step in range(steps):
        columns = pl.ds(step * tile, tile)
        map_copies.append(
            pltpu.make_async_copy(
                map_ref.at[:, columns], mapping.at[:, columns], map_arrived.at[step]
            )
        )
    for copy in copies + map_copies:
        copy.start()
    for copy in copies:
        copy.wait()
    for step in range(steps):
        map_copies[step].wait()
        left = first if step * tile < depths else second
        column = step * tile if step * tile < depths else step * tile - depths
        term = lax.dot_general(
            left[:, column : column + tile],
            mapping[:, step * tile : (step + 1) * tile],
            (((1,), (1,)), ((), ())),
            preferred_element_type=F32,
        )
        if step:
            total[...] += term
        else:
            total[...] = term
    half_rows = total.shape[0] // 2
    side = place_ref[2 * blocks]
    own_ref[...] = total[pl.ds(pl.multiple_of(side * half_rows, half_rows), half_rows), :].T
    send_ref[...] = total[
        pl.ds(pl.multiple_of((1 - side) * half_rows, half_rows), half_rows), :
    ].T.astype(BF16)


def project(first, second, columns_map, place):
    width, depth = columns_map.shape
    rows = first[0].shape[1]
    counts = [part.shape[0] for part in first]
    total_rows = rows * sum(counts)
    steps = 4
    anywhere = pl.BlockSpec(memory_space=pl.ANY)
    whole = pl.BlockSpec(memory_space=pltpu.VMEM)
    return pl.pallas_call(
        functools.partial(
            project_kernel, counts=counts, rows=rows, depths=depth // 2, steps=steps
        ),
        in_specs=[pl.BlockSpec(memory_space=pltpu.SMEM)] + [anywhere] * (2 * len(counts) + 1),
        out_specs=[whole] * 2,
        out_shape=[
            jax.ShapeDtypeStruct((width, total_rows // 2), F32),
            jax.ShapeDtypeStruct((width, total_rows // 2), BF16),
        ],
        scratch_shapes=[
            pltpu.VMEM((total_rows, first[0].shape[2]), BF16),
            pltpu.VMEM((total_rows, second[0].shape[2]), BF16),
            pltpu.VMEM((width, depth), BF16),
            pltpu.VMEM((total_rows, width), F32),
            pltpu.SemaphoreType.DMA((2 * sum(counts),)),
            pltpu.SemaphoreType.DMA((steps,)),
        ],
        compiler_params=pltpu.CompilerParams(vmem_limit_bytes=VMEM_LIMIT),
        cost_estimate=pl.CostEstimate(
            flops=2 * total_rows * depth * width,
            bytes_accessed=2 * (total_rows * depth + depth * width),
            transcendentals=0,
        ),
    )(place, *first, *second, columns_map)


def expert_kernel(place_ref, *refs, blocks, heights, halves, carried, sizes):
    count = len(blocks)
    own, other, refs = refs[:count], refs[count : 2 * count], refs[2 * count :]
    gain_refs, in_ref, refs = refs[:2], refs[2], refs[3:]
    sums_in, refs = refs[: 2 * carried], refs[2 * carried :]
    if sizes:
        gate_ref, down_ref, *refs = refs
        outs, refs = refs[: 2 * len(sizes[2])], refs[2 * len(sizes[2]) :]
        total, squares, weights, rows, arrived, part_arrived = refs[:6]
        activated, results, down, down_arrived, sent = refs[6:]
        down_copy = pltpu.make_async_copy(down_ref, down, down_arrived)
    else:
        total, squares, weights, rows, arrived, part_arrived = refs
    lanes = rows.shape[1] // 2
    offsets = [sum(n * h for n, h in zip(blocks[:at], heights[:at])) for at in range(count + 1)]
    spots = []
    for entry in range(count):
        for k in range(blocks[entry]):
            row = offsets[entry] + k * heights[entry]
            spots.append((entry, k, row, heights[entry]))
    part_copies, weight_copies = [], []
    for at, (entry, k, row, height) in enumerate(spots):
        for side, ref in enumerate((own[entry], other[entry])):
            part_copies.append(
                pltpu.make_async_copy(
                    ref.at[k],
                    rows.at[pl.ds(row, height), pl.ds(side * lanes, lanes)],
                    part_arrived.at[2 * at + side],
                )
            )
        source = pl.multiple_of(place_ref[at], 8)
        weight_copies.append(
            pltpu.make_async_copy(
                in_ref.at[pl.ds(source, height)], weights.at[pl.ds(row, height)], arrived.at[at]
            )
        )
    for copy in part_copies + weight_copies:
        copy.start()
    if sizes:
        down_copy.start()
    if sums_in:
        squares[...] = sums_in[1][...]
    else:
        squares[...] = jnp.zeros_like(squares)
    diagonals = {
        height: lax.broadcasted_iota(jnp.int32, (height, height), 0)
        == lax.broadcasted_iota(jnp.int32, (height, height), 1)
        for height in set(heights)
    }
    for at, (entry, k, row, height) in enumerate(spots):
        part_copies[2 * at].wait()
        part_copies[2 * at + 1].wait()
        wide = rows[row : row + height].astype(F32)
        squares[...] += jnp.sum((wide * wide).reshape(height // 8, 8, 2 * lanes), axis=0)
        gain = gain_refs[halves[entry]][pl.ds(place_ref[len(spots) + at], 1), :]
        gain = jnp.where(diagonals[height], gain, 0.0).astype(BF16)
        rows[row : row + height] = jnp.dot(
            gain, rows[row : row + height], preferred_element_type=F32
        ).astype(BF16)
    for entry in range(count):
        for at, spot in enumerate(spots):
            if spot[0] == entry:
                weight_copies[at].wait()
        term = lax.dot_general(
            rows[offsets[entry] : offsets[entry + 1]],
            weights[offsets[entry] : offsets[entry + 1]],
            (((0,), (0,)), ((), ())),
            preferred_element_type=F32,
        )
        if entry:
            total[...] += term
        elif sums_in:
            total[...] = sums_in[0][...] + term
        else:
            total[...] = term
    if not sizes:
        return

    units = total.shape[1] // 2
    mean = jnp.sum(squares[...].T, axis=1, keepdims=True) / in_ref.shape[0]
    level = lax.rsqrt(mean + 1e-06)
    gate_part = total[:, :units] * level
    up_part = total[:, units:] * level
    raised = gate_part / (1.0 + jnp.exp(-gate_part))
    total[:, :units] = raised * up_part * gate_ref[...]
    owner_rows, moved, groups = sizes
    line = sum(len(group) for group in groups)
    side_rows = total.shape[0] // 2
    order_at = 2 * len(spots)
    for first_row in (0, side_rows):
        for pair in range(side_rows // (2 * owner_rows)):
            pieces = []
            for j in (0, 1):
                row = first_row + place_ref[order_at + 2 * pair + j] * owner_rows
                row = pl.multiple_of(row, owner_rows)
                pieces.append(total[pl.ds(row, owner_rows), :units])
            row = first_row + 2 * pair * owner_rows
            activated[row : row + 2 * owner_rows, :] = jnp.concatenate(pieces).astype(BF16)
    down_copy.wait()
    width = down.shape[1] // 2
    tile = 512
    plane_rows = side_rows // 4
    copies = []
    for half in (0, 1):
        order = [*moved[half], *(group for group in range(4) if group not in moved[half])]
        for column in range(0, width, tile):
            product = jnp.dot(
                activated[...],
                down[:, half * width + column : half * width + column + tile],
                preferred_element_type=F32,
            ).astype(BF16)
            for side in (0, 1):
                source = 0
                for group in groups:
                    for place, at in enumerate(order):
                        size = len(group) * owner_rows
                        row = side * side_rows + at * plane_rows + source
                        target = half * 2 * side_rows + side * side_rows + 4 * source + place * size
                        results[target : target + size, column : column + tile] = product[
                            row : row + size, :
                        ]
                    source += size
        for side in (1, 0):
            source = 0
            for which, group in enumerate(groups):
                size = 4 * len(group) * owner_rows
                target = half * 2 * side_rows + side * side_rows + 4 * source
                copies.append(
                    pltpu.make_async_copy(
                        results.at[pl.ds(target, size)],
                        outs[2 * which + side].at[half],
                        sent.at[len(copies)],
                    )
                )
                copies[-1].start()
                source += len(group) * owner_rows
    for copy in copies:
        copy.wait()


def expert_rows(parts, other_parts, halves, gains, weights, place, carried, finish):
    model_width, double = weights.shape
    lanes = parts[0].shape[2]
    tokens = 2 * lanes
    blocks = [part.shape[0] for part in parts]
    heights = [part.shape[1] for part in parts]
    depth = sum(n * h for n, h in zip(blocks, heights))
    whole = pl.BlockSpec(memory_space=pltpu.VMEM)
    anywhere = pl.BlockSpec(memory_space=pl.ANY)
    sums = [jax.ShapeDtypeStruct((tokens, double), F32), jax.ShapeDtypeStruct((8, tokens), F32)]
    scratch = [
        pltpu.VMEM((depth, double), BF16),
        pltpu.VMEM((depth, tokens), BF16),
        pltpu.SemaphoreType.DMA((sum(blocks),)),
        pltpu.SemaphoreType.DMA((2 * sum(blocks),)),
    ]
    operands = [place, *parts, *other_parts, *gains, weights, *carried]
    in_specs = [pl.BlockSpec(memory_space=pltpu.SMEM)] + [anywhere] * (2 * len(parts))
    in_specs += [whole] * 2 + [anywhere] + [whole] * len(carried)
    sizes = None
    out_shape, out_specs = sums, [whole] * 2
    if finish is not None:
        gates, down, *sizes = finish
        operands += [gates, down]
        in_specs += [whole, anywhere]
        owner_rows, _, groups = sizes
        out_shape = [
            jax.ShapeDtypeStruct((2, 4 * len(group) * owner_rows, model_width // 2), BF16)
            for group in groups
            for _ in range(2)
        ]
        out_specs = [anywhere] * len(out_shape)
        scratch = [pltpu.VMEM(a.shape, F32) for a in sums] + scratch
        scratch += [
            pltpu.VMEM((tokens, double // 2), BF16),
            pltpu.VMEM((2 * tokens, model_width // 2), BF16),
            pltpu.VMEM(down.shape, BF16),
            pltpu.SemaphoreType.DMA,
            pltpu.SemaphoreType.DMA((2 * len(out_shape),)),
        ]
    return pl.pallas_call(
        functools.partial(
            expert_kernel,
            blocks=blocks,
            heights=heights,
            halves=halves,
            carried=len(carried) // 2,
            sizes=sizes,
        ),
        in_specs=in_specs,
        out_specs=out_specs,
        out_shape=out_shape,
        scratch_shapes=scratch,
        compiler_params=pltpu.CompilerParams(vmem_limit_bytes=VMEM_LIMIT),
        cost_estimate=pl.CostEstimate(
            flops=2 * tokens * depth * double,
            bytes_accessed=2 * depth * (double + tokens),
            transcendentals=0,
        ),
    )(*operands)


def on_device(
    queries,
    latent_cache,
    lengths,
    value_lift,
    output_map,
    residual,
    norm_gain,
    expert_ids,
    gate_values,
    expert_in,
    expert_down,
):
    request_count = queries.shape[0]
    latent_width = value_lift.shape[1]
    half_heads = value_lift.shape[0]
    value_width = value_lift.shape[2]
    token_count, model_width = residual.shape
    chips = lax.axis_size("dev")
    plane = 4
    line = chips // plane
    columns = output_map.shape[1]
    experts = chips // 2
    units = expert_down.shape[1]
    side = lax.axis_index("side")
    chip = lax.axis_index("dev")
    line_at, plane_at = chip // plane, chip % plane
    half_tokens = token_count * chips

    def line_hop(value, k):
        return hop(value, "dev", chips, k * plane)

    def plane_hop(value, k):
        return hop(value, "dev", chips, k)

    def swap(value):
        return hop(value, "side", 2, 1)

    def placed(offsets):
        return [(line_at ^ k_line) * plane + (plane_at ^ k_plane) for k_plane, k_line in offsets]

    chosen = expert_ids[:, :, None] == jnp.arange(experts, dtype=jnp.int32)[None, None, :]
    weights = jnp.sum(jnp.where(chosen, gate_values[:, :, None], 0.0), axis=1)
    weights_high = lax.reduce_precision(weights, 8, 7)
    weight_terms = jnp.concatenate([weights_high, weights - weights_high], axis=1).astype(BF16)
    weight_width = -(-token_count * 2 * experts // (request_count * 128)) * 128
    weight_block = jnp.pad(
        weight_terms.reshape(-1), (0, request_count * weight_width - weight_terms.size)
    ).reshape(request_count, weight_width)

    own_latent, sent_latent, stats = attend(
        queries, latent_cache.swapaxes(1, 2), lengths, side, latent_width
    )
    stats = stats[:, :, :2]

    def heads_of(value, which):
        return lax.dynamic_slice_in_dim(value, which * half_heads, half_heads, 1)

    other_latent = swap(sent_latent)
    other_stats = swap(heads_of(stats, 1 - side))
    own_stats = heads_of(stats, side)
    top = jnp.maximum(own_stats[:, :, 0], other_stats[:, :, 0])
    own_share = own_stats[:, :, 1] * jnp.exp(own_stats[:, :, 0] - top)
    other_share = other_stats[:, :, 1] * jnp.exp(other_stats[:, :, 0] - top)
    share_sum = own_share + other_share
    latent_out = (
        own_latent.astype(F32) * (own_share / share_sum)[:, :, None]
        + other_latent.astype(F32) * (other_share / share_sum)[:, :, None]
    ).astype(BF16)
    head_values = jnp.einsum("rhc,hcv->rhv", latent_out, value_lift, preferred_element_type=F32)
    head_values = head_values.astype(BF16).reshape(request_count, half_heads * value_width)

    groups = [list(range(line))]

    half_depth = half_heads * value_width // 2
    first_width = half_depth + weight_width
    sent = jnp.concatenate(
        [head_values[:, :half_depth], weight_block, head_values[:, half_depth:]], axis=1
    )
    sent, residual, expert_in, norm_gain = lax.optimization_barrier(
        (sent, residual, expert_in, norm_gain)
    )

    residual_blocks = residual.reshape(token_count, chips, columns).swapaxes(0, 1)
    residual_columns = lax.all_to_all(
        residual_blocks, "dev", split_axis=0, concat_axis=0, tiled=True
    )
    residual_columns = residual_columns.reshape(half_tokens, columns).T
    (first, second), in_rows = gather(
        sent,
        lambda column: (column[:, :, :first_width], column[:, :, first_width:]),
        groups,
        line_hop,
        plane_hop,
        expert_in.reshape(model_width, 2 * units),
    )
    place = jnp.stack(
        [
            at
            for half in (first, second)
            for _, offsets in half
            for at in placed(offsets)
        ]
        + [side]
    ).astype(jnp.int32)
    first_parts, second_parts = [[part for part, _ in half] for half in (first, second)]
    own_columns, sent_columns = project(first_parts, second_parts, output_map.T, place)
    attention = own_columns + swap(sent_columns).astype(F32)
    hidden = (residual_columns.astype(F32) + attention).astype(BF16)

    gathered = jnp.concatenate([part[:, :, half_depth:] for part, _ in first])
    gathered = gathered.reshape(chips, -1)[:, : token_count * 2 * experts]
    gathered = gathered.reshape(chips, token_count, 2, experts).astype(F32)
    gathered = lax.dynamic_index_in_dim(gathered, chip // 2, 3, keepdims=False).sum(axis=2)
    spots = place[:chips]
    own_gates = jnp.zeros((chips, token_count), F32).at[spots].set(gathered).reshape(-1, 1)
    gates = jnp.concatenate([own_gates, swap(own_gates)])

    first_rows = -(-columns // 32) * 16
    gains = norm_gain.astype(F32).reshape(chips, columns)
    gains = [gains[:, :first_rows], gains[:, first_rows:]]
    back_groups = [list(range(line))]
    hidden_groups = [list(range(line))]
    (first, second), gates = gather(
        hidden,
        lambda column: (column[:, :first_rows], column[:, first_rows:]),
        hidden_groups,
        line_hop,
        plane_hop,
        gates,
    )
    down = expert_down[0]
    out_at = [(p, k) for p in range(plane) for k in range(line)]
    moved = ((1, 3), (2, 3))
    stages = [[0], [1], [2]]
    carried = ()
    for at, stage in enumerate(stages):
        last = at == len(stages) - 1
        parts, halves, spots = [], [], []
        for which in stage:
            for half, (part, offsets) in enumerate((first[which], second[which])):
                parts.append(part)
                halves.append(half)
                spots += [(spot, half) for spot in placed(offsets)]
        table = [spot * columns + half * first_rows for spot, half in spots]
        table += [spot for spot, _ in spots]
        if last:
            parts, carried = lax.optimization_barrier((parts, carried))
            table += placed((p, k) for p in range(plane) for g in back_groups for k in g)
        carried = expert_rows(
            parts,
            [swap(part) for part in parts],
            halves,
            gains,
            in_rows,
            jnp.stack(table).astype(jnp.int32),
            carried,
            (gates, down, token_count, moved, back_groups) if last else None,
        )

    routed_sum = 0.0
    sent_sum = None
    for at, group in enumerate(back_groups):
        own, other = carried[2 * at : 2 * at + 2]
        if sent_sum is not None:
            other, _ = lax.optimization_barrier((other, sent_sum))
        other = swap(other)
        half_sums = []
        for half, (one, two) in enumerate(((1, 2), (2, 1))):
            rows = own.shape[1] // 2
            moved_sum = own[half, :rows].astype(F32) + other[half, :rows].astype(F32)
            sent_sum = moved_sum.astype(BF16)
            kept_sum = own[half, rows:].astype(F32) + other[half, rows:].astype(F32)
            kept_sum = kept_sum + plane_hop(sent_sum, one).astype(F32)
            rows = rows // 2
            arrived = plane_hop(kept_sum[rows:].astype(BF16), two).astype(F32)
            half_sums.append(kept_sum[:rows] + arrived)
        plane_sum = jnp.concatenate(half_sums, axis=1).reshape(len(group), token_count, model_width)
        for place_at, k in enumerate(group):
            if k:
                routed_sum += line_hop(plane_sum[place_at].astype(BF16), k).astype(F32)
            else:
                routed_sum += plane_sum[place_at]

    tokens = chip * token_count + jnp.arange(token_count, dtype=jnp.int32)
    picked = (tokens[:, None] == jnp.arange(half_tokens, dtype=jnp.int32)[None, :]).astype(BF16)
    own_parts, _ = lax.optimization_barrier(([part for half in (first, second) for part, _ in half], sent_sum))
    own_rows = []
    for half, parts in ((first, own_parts[: len(first)]), (second, own_parts[len(first) :])):
        blocks = jnp.concatenate(
            [jnp.einsum("qt,krt->kqr", picked, part, preferred_element_type=F32) for part in parts]
        )
        offsets = [at for _, part_offsets in half for at in part_offsets]
        spots = jnp.stack(placed(offsets))
        own_rows.append(jnp.zeros_like(blocks).at[spots].set(blocks))
    own_hidden = jnp.concatenate(own_rows, axis=2).swapaxes(0, 1).reshape(token_count, model_width)
    return (own_hidden + routed_sum).astype(BF16)


def solution(mesh):
    in_specs = (
        P("dev", None, None),
        P("dev", "side", None),
        P("dev"),
        P("side", None, None),
        P("side", "dev"),
        P(("side", "dev"), None),
        P(),
        P(("side", "dev"), None),
        P(("side", "dev"), None),
        P("dev", None, None, "side"),
        P("dev", "side", None),
    )
    out_specs = P(("side", "dev"), None)
    return jax.shard_map(
        on_device, mesh=mesh, in_specs=in_specs, out_specs=out_specs, check_vma=False
    )
```

```python
import functools

import jax
import jax.numpy as jnp
from jax import lax
from jax.experimental import pallas as pl
from jax.experimental.pallas import tpu as pltpu
from jax.sharding import PartitionSpec as P

QKD = 192
F32 = jnp.float32
BF16 = jnp.bfloat16
VMEM_LIMIT = 48 * 2**20
LAST_VMEM_LIMIT = 52 * 2**20


def hop(value, axis, size, mask):
    return lax.ppermute(value, axis, [(i, i ^ mask) for i in range(size)])


def gather(block, split, groups, line_hop, plane_hop, beside, after):
    arrived = {0: block}
    for group in groups:
        for k in group:
            if k:
                arrived[k] = line_hop(block, k)
    halves = ([], [])
    for at, group in enumerate(groups):
        if at == 0 and len(group) > 1:
            block, arrived[group[1]] = lax.optimization_barrier((block, arrived[group[1]]))
            arrived[0] = block
        column = jnp.stack([arrived[k] for k in group])
        if at == len(groups) - 1:
            column, beside = lax.optimization_barrier((column, beside))
        split_column = split(column)
        nears = [plane_hop(half, one) for half, one in zip(split_column, (1, 2))]
        if at == len(groups) - 1:
            nears, after = lax.optimization_barrier((nears, after))
        for parts, half, near, (one, two) in zip(halves, split_column, nears, ((1, 2), (2, 1))):
            rest = plane_hop(jnp.concatenate([half, near]), two)
            parts.append((half, [(0, k) for k in group]))
            parts.append((near, [(one, k) for k in group]))
            parts.append((rest, [(p, k) for p in (two, 3) for k in group]))
    return halves, beside, after


def attend_kernel(length_ref, query_ref, cache_ref, own_ref, other_ref, stats_ref, latents, *, scale):
    group, heads, _ = query_ref.shape
    latent_width = own_ref.shape[2]
    slots = cache_ref.shape[2]
    half = heads // 2
    first = pl.program_id(0) * group
    side = length_ref[length_ref.shape[0] - 1]
    positions = side * slots + lax.broadcasted_iota(jnp.int32, (heads, slots), 1)
    lanes = lax.broadcasted_iota(jnp.int32, (heads, stats_ref.shape[2]), 1)
    everyone = range(group)
    usable = [positions < length_ref[first + at] for at in everyone]
    scores = [
        jnp.dot(query_ref[at], cache_ref[at], preferred_element_type=F32) * scale for at in everyone
    ]
    masked = [jnp.where(usable[at], scores[at], -1e30) for at in everyone]
    tops = [jnp.max(masked[at], axis=1, keepdims=True) for at in everyone]
    raised = [jnp.where(usable[at], jnp.exp(masked[at] - tops[at]), 0.0) for at in everyone]
    totals = [jnp.sum(raised[at], axis=1, keepdims=True) for at in everyone]
    sums = [
        lax.dot_general(
            raised[at].astype(BF16),
            cache_ref[at, :latent_width, :],
            (((1,), (1,)), ((), ())),
            preferred_element_type=F32,
        )
        for at in everyone
    ]
    for at in everyone:
        latents[at] = sums[at] / jnp.maximum(totals[at], 1e-30)
        stats_ref[at] = jnp.where(lanes == 0, tops[at], totals[at])
    for at in everyone:
        own_ref[at] = latents[at, pl.ds(pl.multiple_of(side * half, half), half), :].astype(BF16)
        other_ref[at] = latents[
            at, pl.ds(pl.multiple_of((1 - side) * half, half), half), :
        ].astype(BF16)


def attend(queries, cache_columns, lengths, side, latent_width):
    requests, heads, width = queries.shape
    slots = cache_columns.shape[2]
    group = 4
    table = jnp.concatenate([lengths, side.reshape(1)]).astype(jnp.int32)
    return pl.pallas_call(
        functools.partial(attend_kernel, scale=QKD ** (-0.5)),
        grid_spec=pltpu.PrefetchScalarGridSpec(
            num_scalar_prefetch=1,
            grid=(requests // group,),
            in_specs=[
                pl.BlockSpec((group, heads, width), lambda r, table: (r, 0, 0)),
                pl.BlockSpec((group, width, slots), lambda r, table: (r, 0, 0)),
            ],
            out_specs=[
                pl.BlockSpec((group, heads // 2, latent_width), lambda r, table: (r, 0, 0)),
                pl.BlockSpec((group, heads // 2, latent_width), lambda r, table: (r, 0, 0)),
                pl.BlockSpec((group, heads, 128), lambda r, table: (r, 0, 0)),
            ],
            scratch_shapes=[pltpu.VMEM((group, heads, latent_width), F32)],
        ),
        out_shape=[
            jax.ShapeDtypeStruct((requests, heads // 2, latent_width), BF16),
            jax.ShapeDtypeStruct((requests, heads // 2, latent_width), BF16),
            jax.ShapeDtypeStruct((requests, heads, 128), F32),
        ],
        compiler_params=pltpu.CompilerParams(vmem_limit_bytes=48 * 2**20),
        cost_estimate=pl.CostEstimate(
            flops=4 * requests * heads * width * slots,
            bytes_accessed=2 * requests * width * (heads + slots),
            transcendentals=requests * heads * slots,
        ),
    )(table, queries, cache_columns)


def project_kernel(place_ref, *refs, counts, rows, depths, steps):
    groups = len(counts)
    parts = (refs[:groups], refs[groups : 2 * groups])
    map_ref, own_ref, send_ref, first, second, mapping, total, arrived, map_arrived = refs[2 * groups :]
    blocks = sum(counts)
    copies, map_copies = [], []
    for half, left in enumerate((first, second)):
        at = half * blocks
        for part, count in zip(parts[half], counts):
            for k in range(count):
                row = pl.multiple_of(place_ref[at] * rows, rows)
                copies.append(
                    pltpu.make_async_copy(part.at[k], left.at[pl.ds(row, rows)], arrived.at[at])
                )
                at += 1
    tile = mapping.shape[1] // steps
    for step in range(steps):
        columns = pl.ds(step * tile, tile)
        map_copies.append(
            pltpu.make_async_copy(
                map_ref.at[:, columns], mapping.at[:, columns], map_arrived.at[step]
            )
        )
    in_half = steps // 2
    for half in (0, 1):
        for copy in copies[half * blocks : (half + 1) * blocks]:
            copy.start()
        for copy in map_copies[half * in_half : (half + 1) * in_half]:
            copy.start()
    for step in range(steps):
        if step % in_half == 0:
            half = step // in_half
            for copy in copies[half * blocks : (half + 1) * blocks]:
                copy.wait()
        map_copies[step].wait()
        left = first if step * tile < depths else second
        column = step * tile if step * tile < depths else step * tile - depths
        term = lax.dot_general(
            left[:, column : column + tile],
            mapping[:, step * tile : (step + 1) * tile],
            (((1,), (1,)), ((), ())),
            preferred_element_type=F32,
        )
        if step:
            total[...] += term
        else:
            total[...] = term
    half_rows = total.shape[0] // 2
    side = place_ref[2 * blocks]
    own_ref[...] = total[pl.ds(pl.multiple_of(side * half_rows, half_rows), half_rows), :].T
    send_ref[...] = total[
        pl.ds(pl.multiple_of((1 - side) * half_rows, half_rows), half_rows), :
    ].T.astype(BF16)


def project(first, second, columns_map, place):
    width, depth = columns_map.shape
    rows = first[0].shape[1]
    counts = [part.shape[0] for part in first]
    total_rows = rows * sum(counts)
    steps = 4
    anywhere = pl.BlockSpec(memory_space=pl.ANY)
    whole = pl.BlockSpec(memory_space=pltpu.VMEM)
    return pl.pallas_call(
        functools.partial(
            project_kernel, counts=counts, rows=rows, depths=depth // 2, steps=steps
        ),
        in_specs=[pl.BlockSpec(memory_space=pltpu.SMEM)] + [anywhere] * (2 * len(counts) + 1),
        out_specs=[whole] * 2,
        out_shape=[
            jax.ShapeDtypeStruct((width, total_rows // 2), F32),
            jax.ShapeDtypeStruct((width, total_rows // 2), BF16),
        ],
        scratch_shapes=[
            pltpu.VMEM((total_rows, first[0].shape[2]), BF16),
            pltpu.VMEM((total_rows, second[0].shape[2]), BF16),
            pltpu.VMEM((width, depth), BF16),
            pltpu.VMEM((total_rows, width), F32),
            pltpu.SemaphoreType.DMA((2 * sum(counts),)),
            pltpu.SemaphoreType.DMA((steps,)),
        ],
        compiler_params=pltpu.CompilerParams(vmem_limit_bytes=60 * 2**20),
        cost_estimate=pl.CostEstimate(
            flops=2 * total_rows * depth * width,
            bytes_accessed=2 * (total_rows * depth + depth * width),
            transcendentals=0,
        ),
    )(place, *first, *second, columns_map)


def expert_kernel(place_ref, *refs, blocks, heights, halves, carried, sizes):
    count = len(blocks)
    own, other, refs = refs[:count], refs[count : 2 * count], refs[2 * count :]
    gain_refs, in_ref, refs = refs[:2], refs[2], refs[3:]
    sums_in, refs = refs[: 2 * carried], refs[2 * carried :]
    if sizes:
        gate_ref, down_ref, *refs = refs
        outs, refs = refs[: 4 * len(sizes[2])], refs[4 * len(sizes[2]) :]
        total, squares, weights, rows, arrived, part_arrived = refs[:6]
        activated, results, down, down_arrived, sent = refs[6:]
        down_copy = pltpu.make_async_copy(down_ref, down, down_arrived)
    else:
        total, squares, weights, rows, arrived, part_arrived = refs
    lanes = rows.shape[1] // 2
    offsets = [sum(n * h for n, h in zip(blocks[:at], heights[:at])) for at in range(count + 1)]
    spots = []
    for entry in range(count):
        for k in range(blocks[entry]):
            row = offsets[entry] + k * heights[entry]
            spots.append((entry, k, row, heights[entry]))
    part_copies, weight_copies = [], []
    for at, (entry, k, row, height) in enumerate(spots):
        for side, ref in enumerate((own[entry], other[entry])):
            part_copies.append(
                pltpu.make_async_copy(
                    ref.at[k],
                    rows.at[pl.ds(row, height), pl.ds(side * lanes, lanes)],
                    part_arrived.at[2 * at + side],
                )
            )
        source = pl.multiple_of(place_ref[at], 8)
        weight_copies.append(
            pltpu.make_async_copy(
                in_ref.at[pl.ds(source, height)], weights.at[pl.ds(row, height)], arrived.at[at]
            )
        )
    for copy in part_copies + weight_copies:
        copy.start()
    if sizes:
        down_copy.start()
    if sums_in:
        squares[...] = sums_in[1][...]
    else:
        squares[...] = jnp.zeros_like(squares)
    diagonals = {
        height: lax.broadcasted_iota(jnp.int32, (height, height), 0)
        == lax.broadcasted_iota(jnp.int32, (height, height), 1)
        for height in set(heights)
    }
    for at, (entry, k, row, height) in enumerate(spots):
        part_copies[2 * at].wait()
        part_copies[2 * at + 1].wait()
        wide = rows[row : row + height].astype(F32)
        squares[...] += jnp.sum((wide * wide).reshape(height // 8, 8, 2 * lanes), axis=0)
        gain = gain_refs[halves[entry]][pl.ds(place_ref[len(spots) + at], 1), :]
        gain = jnp.where(diagonals[height], gain, 0.0).astype(BF16)
        rows[row : row + height] = jnp.dot(
            gain, rows[row : row + height], preferred_element_type=F32
        ).astype(BF16)
    for entry in range(count):
        for at, spot in enumerate(spots):
            if spot[0] == entry:
                weight_copies[at].wait()
        term = lax.dot_general(
            rows[offsets[entry] : offsets[entry + 1]],
            weights[offsets[entry] : offsets[entry + 1]],
            (((0,), (0,)), ((), ())),
            preferred_element_type=F32,
        )
        if entry:
            total[...] += term
        elif sums_in:
            total[...] = sums_in[0][...] + term
        else:
            total[...] = term
    if not sizes:
        return

    units = total.shape[1] // 2
    mean = jnp.sum(squares[...].T, axis=1, keepdims=True) / in_ref.shape[0]
    level = lax.rsqrt(mean + 1e-06)
    gate_part = total[:, :units] * level
    up_part = total[:, units:] * level
    raised = gate_part / (1.0 + jnp.exp(-gate_part))
    total[:, :units] = raised * up_part * gate_ref[...]
    owner_rows, moved, groups = sizes
    line = sum(len(group) for group in groups)
    side_rows = total.shape[0] // 2
    order_at = 2 * len(spots)
    for first_row in (0, side_rows):
        for pair in range(side_rows // (2 * owner_rows)):
            pieces = []
            for j in (0, 1):
                row = first_row + place_ref[order_at + 2 * pair + j] * owner_rows
                row = pl.multiple_of(row, owner_rows)
                pieces.append(total[pl.ds(row, owner_rows), :units])
            row = first_row + 2 * pair * owner_rows
            activated[row : row + 2 * owner_rows, :] = jnp.concatenate(pieces).astype(BF16)
    down_copy.wait()
    width = down.shape[1] // 2
    tile = 512
    plane_rows = side_rows // 4
    copies = []
    for half in (0, 1):
        order = [*moved[half], *(group for group in range(4) if group not in moved[half])]
        for column in range(0, width, tile):
            product = jnp.dot(
                activated[...],
                down[:, half * width + column : half * width + column + tile],
                preferred_element_type=F32,
            ).astype(BF16)
            for side in (0, 1):
                source = 0
                for group in groups:
                    for place, at in enumerate(order):
                        size = len(group) * owner_rows
                        row = side * side_rows + at * plane_rows + source
                        target = half * 2 * side_rows + side * side_rows + 4 * source + place * size
                        results[target : target + size, column : column + tile] = product[
                            row : row + size, :
                        ]
                    source += size
        for side in (1, 0):
            source = 0
            for which, group in enumerate(groups):
                size = 4 * len(group) * owner_rows
                target = half * 2 * side_rows + side * side_rows + 4 * source
                copies.append(
                    pltpu.make_async_copy(
                        results.at[pl.ds(target, size)],
                        outs[4 * which + 2 * half + side],
                        sent.at[len(copies)],
                    )
                )
                copies[-1].start()
                source += len(group) * owner_rows
    for copy in copies:
        copy.wait()


def expert_rows(parts, other_parts, halves, gains, weights, place, carried, finish):
    model_width, double = weights.shape
    lanes = parts[0].shape[2]
    tokens = 2 * lanes
    blocks = [part.shape[0] for part in parts]
    heights = [part.shape[1] for part in parts]
    depth = sum(n * h for n, h in zip(blocks, heights))
    whole = pl.BlockSpec(memory_space=pltpu.VMEM)
    anywhere = pl.BlockSpec(memory_space=pl.ANY)
    sums = [jax.ShapeDtypeStruct((tokens, double), F32), jax.ShapeDtypeStruct((8, tokens), F32)]
    scratch = [
        pltpu.VMEM((depth, double), BF16),
        pltpu.VMEM((depth, tokens), BF16),
        pltpu.SemaphoreType.DMA((sum(blocks),)),
        pltpu.SemaphoreType.DMA((2 * sum(blocks),)),
    ]
    operands = [place, *parts, *other_parts, *gains, weights, *carried]
    in_specs = [pl.BlockSpec(memory_space=pltpu.SMEM)] + [anywhere] * (2 * len(parts))
    in_specs += [whole] * 2 + [anywhere] + [whole] * len(carried)
    sizes = None
    out_shape, out_specs = sums, [whole] * 2
    if finish is not None:
        gates, down, *sizes = finish
        operands += [gates, down]
        in_specs += [whole, anywhere]
        owner_rows, _, groups = sizes
        out_shape = [
            jax.ShapeDtypeStruct((4 * len(group) * owner_rows, model_width // 2), BF16)
            for group in groups
            for _ in range(4)
        ]
        out_specs = [anywhere] * len(out_shape)
        scratch = [pltpu.VMEM(a.shape, F32) for a in sums] + scratch
        scratch += [
            pltpu.VMEM((tokens, double // 2), BF16),
            pltpu.VMEM((2 * tokens, model_width // 2), BF16),
            pltpu.VMEM(down.shape, BF16),
            pltpu.SemaphoreType.DMA,
            pltpu.SemaphoreType.DMA((len(out_shape),)),
        ]
    return pl.pallas_call(
        functools.partial(
            expert_kernel,
            blocks=blocks,
            heights=heights,
            halves=halves,
            carried=len(carried) // 2,
            sizes=sizes,
        ),
        in_specs=in_specs,
        out_specs=out_specs,
        out_shape=out_shape,
        scratch_shapes=scratch,
        compiler_params=pltpu.CompilerParams(
            vmem_limit_bytes=VMEM_LIMIT if finish is None else LAST_VMEM_LIMIT
        ),
        cost_estimate=pl.CostEstimate(
            flops=2 * tokens * depth * double,
            bytes_accessed=2 * depth * (double + tokens),
            transcendentals=0,
        ),
    )(*operands)


def on_device(
    queries,
    latent_cache,
    lengths,
    value_lift,
    output_map,
    residual,
    norm_gain,
    expert_ids,
    gate_values,
    expert_in,
    expert_down,
):
    request_count = queries.shape[0]
    latent_width = value_lift.shape[1]
    half_heads = value_lift.shape[0]
    value_width = value_lift.shape[2]
    token_count, model_width = residual.shape
    chips = lax.axis_size("dev")
    plane = 4
    line = chips // plane
    columns = output_map.shape[1]
    experts = chips // 2
    units = expert_down.shape[1]
    side = lax.axis_index("side")
    chip = lax.axis_index("dev")
    line_at, plane_at = chip // plane, chip % plane
    half_tokens = token_count * chips

    def line_hop(value, k):
        return hop(value, "dev", chips, k * plane)

    def plane_hop(value, k):
        return hop(value, "dev", chips, k)

    def swap(value):
        return hop(value, "side", 2, 1)

    def placed(offsets):
        return [(line_at ^ k_line) * plane + (plane_at ^ k_plane) for k_plane, k_line in offsets]

    chosen = expert_ids[:, :, None] == jnp.arange(experts, dtype=jnp.int32)[None, None, :]
    weights = jnp.sum(jnp.where(chosen, gate_values[:, :, None], 0.0), axis=1)
    weights_high = lax.reduce_precision(weights, 8, 7)
    weight_terms = jnp.concatenate([weights_high, weights - weights_high], axis=1).astype(BF16)
    weight_width = -(-token_count * 2 * experts // (request_count * 128)) * 128
    weight_block = jnp.pad(
        weight_terms.reshape(-1), (0, request_count * weight_width - weight_terms.size)
    ).reshape(request_count, weight_width)

    own_latent, sent_latent, stats = attend(
        queries, latent_cache.swapaxes(1, 2), lengths, side, latent_width
    )
    stats = stats[:, :, :2]

    def heads_of(value, which):
        return lax.dynamic_slice_in_dim(value, which * half_heads, half_heads, 1)

    other_latent = swap(sent_latent)
    other_stats = swap(heads_of(stats, 1 - side))
    own_stats = heads_of(stats, side)
    top = jnp.maximum(own_stats[:, :, 0], other_stats[:, :, 0])
    own_share = own_stats[:, :, 1] * jnp.exp(own_stats[:, :, 0] - top)
    other_share = other_stats[:, :, 1] * jnp.exp(other_stats[:, :, 0] - top)
    share_sum = own_share + other_share
    latent_out = (
        own_latent.astype(F32) * (own_share / share_sum)[:, :, None]
        + other_latent.astype(F32) * (other_share / share_sum)[:, :, None]
    ).astype(BF16)
    head_values = jnp.einsum("rhc,hcv->rhv", latent_out, value_lift, preferred_element_type=F32)
    head_values = head_values.astype(BF16).reshape(request_count, half_heads * value_width)

    groups = [list(range(line // 2)), list(range(line // 2, line))]

    half_depth = half_heads * value_width // 2
    first_width = half_depth + weight_width
    sent = jnp.concatenate(
        [head_values[:, :half_depth], weight_block, head_values[:, half_depth:]], axis=1
    )
    sent, residual, expert_in, norm_gain = lax.optimization_barrier(
        (sent, residual, expert_in, norm_gain)
    )

    (first, second), in_rows, residual = gather(
        sent,
        lambda column: (column[:, :, :first_width], column[:, :, first_width:]),
        groups,
        line_hop,
        plane_hop,
        expert_in.reshape(model_width, 2 * units),
        residual,
    )

    residual_blocks = residual.reshape(token_count, chips, columns).swapaxes(0, 1)
    residual_columns = lax.all_to_all(
        residual_blocks, "dev", split_axis=0, concat_axis=0, tiled=True
    )

    place = jnp.stack(
        [
            at
            for half in (first, second)
            for _, offsets in half
            for at in placed(offsets)
        ]
        + [side]
    ).astype(jnp.int32)
    first_parts, second_parts = [[part for part, _ in half] for half in (first, second)]
    own_columns, sent_columns = project(first_parts, second_parts, output_map.T, place)
    sent_columns, residual_columns = lax.optimization_barrier((sent_columns, residual_columns))
    residual_columns = residual_columns.reshape(half_tokens, columns).T
    attention = own_columns + swap(sent_columns).astype(F32)
    hidden = (residual_columns.astype(F32) + attention).astype(BF16)

    gathered = jnp.concatenate([part[:, :, half_depth:] for part, _ in first])
    gathered = gathered.reshape(chips, -1)[:, : token_count * 2 * experts]
    gathered = gathered.reshape(chips, token_count, 2, experts).astype(F32)
    gathered = lax.dynamic_index_in_dim(gathered, chip // 2, 3, keepdims=False).sum(axis=2)
    spots = place[:chips]
    own_gates = jnp.zeros((chips, token_count), F32).at[spots].set(gathered).reshape(-1, 1)
    gates = jnp.concatenate([own_gates, swap(own_gates)])

    first_rows = -(-columns // 32) * 16
    gains = norm_gain.astype(F32).reshape(chips, columns)
    gains = [gains[:, :first_rows], gains[:, first_rows:]]
    back_groups = [list(range(line))]
    hidden_groups = [list(range(line))]
    (first, second), gates, _ = gather(
        hidden,
        lambda column: (column[:, :first_rows], column[:, first_rows:]),
        hidden_groups,
        line_hop,
        plane_hop,
        gates,
        (),
    )
    down = expert_down[0]
    out_at = [(p, k) for p in range(plane) for k in range(line)]
    moved = ((1, 3), (2, 3))
    stages = [[0], [1], [2]]
    carried = ()
    for at, stage in enumerate(stages):
        last = at == len(stages) - 1
        parts, halves, spots = [], [], []
        for which in stage:
            for half, (part, offsets) in enumerate((first[which], second[which])):
                parts.append(part)
                halves.append(half)
                spots += [(spot, half) for spot in placed(offsets)]
        table = [spot * columns + half * first_rows for spot, half in spots]
        table += [spot for spot, _ in spots]
        if last:
            parts, carried = lax.optimization_barrier((parts, carried))
            table += placed((p, k) for p in range(plane) for g in back_groups for k in g)
        carried = expert_rows(
            parts,
            [swap(part) for part in parts],
            halves,
            gains,
            in_rows,
            jnp.stack(table).astype(jnp.int32),
            carried,
            (gates, down, token_count, moved, back_groups) if last else None,
        )

    orders = ((1, 2), (2, 1))
    group_count = len(back_groups)
    kept, sent = [], []
    for at in range(group_count):
        own, other = carried[4 * at : 4 * at + 4 : 2], carried[4 * at + 1 : 4 * at + 4 : 2]
        if at:
            other, _ = lax.optimization_barrier((other, sent[-1]))
        other = [swap(half) for half in other]
        rows = own[0].shape[0] // 2
        sent.append(
            [
                (own[h][:rows].astype(F32) + other[h][:rows].astype(F32)).astype(BF16)
                for h in (0, 1)
            ]
        )
        kept.append([own[h][rows:].astype(F32) + other[h][rows:].astype(F32) for h in (0, 1)])
    sent_sum = sent[0]
    passed, whole = [], []
    for at in range(group_count):
        arrived = [plane_hop(sent[at][h], orders[h][0]) for h in (0, 1)]
        summed = [kept[at][h] + arrived[h].astype(F32) for h in (0, 1)]
        rows = summed[0].shape[0] // 2
        passed.append([summed[h][rows:].astype(BF16) for h in (0, 1)])
        whole.append([summed[h][:rows] for h in (0, 1)])
    routed_sum = 0.0
    for at, group in enumerate(back_groups):
        moving = passed[at]
        if at + 1 < group_count:
            moving, _ = lax.optimization_barrier((moving, sent[at + 1]))
        arrived = [plane_hop(moving[h], orders[h][1]) for h in (0, 1)]
        plane_sum = [whole[at][h] + arrived[h].astype(F32) for h in (0, 1)]
        plane_sum = jnp.concatenate(plane_sum, axis=1).reshape(len(group), token_count, model_width)
        leaving = [plane_sum[place_at].astype(BF16) if k else None for place_at, k in enumerate(group)]
        if at + 1 < group_count:
            leaving, _ = lax.optimization_barrier((leaving, passed[at + 1]))
        for place_at, k in enumerate(group):
            if k:
                routed_sum += line_hop(leaving[place_at], k).astype(F32)
            else:
                routed_sum += plane_sum[place_at]

    tokens = chip * token_count + jnp.arange(token_count, dtype=jnp.int32)
    picked = (tokens[:, None] == jnp.arange(half_tokens, dtype=jnp.int32)[None, :]).astype(BF16)
    own_parts, _ = lax.optimization_barrier(([part for half in (first, second) for part, _ in half], sent_sum))
    own_rows = []
    for half, parts in ((first, own_parts[: len(first)]), (second, own_parts[len(first) :])):
        blocks = jnp.concatenate(
            [jnp.einsum("qt,krt->kqr", picked, part, preferred_element_type=F32) for part in parts]
        )
        offsets = [at for _, part_offsets in half for at in part_offsets]
        spots = jnp.stack(placed(offsets))
        own_rows.append(jnp.zeros_like(blocks).at[spots].set(blocks))
    own_hidden = jnp.concatenate(own_rows, axis=2).swapaxes(0, 1).reshape(token_count, model_width)
    return (own_hidden + routed_sum).astype(BF16)


def solution(mesh):
    in_specs = (
        P("dev", None, None),
        P("dev", "side", None),
        P("dev"),
        P("side", None, None),
        P("side", "dev"),
        P(("side", "dev"), None),
        P(),
        P(("side", "dev"), None),
        P(("side", "dev"), None),
        P("dev", None, None, "side"),
        P("dev", "side", None),
    )
    out_specs = P(("side", "dev"), None)
    return jax.shard_map(
        on_device, mesh=mesh, in_specs=in_specs, out_specs=out_specs, check_vma=False
    )
```

```python
import functools

import jax
import jax.numpy as jnp
from jax import lax
from jax.experimental import pallas as pl
from jax.experimental.pallas import tpu as pltpu
from jax.sharding import PartitionSpec as P

QKD = 192
F32 = jnp.float32
BF16 = jnp.bfloat16
VMEM_LIMIT = 48 * 2**20
LAST_VMEM_LIMIT = 52 * 2**20


def hop(value, axis, size, mask):
    return lax.ppermute(value, axis, [(i, i ^ mask) for i in range(size)])


def gather(block, split, groups, line_hop, plane_hop, beside, after):
    arrived = {0: block}
    for group in groups:
        for k in group:
            if k:
                arrived[k] = line_hop(block, k)
    halves = ([], [])
    for at, group in enumerate(groups):
        if at == 0 and len(group) > 1:
            block, arrived[group[1]] = lax.optimization_barrier((block, arrived[group[1]]))
            arrived[0] = block
        column = jnp.stack([arrived[k] for k in group])
        if at == len(groups) - 1:
            column, beside = lax.optimization_barrier((column, beside))
        split_column = split(column)
        nears = [plane_hop(half, one) for half, one in zip(split_column, (1, 2))]
        if at == len(groups) - 1:
            nears, after = lax.optimization_barrier((nears, after))
        for parts, half, near, (one, two) in zip(halves, split_column, nears, ((1, 2), (2, 1))):
            rest = plane_hop(jnp.concatenate([half, near]), two)
            parts.append((half, [(0, k) for k in group]))
            parts.append((near, [(one, k) for k in group]))
            parts.append((rest, [(p, k) for p in (two, 3) for k in group]))
    return halves, beside, after


def attend_kernel(
    length_ref, side_ref, query_ref, cache_ref, own_ref, other_ref, stats_ref, latents, *, scale
):
    group, heads, _ = query_ref.shape
    latent_width = own_ref.shape[2]
    slots = cache_ref.shape[2]
    half = heads // 2
    first = pl.program_id(0) * group
    side = side_ref[0]
    positions = side * slots + lax.broadcasted_iota(jnp.int32, (heads, slots), 1)
    lanes = lax.broadcasted_iota(jnp.int32, (heads, stats_ref.shape[2]), 1)
    everyone = range(group)
    usable = [positions < length_ref[first + at] for at in everyone]
    scores = [
        jnp.dot(query_ref[at], cache_ref[at], preferred_element_type=F32) * scale for at in everyone
    ]
    masked = [jnp.where(usable[at], scores[at], -1e30) for at in everyone]
    tops = [jnp.max(masked[at], axis=1, keepdims=True) for at in everyone]
    raised = [jnp.where(usable[at], jnp.exp(masked[at] - tops[at]), 0.0) for at in everyone]
    totals = [jnp.sum(raised[at], axis=1, keepdims=True) for at in everyone]
    sums = [
        lax.dot_general(
            raised[at].astype(BF16),
            cache_ref[at, :latent_width, :],
            (((1,), (1,)), ((), ())),
            preferred_element_type=F32,
        )
        for at in everyone
    ]
    for at in everyone:
        latents[at] = sums[at] / jnp.maximum(totals[at], 1e-30)
        stats_ref[at] = jnp.where(lanes == 0, tops[at], totals[at])
    for at in everyone:
        own_ref[at] = latents[at, pl.ds(pl.multiple_of(side * half, half), half), :].astype(BF16)
        other_ref[at] = latents[
            at, pl.ds(pl.multiple_of((1 - side) * half, half), half), :
        ].astype(BF16)


def attend(queries, cache_columns, lengths, side, latent_width):
    requests, heads, width = queries.shape
    slots = cache_columns.shape[2]
    group = 4
    return pl.pallas_call(
        functools.partial(attend_kernel, scale=QKD ** (-0.5)),
        grid_spec=pltpu.PrefetchScalarGridSpec(
            num_scalar_prefetch=2,
            grid=(requests // group,),
            in_specs=[
                pl.BlockSpec((group, heads, width), lambda r, lengths, side: (r, 0, 0)),
                pl.BlockSpec((group, width, slots), lambda r, lengths, side: (r, 0, 0)),
            ],
            out_specs=[
                pl.BlockSpec((group, heads // 2, latent_width), lambda r, lengths, side: (r, 0, 0)),
                pl.BlockSpec((group, heads // 2, latent_width), lambda r, lengths, side: (r, 0, 0)),
                pl.BlockSpec((group, heads, 128), lambda r, lengths, side: (r, 0, 0)),
            ],
            scratch_shapes=[pltpu.VMEM((group, heads, latent_width), F32)],
        ),
        out_shape=[
            jax.ShapeDtypeStruct((requests, heads // 2, latent_width), BF16),
            jax.ShapeDtypeStruct((requests, heads // 2, latent_width), BF16),
            jax.ShapeDtypeStruct((requests, heads, 128), F32),
        ],
        compiler_params=pltpu.CompilerParams(vmem_limit_bytes=48 * 2**20),
        cost_estimate=pl.CostEstimate(
            flops=4 * requests * heads * width * slots,
            bytes_accessed=2 * requests * width * (heads + slots),
            transcendentals=requests * heads * slots,
        ),
    )(lengths, side.reshape(1), queries, cache_columns)


def project_kernel(place_ref, *refs, counts, rows, depths, steps):
    groups = len(counts)
    parts = (refs[:groups], refs[groups : 2 * groups])
    map_ref, own_ref, send_ref, first, second, mapping, total, arrived, map_arrived = refs[2 * groups :]
    blocks = sum(counts)
    copies, map_copies = [], []
    for half, left in enumerate((first, second)):
        at = half * blocks
        for part, count in zip(parts[half], counts):
            for k in range(count):
                row = pl.multiple_of(place_ref[at] * rows, rows)
                copies.append(
                    pltpu.make_async_copy(part.at[k], left.at[pl.ds(row, rows)], arrived.at[at])
                )
                at += 1
    tile = mapping.shape[1] // steps
    for step in range(steps):
        columns = pl.ds(step * tile, tile)
        map_copies.append(
            pltpu.make_async_copy(
                map_ref.at[:, columns], mapping.at[:, columns], map_arrived.at[step]
            )
        )
    in_half = steps // 2
    for half in (0, 1):
        for copy in copies[half * blocks : (half + 1) * blocks]:
            copy.start()
        for copy in map_copies[half * in_half : (half + 1) * in_half]:
            copy.start()
    for step in range(steps):
        if step % in_half == 0:
            half = step // in_half
            for copy in copies[half * blocks : (half + 1) * blocks]:
                copy.wait()
        map_copies[step].wait()
        left = first if step * tile < depths else second
        column = step * tile if step * tile < depths else step * tile - depths
        term = lax.dot_general(
            left[:, column : column + tile],
            mapping[:, step * tile : (step + 1) * tile],
            (((1,), (1,)), ((), ())),
            preferred_element_type=F32,
        )
        if step:
            total[...] += term
        else:
            total[...] = term
    half_rows = total.shape[0] // 2
    side = place_ref[2 * blocks]
    own_ref[...] = total[pl.ds(pl.multiple_of(side * half_rows, half_rows), half_rows), :].T
    send_ref[...] = total[
        pl.ds(pl.multiple_of((1 - side) * half_rows, half_rows), half_rows), :
    ].T.astype(BF16)


def project(first, second, columns_map, place):
    width, depth = columns_map.shape
    rows = first[0].shape[1]
    counts = [part.shape[0] for part in first]
    total_rows = rows * sum(counts)
    steps = 4
    anywhere = pl.BlockSpec(memory_space=pl.ANY)
    whole = pl.BlockSpec(memory_space=pltpu.VMEM)
    return pl.pallas_call(
        functools.partial(
            project_kernel, counts=counts, rows=rows, depths=depth // 2, steps=steps
        ),
        in_specs=[pl.BlockSpec(memory_space=pltpu.SMEM)] + [anywhere] * (2 * len(counts) + 1),
        out_specs=[whole] * 2,
        out_shape=[
            jax.ShapeDtypeStruct((width, total_rows // 2), F32),
            jax.ShapeDtypeStruct((width, total_rows // 2), BF16),
        ],
        scratch_shapes=[
            pltpu.VMEM((total_rows, first[0].shape[2]), BF16),
            pltpu.VMEM((total_rows, second[0].shape[2]), BF16),
            pltpu.VMEM((width, depth), BF16),
            pltpu.VMEM((total_rows, width), F32),
            pltpu.SemaphoreType.DMA((2 * sum(counts),)),
            pltpu.SemaphoreType.DMA((steps,)),
        ],
        compiler_params=pltpu.CompilerParams(vmem_limit_bytes=60 * 2**20),
        cost_estimate=pl.CostEstimate(
            flops=2 * total_rows * depth * width,
            bytes_accessed=2 * (total_rows * depth + depth * width),
            transcendentals=0,
        ),
    )(place, *first, *second, columns_map)


def expert_kernel(place_ref, *refs, blocks, heights, halves, carried, sizes):
    count = len(blocks)
    own, other, refs = refs[:count], refs[count : 2 * count], refs[2 * count :]
    gain_refs, in_ref, refs = refs[:2], refs[2], refs[3:]
    sums_in, refs = refs[: 2 * carried], refs[2 * carried :]
    if sizes:
        gate_ref, down_ref, *refs = refs
        activated, outs, refs = refs[0], refs[1:5], refs[5:]
        total, squares, weights, rows, arrived, part_arrived = refs[:6]
        results, down, down_arrived, sent = refs[6:]
        width = down.shape[1] // 2
        down_copies = []
        for half in (0, 1):
            columns = pl.ds(half * width, width)
            down_copies.append(
                pltpu.make_async_copy(
                    down_ref.at[:, columns], down.at[:, columns], down_arrived.at[half]
                )
            )
    else:
        total, squares, weights, rows, arrived, part_arrived = refs
    lanes = rows.shape[1] // 2
    offsets = [sum(n * h for n, h in zip(blocks[:at], heights[:at])) for at in range(count + 1)]
    spots = []
    for entry in range(count):
        for k in range(blocks[entry]):
            row = offsets[entry] + k * heights[entry]
            spots.append((entry, k, row, heights[entry]))
    part_copies, weight_copies = [], []
    for at, (entry, k, row, height) in enumerate(spots):
        for side, ref in enumerate((own[entry], other[entry])):
            part_copies.append(
                pltpu.make_async_copy(
                    ref.at[k],
                    rows.at[pl.ds(row, height), pl.ds(side * lanes, lanes)],
                    part_arrived.at[2 * at + side],
                )
            )
        source = pl.multiple_of(place_ref[at], 8)
        weight_copies.append(
            pltpu.make_async_copy(
                in_ref.at[pl.ds(source, height)], weights.at[pl.ds(row, height)], arrived.at[at]
            )
        )
    for copy in part_copies + weight_copies:
        copy.start()
    if sizes:
        for copy in down_copies:
            copy.start()
    if sums_in:
        squares[...] = sums_in[1][...]
    else:
        squares[...] = jnp.zeros_like(squares)
    diagonals = {
        height: lax.broadcasted_iota(jnp.int32, (height, height), 0)
        == lax.broadcasted_iota(jnp.int32, (height, height), 1)
        for height in set(heights)
    }
    for at, (entry, k, row, height) in enumerate(spots):
        part_copies[2 * at].wait()
        part_copies[2 * at + 1].wait()
        wide = rows[row : row + height].astype(F32)
        squares[...] += jnp.sum((wide * wide).reshape(height // 8, 8, 2 * lanes), axis=0)
        gain = gain_refs[halves[entry]][pl.ds(place_ref[len(spots) + at], 1), :]
        gain = jnp.where(diagonals[height], gain, 0.0).astype(BF16)
        rows[row : row + height] = jnp.dot(
            gain, rows[row : row + height], preferred_element_type=F32
        ).astype(BF16)
    for entry in range(count):
        for at, spot in enumerate(spots):
            if spot[0] == entry:
                weight_copies[at].wait()
        term = lax.dot_general(
            rows[offsets[entry] : offsets[entry + 1]],
            weights[offsets[entry] : offsets[entry + 1]],
            (((0,), (0,)), ((), ())),
            preferred_element_type=F32,
        )
        if entry:
            total[...] += term
        elif sums_in:
            total[...] = sums_in[0][...] + term
        else:
            total[...] = term
    if not sizes:
        return

    units = total.shape[1] // 2
    mean = jnp.sum(squares[...].T, axis=1, keepdims=True) / in_ref.shape[0]
    level = lax.rsqrt(mean + 1e-06)
    gate_part = total[:, :units] * level
    up_part = total[:, units:] * level
    raised = gate_part / (1.0 + jnp.exp(-gate_part))
    total[:, :units] = raised * up_part * gate_ref[...]
    owner_rows, _ = sizes
    side_rows = total.shape[0] // 2
    order_at = 2 * len(spots)
    for first_row in (0, side_rows):
        for pair in range(side_rows // (2 * owner_rows)):
            pieces = []
            for j in (0, 1):
                row = first_row + place_ref[order_at + 2 * pair + j] * owner_rows
                row = pl.multiple_of(row, owner_rows)
                pieces.append(total[pl.ds(row, owner_rows), :units])
            row = first_row + 2 * pair * owner_rows
            activated[row : row + 2 * owner_rows, :] = jnp.concatenate(pieces).astype(BF16)
    lower(activated, down, results, outs, sent, down_copies, sizes, False)


def lower_kernel(activated_ref, down_ref, *refs, sizes, kept):
    outs, (results, down, arrived, sent) = refs[:4], refs[4:]
    copies = []
    width = down.shape[1] // 2
    for half in (0, 1):
        columns = pl.ds(half * width, width)
        copies.append(
            pltpu.make_async_copy(down_ref.at[:, columns], down.at[:, columns], arrived.at[half])
        )
        copies[-1].start()
    lower(activated_ref, down, results, outs, sent, copies, sizes, kept)


def lower(activated, down, results, outs, sent, arrivals, sizes, kept):
    _, moved = sizes
    width = down.shape[1] // 2
    tile = 512
    side_rows = activated.shape[0] // 2
    plane_rows = side_rows // 4
    copies = []
    for half in (0, 1):
        order = [at for at in range(4) if (at in moved[half]) != kept]
        rows = [
            activated[side * side_rows + at * plane_rows : side * side_rows + (at + 1) * plane_rows, :]
            for side in (1, 0)
            for at in order
        ]
        rows = jnp.concatenate(rows)
        arrivals[half].wait()
        for column in range(0, width, tile):
            results[half, :, column : column + tile] = jnp.dot(
                rows,
                down[:, half * width + column : half * width + column + tile],
                preferred_element_type=F32,
            ).astype(BF16)
        for at, side in enumerate((1, 0)):
            copies.append(
                pltpu.make_async_copy(
                    results.at[half, pl.ds(at * 2 * plane_rows, 2 * plane_rows)],
                    outs[2 * half + side],
                    sent.at[len(copies)],
                )
            )
            copies[-1].start()
    for copy in copies:
        copy.wait()


def lower_kept(activated, down, sizes):
    tokens, units = activated.shape
    anywhere = pl.BlockSpec(memory_space=pl.ANY)
    return pl.pallas_call(
        functools.partial(lower_kernel, sizes=sizes, kept=True),
        in_specs=[pl.BlockSpec(memory_space=pltpu.VMEM), anywhere],
        out_specs=[anywhere] * 4,
        out_shape=[jax.ShapeDtypeStruct((tokens // 4, down.shape[1] // 2), BF16)] * 4,
        scratch_shapes=[
            pltpu.VMEM((2, tokens // 2, down.shape[1] // 2), BF16),
            pltpu.VMEM(down.shape, BF16),
            pltpu.SemaphoreType.DMA((2,)),
            pltpu.SemaphoreType.DMA((4,)),
        ],
        compiler_params=pltpu.CompilerParams(vmem_limit_bytes=LAST_VMEM_LIMIT),
        cost_estimate=pl.CostEstimate(
            flops=tokens * units * down.shape[1],
            bytes_accessed=2 * down.shape[1] * (units + tokens // 2),
            transcendentals=0,
        ),
    )(activated, down)


def expert_rows(parts, other_parts, halves, gains, weights, place, carried, finish):
    model_width, double = weights.shape
    lanes = parts[0].shape[2]
    tokens = 2 * lanes
    blocks = [part.shape[0] for part in parts]
    heights = [part.shape[1] for part in parts]
    depth = sum(n * h for n, h in zip(blocks, heights))
    whole = pl.BlockSpec(memory_space=pltpu.VMEM)
    anywhere = pl.BlockSpec(memory_space=pl.ANY)
    sums = [jax.ShapeDtypeStruct((tokens, double), F32), jax.ShapeDtypeStruct((8, tokens), F32)]
    scratch = [
        pltpu.VMEM((depth, double), BF16),
        pltpu.VMEM((depth, tokens), BF16),
        pltpu.SemaphoreType.DMA((sum(blocks),)),
        pltpu.SemaphoreType.DMA((2 * sum(blocks),)),
    ]
    operands = [place, *parts, *other_parts, *gains, weights, *carried]
    in_specs = [pl.BlockSpec(memory_space=pltpu.SMEM)] + [anywhere] * (2 * len(parts))
    in_specs += [whole] * 2 + [anywhere] + [whole] * len(carried)
    sizes = None
    out_shape, out_specs = sums, [whole] * 2
    if finish is not None:
        gates, down, *sizes = finish
        operands += [gates, down]
        in_specs += [whole, anywhere]
        out_shape = [jax.ShapeDtypeStruct((tokens, double // 2), BF16)]
        out_shape += [jax.ShapeDtypeStruct((tokens // 4, model_width // 2), BF16)] * 4
        out_specs = [whole] + [anywhere] * 4
        scratch = [pltpu.VMEM(a.shape, F32) for a in sums] + scratch
        scratch += [
            pltpu.VMEM((2, tokens // 2, model_width // 2), BF16),
            pltpu.VMEM(down.shape, BF16),
            pltpu.SemaphoreType.DMA((2,)),
            pltpu.SemaphoreType.DMA((4,)),
        ]
    return pl.pallas_call(
        functools.partial(
            expert_kernel,
            blocks=blocks,
            heights=heights,
            halves=halves,
            carried=len(carried) // 2,
            sizes=sizes,
        ),
        in_specs=in_specs,
        out_specs=out_specs,
        out_shape=out_shape,
        scratch_shapes=scratch,
        compiler_params=pltpu.CompilerParams(
            vmem_limit_bytes=VMEM_LIMIT if finish is None else LAST_VMEM_LIMIT
        ),
        cost_estimate=pl.CostEstimate(
            flops=2 * tokens * depth * double,
            bytes_accessed=2 * depth * (double + tokens),
            transcendentals=0,
        ),
    )(*operands)


def on_device(
    queries,
    latent_cache,
    lengths,
    value_lift,
    output_map,
    residual,
    norm_gain,
    expert_ids,
    gate_values,
    expert_in,
    expert_down,
):
    request_count = queries.shape[0]
    latent_width = value_lift.shape[1]
    half_heads = value_lift.shape[0]
    value_width = value_lift.shape[2]
    token_count, model_width = residual.shape
    chips = lax.axis_size("dev")
    plane = 4
    line = chips // plane
    columns = output_map.shape[1]
    experts = chips // 2
    units = expert_down.shape[1]
    side = lax.axis_index("side")
    chip = lax.axis_index("dev")
    line_at, plane_at = chip // plane, chip % plane
    half_tokens = token_count * chips

    def line_hop(value, k):
        return hop(value, "dev", chips, k * plane)

    def plane_hop(value, k):
        return hop(value, "dev", chips, k)

    def swap(value):
        return hop(value, "side", 2, 1)

    def placed(offsets):
        return [(line_at ^ k_line) * plane + (plane_at ^ k_plane) for k_plane, k_line in offsets]

    chosen = expert_ids[:, :, None] == jnp.arange(experts, dtype=jnp.int32)[None, None, :]
    weights = jnp.sum(jnp.where(chosen, gate_values[:, :, None], 0.0), axis=1)
    weights_high = lax.reduce_precision(weights, 8, 7)
    weight_terms = jnp.concatenate([weights_high, weights - weights_high], axis=1).astype(BF16)
    weight_width = -(-token_count * 2 * experts // (request_count * 128)) * 128
    weight_block = jnp.pad(
        weight_terms.reshape(-1), (0, request_count * weight_width - weight_terms.size)
    ).reshape(request_count, weight_width)

    own_latent, sent_latent, stats = attend(
        queries, latent_cache.swapaxes(1, 2), lengths, side, latent_width
    )
    stats = stats[:, :, :2]

    def heads_of(value, which):
        return lax.dynamic_slice_in_dim(value, which * half_heads, half_heads, 1)

    other_latent = swap(sent_latent)
    other_stats = swap(heads_of(stats, 1 - side))
    own_stats = heads_of(stats, side)
    top = jnp.maximum(own_stats[:, :, 0], other_stats[:, :, 0])
    own_share = own_stats[:, :, 1] * jnp.exp(own_stats[:, :, 0] - top)
    other_share = other_stats[:, :, 1] * jnp.exp(other_stats[:, :, 0] - top)
    share_sum = own_share + other_share
    latent_out = (
        own_latent.astype(F32) * (own_share / share_sum)[:, :, None]
        + other_latent.astype(F32) * (other_share / share_sum)[:, :, None]
    ).astype(BF16)
    head_values = jnp.einsum("rhc,hcv->rhv", latent_out, value_lift, preferred_element_type=F32)
    head_values = head_values.astype(BF16).reshape(request_count, half_heads * value_width)

    groups = [list(range(line // 2)), list(range(line // 2, line))]

    half_depth = half_heads * value_width // 2
    first_width = half_depth + weight_width
    sent = jnp.concatenate(
        [head_values[:, :half_depth], weight_block, head_values[:, half_depth:]], axis=1
    )
    sent, residual, expert_in, norm_gain = lax.optimization_barrier(
        (sent, residual, expert_in, norm_gain)
    )

    (first, second), in_rows, residual = gather(
        sent,
        lambda column: (column[:, :, :first_width], column[:, :, first_width:]),
        groups,
        line_hop,
        plane_hop,
        expert_in.reshape(model_width, 2 * units),
        residual,
    )

    residual_blocks = residual.reshape(token_count, chips, columns).swapaxes(0, 1)
    residual_columns = lax.all_to_all(
        residual_blocks, "dev", split_axis=0, concat_axis=0, tiled=True
    )

    place = jnp.stack(
        [
            at
            for half in (first, second)
            for _, offsets in half
            for at in placed(offsets)
        ]
        + [side]
    ).astype(jnp.int32)
    first_parts, second_parts = [[part for part, _ in half] for half in (first, second)]
    own_columns, sent_columns = project(first_parts, second_parts, output_map.T, place)
    sent_columns, residual_columns = lax.optimization_barrier((sent_columns, residual_columns))
    residual_columns = residual_columns.reshape(half_tokens, columns).T
    attention = own_columns + swap(sent_columns).astype(F32)
    hidden = (residual_columns.astype(F32) + attention).astype(BF16)

    gathered = jnp.concatenate([part[:, :, half_depth:] for part, _ in first])
    gathered = gathered.reshape(chips, -1)[:, : token_count * 2 * experts]
    gathered = gathered.reshape(chips, token_count, 2, experts).astype(F32)
    gathered = lax.dynamic_index_in_dim(gathered, chip // 2, 3, keepdims=False).sum(axis=2)
    spots = place[:chips]
    own_gates = jnp.zeros((chips, token_count), F32).at[spots].set(gathered).reshape(-1, 1)
    gates = jnp.concatenate([own_gates, swap(own_gates)])

    first_rows = -(-columns // 32) * 16
    gains = norm_gain.astype(F32).reshape(chips, columns)
    gains = [gains[:, :first_rows], gains[:, first_rows:]]
    hidden_groups = [list(range(line))]
    (first, second), gates, _ = gather(
        hidden,
        lambda column: (column[:, :first_rows], column[:, first_rows:]),
        hidden_groups,
        line_hop,
        plane_hop,
        gates,
        (),
    )
    down = expert_down[0]
    out_at = [(p, k) for p in range(plane) for k in range(line)]
    moved = ((1, 3), (2, 3))
    stages = [[0], [1], [2]]
    carried = ()
    for at, stage in enumerate(stages):
        last = at == len(stages) - 1
        parts, halves, spots = [], [], []
        for which in stage:
            for half, (part, offsets) in enumerate((first[which], second[which])):
                parts.append(part)
                halves.append(half)
                spots += [(spot, half) for spot in placed(offsets)]
        table = [spot * columns + half * first_rows for spot, half in spots]
        table += [spot for spot, _ in spots]
        if last:
            parts, carried = lax.optimization_barrier((parts, carried))
            table += placed((p, k) for p in range(plane) for k in range(line))
        carried = expert_rows(
            parts,
            [swap(part) for part in parts],
            halves,
            gains,
            in_rows,
            jnp.stack(table).astype(jnp.int32),
            carried,
            (gates, down, token_count, moved) if last else None,
        )

    def both_cores(partials):
        other = [swap(partials[2 * h + 1]).astype(F32) for h in (0, 1)]
        return [partials[2 * h].astype(F32) + other[h] for h in (0, 1)]

    activated, *partials = carried
    sent_sum = [part.astype(BF16) for part in both_cores(partials)]
    activated, _ = lax.optimization_barrier((activated, sent_sum))
    kept = both_cores(lower_kept(activated, down, (token_count, moved)))
    half_sums = []
    for h, (one, two) in enumerate(((1, 2), (2, 1))):
        summed = kept[h] + plane_hop(sent_sum[h], one).astype(F32)
        rows = summed.shape[0] // 2
        arrived = plane_hop(summed[rows:].astype(BF16), two).astype(F32)
        half_sums.append(summed[:rows] + arrived)
    plane_sum = jnp.concatenate(half_sums, axis=1).reshape(line, token_count, model_width)
    routed_sum = plane_sum[0]
    for k in range(1, line):
        routed_sum += line_hop(plane_sum[k].astype(BF16), k).astype(F32)

    tokens = chip * token_count + jnp.arange(token_count, dtype=jnp.int32)
    picked = (tokens[:, None] == jnp.arange(half_tokens, dtype=jnp.int32)[None, :]).astype(BF16)
    own_parts, _ = lax.optimization_barrier(([part for half in (first, second) for part, _ in half], sent_sum))
    own_rows = []
    for half, parts in ((first, own_parts[: len(first)]), (second, own_parts[len(first) :])):
        blocks = jnp.concatenate(
            [jnp.einsum("qt,krt->kqr", picked, part, preferred_element_type=F32) for part in parts]
        )
        offsets = [at for _, part_offsets in half for at in part_offsets]
        spots = jnp.stack(placed(offsets))
        own_rows.append(jnp.zeros_like(blocks).at[spots].set(blocks))
    own_hidden = jnp.concatenate(own_rows, axis=2).swapaxes(0, 1).reshape(token_count, model_width)
    return (own_hidden + routed_sum).astype(BF16)


def solution(mesh):
    in_specs = (
        P("dev", None, None),
        P("dev", "side", None),
        P("dev"),
        P("side", None, None),
        P("side", "dev"),
        P(("side", "dev"), None),
        P(),
        P(("side", "dev"), None),
        P(("side", "dev"), None),
        P("dev", None, None, "side"),
        P("dev", "side", None),
    )
    out_specs = P(("side", "dev"), None)
    return jax.shard_map(
        on_device, mesh=mesh, in_specs=in_specs, out_specs=out_specs, check_vma=False
    )
```

```python
import functools

import jax
import jax.numpy as jnp
from jax import lax
from jax.experimental import pallas as pl
from jax.experimental.pallas import tpu as pltpu
from jax.sharding import PartitionSpec as P

QKD = 192
F32 = jnp.float32
BF16 = jnp.bfloat16
VMEM_LIMIT = 48 * 2**20
LAST_VMEM_LIMIT = 52 * 2**20


def hop(value, axis, size, mask):
    return lax.ppermute(value, axis, [(i, i ^ mask) for i in range(size)])


def gather(block, split, groups, line_hop, plane_hop, beside, after):
    arrived = {0: block}
    for group in groups:
        for k in group:
            if k:
                arrived[k] = line_hop(block, k)
    halves = ([], [])
    for at, group in enumerate(groups):
        if at == 0 and len(group) > 1:
            block, arrived[group[1]] = lax.optimization_barrier((block, arrived[group[1]]))
            arrived[0] = block
        column = jnp.stack([arrived[k] for k in group])
        if at == len(groups) - 1:
            column, beside = lax.optimization_barrier((column, beside))
        split_column = split(column)
        nears = [plane_hop(half, one) for half, one in zip(split_column, (1, 2))]
        if at == len(groups) - 1:
            nears, after = lax.optimization_barrier((nears, after))
        for parts, half, near, (one, two) in zip(halves, split_column, nears, ((1, 2), (2, 1))):
            rest = plane_hop(jnp.concatenate([half, near]), two)
            parts.append((half, [(0, k) for k in group]))
            parts.append((near, [(one, k) for k in group]))
            parts.append((rest, [(p, k) for p in (two, 3) for k in group]))
    return halves, beside, after


def attend_kernel(
    length_ref, side_ref, query_ref, cache_ref, own_ref, other_ref, stats_ref, latents, *, scale
):
    group, heads, _ = query_ref.shape
    latent_width = own_ref.shape[2]
    slots = cache_ref.shape[2]
    half = heads // 2
    first = pl.program_id(0) * group
    side = side_ref[0]
    positions = side * slots + lax.broadcasted_iota(jnp.int32, (heads, slots), 1)
    lanes = lax.broadcasted_iota(jnp.int32, (heads, stats_ref.shape[2]), 1)
    everyone = range(group)
    usable = [positions < length_ref[first + at] for at in everyone]
    scores = [
        jnp.dot(query_ref[at], cache_ref[at], preferred_element_type=F32) * scale for at in everyone
    ]
    masked = [jnp.where(usable[at], scores[at], -1e30) for at in everyone]
    tops = [jnp.max(masked[at], axis=1, keepdims=True) for at in everyone]
    raised = [jnp.where(usable[at], jnp.exp(masked[at] - tops[at]), 0.0) for at in everyone]
    totals = [jnp.sum(raised[at], axis=1, keepdims=True) for at in everyone]
    sums = [
        lax.dot_general(
            raised[at].astype(BF16),
            cache_ref[at, :latent_width, :],
            (((1,), (1,)), ((), ())),
            preferred_element_type=F32,
        )
        for at in everyone
    ]
    for at in everyone:
        latents[at] = sums[at] / jnp.maximum(totals[at], 1e-30)
        stats_ref[at] = jnp.where(lanes == 0, tops[at], totals[at])
    for at in everyone:
        own_ref[at] = latents[at, pl.ds(pl.multiple_of(side * half, half), half), :].astype(BF16)
        other_ref[at] = latents[
            at, pl.ds(pl.multiple_of((1 - side) * half, half), half), :
        ].astype(BF16)


def attend(queries, cache_columns, lengths, side, latent_width):
    requests, heads, width = queries.shape
    slots = cache_columns.shape[2]
    group = 8
    return pl.pallas_call(
        functools.partial(attend_kernel, scale=QKD ** (-0.5)),
        grid_spec=pltpu.PrefetchScalarGridSpec(
            num_scalar_prefetch=2,
            grid=(requests // group,),
            in_specs=[
                pl.BlockSpec((group, heads, width), lambda r, lengths, side: (r, 0, 0)),
                pl.BlockSpec((group, width, slots), lambda r, lengths, side: (r, 0, 0)),
            ],
            out_specs=[
                pl.BlockSpec((group, heads // 2, latent_width), lambda r, lengths, side: (r, 0, 0)),
                pl.BlockSpec((group, heads // 2, latent_width), lambda r, lengths, side: (r, 0, 0)),
                pl.BlockSpec((group, heads, 128), lambda r, lengths, side: (r, 0, 0)),
            ],
            scratch_shapes=[pltpu.VMEM((group, heads, latent_width), F32)],
        ),
        out_shape=[
            jax.ShapeDtypeStruct((requests, heads // 2, latent_width), BF16),
            jax.ShapeDtypeStruct((requests, heads // 2, latent_width), BF16),
            jax.ShapeDtypeStruct((requests, heads, 128), F32),
        ],
        compiler_params=pltpu.CompilerParams(vmem_limit_bytes=48 * 2**20),
        cost_estimate=pl.CostEstimate(
            flops=4 * requests * heads * width * slots,
            bytes_accessed=2 * requests * width * (heads + slots),
            transcendentals=requests * heads * slots,
        ),
    )(lengths, side.reshape(1), queries, cache_columns)


def project_kernel(place_ref, *refs, counts, rows, depths, steps):
    groups = len(counts)
    parts = (refs[:groups], refs[groups : 2 * groups])
    map_ref, own_ref, send_ref, first, second, mapping, total, arrived, map_arrived = refs[2 * groups :]
    blocks = sum(counts)
    copies, map_copies = [], []
    for half, left in enumerate((first, second)):
        at = half * blocks
        for part, count in zip(parts[half], counts):
            for k in range(count):
                row = pl.multiple_of(place_ref[at] * rows, rows)
                copies.append(
                    pltpu.make_async_copy(part.at[k], left.at[pl.ds(row, rows)], arrived.at[at])
                )
                at += 1
    tile = mapping.shape[1] // steps
    for step in range(steps):
        columns = pl.ds(step * tile, tile)
        map_copies.append(
            pltpu.make_async_copy(
                map_ref.at[:, columns], mapping.at[:, columns], map_arrived.at[step]
            )
        )
    in_half = steps // 2
    for half in (0, 1):
        for copy in copies[half * blocks : (half + 1) * blocks]:
            copy.start()
        for copy in map_copies[half * in_half : (half + 1) * in_half]:
            copy.start()
    for step in range(steps):
        if step % in_half == 0:
            half = step // in_half
            for copy in copies[half * blocks : (half + 1) * blocks]:
                copy.wait()
        map_copies[step].wait()
        left = first if step * tile < depths else second
        column = step * tile if step * tile < depths else step * tile - depths
        term = lax.dot_general(
            left[:, column : column + tile],
            mapping[:, step * tile : (step + 1) * tile],
            (((1,), (1,)), ((), ())),
            preferred_element_type=F32,
        )
        if step:
            total[...] += term
        else:
            total[...] = term
    half_rows = total.shape[0] // 2
    side = place_ref[2 * blocks]
    own_ref[...] = total[pl.ds(pl.multiple_of(side * half_rows, half_rows), half_rows), :].T
    send_ref[...] = total[
        pl.ds(pl.multiple_of((1 - side) * half_rows, half_rows), half_rows), :
    ].T.astype(BF16)


def project(first, second, columns_map, place):
    width, depth = columns_map.shape
    rows = first[0].shape[1]
    counts = [part.shape[0] for part in first]
    total_rows = rows * sum(counts)
    steps = 4
    anywhere = pl.BlockSpec(memory_space=pl.ANY)
    whole = pl.BlockSpec(memory_space=pltpu.VMEM)
    return pl.pallas_call(
        functools.partial(
            project_kernel, counts=counts, rows=rows, depths=depth // 2, steps=steps
        ),
        in_specs=[pl.BlockSpec(memory_space=pltpu.SMEM)] + [anywhere] * (2 * len(counts) + 1),
        out_specs=[whole] * 2,
        out_shape=[
            jax.ShapeDtypeStruct((width, total_rows // 2), F32),
            jax.ShapeDtypeStruct((width, total_rows // 2), BF16),
        ],
        scratch_shapes=[
            pltpu.VMEM((total_rows, first[0].shape[2]), BF16),
            pltpu.VMEM((total_rows, second[0].shape[2]), BF16),
            pltpu.VMEM((width, depth), BF16),
            pltpu.VMEM((total_rows, width), F32),
            pltpu.SemaphoreType.DMA((2 * sum(counts),)),
            pltpu.SemaphoreType.DMA((steps,)),
        ],
        compiler_params=pltpu.CompilerParams(vmem_limit_bytes=60 * 2**20),
        cost_estimate=pl.CostEstimate(
            flops=2 * total_rows * depth * width,
            bytes_accessed=2 * (total_rows * depth + depth * width),
            transcendentals=0,
        ),
    )(place, *first, *second, columns_map)


def expert_kernel(place_ref, *refs, blocks, heights, halves, carried, sizes):
    count = len(blocks)
    own, other, refs = refs[:count], refs[count : 2 * count], refs[2 * count :]
    gain_refs, in_ref, refs = refs[:2], refs[2], refs[3:]
    sums_in, refs = refs[: 2 * carried], refs[2 * carried :]
    if sizes:
        gate_ref, down_ref, *refs = refs
        activated, outs, refs = refs[0], refs[1:5], refs[5:]
        total, squares, weights, rows, arrived, part_arrived = refs[:6]
        results, down, down_arrived, sent = refs[6:]
        width = down.shape[1] // 2
        down_copies = []
        for half in (0, 1):
            columns = pl.ds(half * width, width)
            down_copies.append(
                pltpu.make_async_copy(
                    down_ref.at[:, columns], down.at[:, columns], down_arrived.at[half]
                )
            )
    else:
        total, squares, weights, rows, arrived, part_arrived = refs
    lanes = rows.shape[1] // 2
    offsets = [sum(n * h for n, h in zip(blocks[:at], heights[:at])) for at in range(count + 1)]
    spots = []
    for entry in range(count):
        for k in range(blocks[entry]):
            row = offsets[entry] + k * heights[entry]
            spots.append((entry, k, row, heights[entry]))
    part_copies, weight_copies = [], []
    for at, (entry, k, row, height) in enumerate(spots):
        for side, ref in enumerate((own[entry], other[entry])):
            part_copies.append(
                pltpu.make_async_copy(
                    ref.at[k],
                    rows.at[pl.ds(row, height), pl.ds(side * lanes, lanes)],
                    part_arrived.at[2 * at + side],
                )
            )
        source = pl.multiple_of(place_ref[at], 8)
        weight_copies.append(
            pltpu.make_async_copy(
                in_ref.at[pl.ds(source, height)], weights.at[pl.ds(row, height)], arrived.at[at]
            )
        )
    for copy in part_copies + weight_copies:
        copy.start()
    if sizes:
        for copy in down_copies:
            copy.start()
    if sums_in:
        squares[...] = sums_in[1][...]
    else:
        squares[...] = jnp.zeros_like(squares)
    for at, (entry, k, row, height) in enumerate(spots):
        part_copies[2 * at].wait()
        part_copies[2 * at + 1].wait()
        wide = rows[row : row + height].astype(F32)
        squares[...] += jnp.sum((wide * wide).reshape(height // 8, 8, 2 * lanes), axis=0)
        lane = lax.broadcasted_iota(jnp.int32, gain_refs[halves[entry]].shape, 1)
        gain = jnp.where(lane == place_ref[len(spots) + at], gain_refs[halves[entry]][...], 0.0)
        gain = jnp.sum(gain, axis=1, keepdims=True)
        rows[row : row + height] = (wide * gain).astype(BF16)
    for entry in range(count):
        for at, spot in enumerate(spots):
            if spot[0] == entry:
                weight_copies[at].wait()
        term = lax.dot_general(
            rows[offsets[entry] : offsets[entry + 1]],
            weights[offsets[entry] : offsets[entry + 1]],
            (((0,), (0,)), ((), ())),
            preferred_element_type=F32,
        )
        if entry:
            total[...] += term
        elif sums_in:
            total[...] = sums_in[0][...] + term
        else:
            total[...] = term
    if not sizes:
        return

    units = total.shape[1] // 2
    mean = jnp.sum(squares[...].T, axis=1, keepdims=True) / in_ref.shape[0]
    level = lax.rsqrt(mean + 1e-06)
    gate_part = total[:, :units] * level
    up_part = total[:, units:] * level
    raised = gate_part / (1.0 + jnp.exp(-gate_part))
    total[:, :units] = raised * up_part * gate_ref[...]
    owner_rows, _ = sizes
    side_rows = total.shape[0] // 2
    order_at = 2 * len(spots)
    for first_row in (0, side_rows):
        for pair in range(side_rows // (2 * owner_rows)):
            pieces = []
            for j in (0, 1):
                row = first_row + place_ref[order_at + 2 * pair + j] * owner_rows
                row = pl.multiple_of(row, owner_rows)
                pieces.append(total[pl.ds(row, owner_rows), :units])
            row = first_row + 2 * pair * owner_rows
            activated[row : row + 2 * owner_rows, :] = jnp.concatenate(pieces).astype(BF16)
    lower(activated, down, results, outs, sent, down_copies, sizes, False)


def lower_kernel(activated_ref, down_ref, *refs, sizes, kept):
    outs, (results, down, arrived, sent) = refs[:4], refs[4:]
    copies = []
    width = down.shape[1] // 2
    for half in (0, 1):
        columns = pl.ds(half * width, width)
        copies.append(
            pltpu.make_async_copy(down_ref.at[:, columns], down.at[:, columns], arrived.at[half])
        )
        copies[-1].start()
    lower(activated_ref, down, results, outs, sent, copies, sizes, kept)


def lower(activated, down, results, outs, sent, arrivals, sizes, kept):
    _, moved = sizes
    width = down.shape[1] // 2
    tile = 512
    side_rows = activated.shape[0] // 2
    plane_rows = side_rows // 4
    copies = []
    for half in (0, 1):
        order = [at for at in range(4) if (at in moved[half]) != kept]
        rows = [
            activated[side * side_rows + at * plane_rows : side * side_rows + (at + 1) * plane_rows, :]
            for side in (1, 0)
            for at in order
        ]
        rows = jnp.concatenate(rows)
        arrivals[half].wait()
        for column in range(0, width, tile):
            results[half, :, column : column + tile] = jnp.dot(
                rows,
                down[:, half * width + column : half * width + column + tile],
                preferred_element_type=F32,
            ).astype(BF16)
        for at, side in enumerate((1, 0)):
            copies.append(
                pltpu.make_async_copy(
                    results.at[half, pl.ds(at * 2 * plane_rows, 2 * plane_rows)],
                    outs[2 * half + side],
                    sent.at[len(copies)],
                )
            )
            copies[-1].start()
    for copy in copies:
        copy.wait()


def lower_kept(activated, down, sizes):
    tokens, units = activated.shape
    anywhere = pl.BlockSpec(memory_space=pl.ANY)
    return pl.pallas_call(
        functools.partial(lower_kernel, sizes=sizes, kept=True),
        in_specs=[pl.BlockSpec(memory_space=pltpu.VMEM), anywhere],
        out_specs=[anywhere] * 4,
        out_shape=[jax.ShapeDtypeStruct((tokens // 4, down.shape[1] // 2), BF16)] * 4,
        scratch_shapes=[
            pltpu.VMEM((2, tokens // 2, down.shape[1] // 2), BF16),
            pltpu.VMEM(down.shape, BF16),
            pltpu.SemaphoreType.DMA((2,)),
            pltpu.SemaphoreType.DMA((4,)),
        ],
        compiler_params=pltpu.CompilerParams(vmem_limit_bytes=LAST_VMEM_LIMIT),
        cost_estimate=pl.CostEstimate(
            flops=tokens * units * down.shape[1],
            bytes_accessed=2 * down.shape[1] * (units + tokens // 2),
            transcendentals=0,
        ),
    )(activated, down)


def expert_rows(parts, other_parts, halves, gains, weights, place, carried, finish):
    model_width, double = weights.shape
    lanes = parts[0].shape[2]
    tokens = 2 * lanes
    blocks = [part.shape[0] for part in parts]
    heights = [part.shape[1] for part in parts]
    depth = sum(n * h for n, h in zip(blocks, heights))
    whole = pl.BlockSpec(memory_space=pltpu.VMEM)
    anywhere = pl.BlockSpec(memory_space=pl.ANY)
    sums = [jax.ShapeDtypeStruct((tokens, double), F32), jax.ShapeDtypeStruct((8, tokens), F32)]
    scratch = [
        pltpu.VMEM((depth, double), BF16),
        pltpu.VMEM((depth, tokens), BF16),
        pltpu.SemaphoreType.DMA((sum(blocks),)),
        pltpu.SemaphoreType.DMA((2 * sum(blocks),)),
    ]
    operands = [place, *parts, *other_parts, *gains, weights, *carried]
    in_specs = [pl.BlockSpec(memory_space=pltpu.SMEM)] + [anywhere] * (2 * len(parts))
    in_specs += [whole] * 2 + [anywhere] + [whole] * len(carried)
    sizes = None
    out_shape, out_specs = sums, [whole] * 2
    if finish is not None:
        gates, down, *sizes = finish
        operands += [gates, down]
        in_specs += [whole, anywhere]
        out_shape = [jax.ShapeDtypeStruct((tokens, double // 2), BF16)]
        out_shape += [jax.ShapeDtypeStruct((tokens // 4, model_width // 2), BF16)] * 4
        out_specs = [whole] + [anywhere] * 4
        scratch = [pltpu.VMEM(a.shape, F32) for a in sums] + scratch
        scratch += [
            pltpu.VMEM((2, tokens // 2, model_width // 2), BF16),
            pltpu.VMEM(down.shape, BF16),
            pltpu.SemaphoreType.DMA((2,)),
            pltpu.SemaphoreType.DMA((4,)),
        ]
    return pl.pallas_call(
        functools.partial(
            expert_kernel,
            blocks=blocks,
            heights=heights,
            halves=halves,
            carried=len(carried) // 2,
            sizes=sizes,
        ),
        in_specs=in_specs,
        out_specs=out_specs,
        out_shape=out_shape,
        scratch_shapes=scratch,
        compiler_params=pltpu.CompilerParams(
            vmem_limit_bytes=VMEM_LIMIT if finish is None else LAST_VMEM_LIMIT
        ),
        cost_estimate=pl.CostEstimate(
            flops=2 * tokens * depth * double,
            bytes_accessed=2 * depth * (double + tokens),
            transcendentals=0,
        ),
    )(*operands)


def on_device(
    queries,
    latent_cache,
    lengths,
    value_lift,
    output_map,
    residual,
    norm_gain,
    expert_ids,
    gate_values,
    expert_in,
    expert_down,
):
    request_count = queries.shape[0]
    latent_width = value_lift.shape[1]
    half_heads = value_lift.shape[0]
    value_width = value_lift.shape[2]
    token_count, model_width = residual.shape
    chips = lax.axis_size("dev")
    plane = 4
    line = chips // plane
    columns = output_map.shape[1]
    experts = chips // 2
    units = expert_down.shape[1]
    side = lax.axis_index("side")
    chip = lax.axis_index("dev")
    line_at, plane_at = chip // plane, chip % plane
    half_tokens = token_count * chips

    def line_hop(value, k):
        return hop(value, "dev", chips, k * plane)

    def plane_hop(value, k):
        return hop(value, "dev", chips, k)

    def swap(value):
        return hop(value, "side", 2, 1)

    def placed(offsets):
        return [(line_at ^ k_line) * plane + (plane_at ^ k_plane) for k_plane, k_line in offsets]

    chosen = expert_ids[:, :, None] == jnp.arange(experts, dtype=jnp.int32)[None, None, :]
    weights = jnp.sum(jnp.where(chosen, gate_values[:, :, None], 0.0), axis=1)
    weights_high = lax.reduce_precision(weights, 8, 7)
    weight_terms = jnp.concatenate([weights_high, weights - weights_high], axis=1).astype(BF16)
    weight_width = -(-token_count * 2 * experts // (request_count * 128)) * 128
    weight_block = jnp.pad(
        weight_terms.reshape(-1), (0, request_count * weight_width - weight_terms.size)
    ).reshape(request_count, weight_width)

    own_latent, sent_latent, stats = attend(
        queries, latent_cache.swapaxes(1, 2), lengths, side, latent_width
    )
    stats = stats[:, :, :2]

    def heads_of(value, which):
        return lax.dynamic_slice_in_dim(value, which * half_heads, half_heads, 1)

    other_latent = swap(sent_latent)
    other_stats = swap(heads_of(stats, 1 - side))
    own_stats = heads_of(stats, side)
    top = jnp.maximum(own_stats[:, :, 0], other_stats[:, :, 0])
    own_share = own_stats[:, :, 1] * jnp.exp(own_stats[:, :, 0] - top)
    other_share = other_stats[:, :, 1] * jnp.exp(other_stats[:, :, 0] - top)
    share_sum = own_share + other_share
    latent_out = (
        own_latent.astype(F32) * (own_share / share_sum)[:, :, None]
        + other_latent.astype(F32) * (other_share / share_sum)[:, :, None]
    ).astype(BF16)
    head_values = jnp.einsum("rhc,hcv->rhv", latent_out, value_lift, preferred_element_type=F32)
    head_values = head_values.astype(BF16).reshape(request_count, half_heads * value_width)

    groups = [list(range(line // 2)), list(range(line // 2, line))]

    half_depth = half_heads * value_width // 2
    first_width = half_depth + weight_width
    sent = jnp.concatenate(
        [head_values[:, :half_depth], weight_block, head_values[:, half_depth:]], axis=1
    )
    sent, residual, expert_in, norm_gain = lax.optimization_barrier(
        (sent, residual, expert_in, norm_gain)
    )

    (first, second), in_rows, residual = gather(
        sent,
        lambda column: (column[:, :, :first_width], column[:, :, first_width:]),
        groups,
        line_hop,
        plane_hop,
        expert_in.reshape(model_width, 2 * units),
        residual,
    )

    residual_blocks = residual.reshape(token_count, chips, columns).swapaxes(0, 1)
    residual_columns = lax.all_to_all(
        residual_blocks, "dev", split_axis=0, concat_axis=0, tiled=True
    )

    place = jnp.stack(
        [
            at
            for half in (first, second)
            for _, offsets in half
            for at in placed(offsets)
        ]
        + [side]
    ).astype(jnp.int32)
    first_parts, second_parts = [[part for part, _ in half] for half in (first, second)]
    own_columns, sent_columns = project(first_parts, second_parts, output_map.T, place)
    sent_columns, residual_columns = lax.optimization_barrier((sent_columns, residual_columns))
    residual_columns = residual_columns.reshape(half_tokens, columns).T
    attention = own_columns + swap(sent_columns).astype(F32)
    hidden = (residual_columns.astype(F32) + attention).astype(BF16)

    gathered = jnp.concatenate([part[:, :, half_depth:] for part, _ in first])
    gathered = gathered.reshape(chips, -1)[:, : token_count * 2 * experts]
    gathered = gathered.reshape(chips, token_count, 2, experts).astype(F32)
    gathered = lax.dynamic_index_in_dim(gathered, chip // 2, 3, keepdims=False).sum(axis=2)
    spots = place[:chips]
    own_gates = jnp.zeros((chips, token_count), F32).at[spots].set(gathered).reshape(-1, 1)
    gates = jnp.concatenate([own_gates, swap(own_gates)])

    first_rows = -(-columns // 32) * 16
    gains = norm_gain.astype(F32).reshape(chips, columns).T
    gains = [gains[:first_rows], gains[first_rows:]]
    hidden_groups = [list(range(line))]
    (first, second), gates, _ = gather(
        hidden,
        lambda column: (column[:, :first_rows], column[:, first_rows:]),
        hidden_groups,
        line_hop,
        plane_hop,
        gates,
        (),
    )
    down = expert_down[0]
    out_at = [(p, k) for p in range(plane) for k in range(line)]
    moved = ((1, 3), (2, 3))
    stages = [[0], [1], [2]]
    carried = ()
    for at, stage in enumerate(stages):
        last = at == len(stages) - 1
        parts, halves, spots = [], [], []
        for which in stage:
            for half, (part, offsets) in enumerate((first[which], second[which])):
                parts.append(part)
                halves.append(half)
                spots += [(spot, half) for spot in placed(offsets)]
        table = [spot * columns + half * first_rows for spot, half in spots]
        table += [spot for spot, _ in spots]
        if last:
            parts, carried = lax.optimization_barrier((parts, carried))
            table += placed((p, k) for p in range(plane) for k in range(line))
        carried = expert_rows(
            parts,
            [swap(part) for part in parts],
            halves,
            gains,
            in_rows,
            jnp.stack(table).astype(jnp.int32),
            carried,
            (gates, down, token_count, moved) if last else None,
        )

    def both_cores(partials):
        other = [swap(partials[2 * h + 1]).astype(F32) for h in (0, 1)]
        return [partials[2 * h].astype(F32) + other[h] for h in (0, 1)]

    activated, *partials = carried
    sent_sum = [part.astype(BF16) for part in both_cores(partials)]
    activated, _ = lax.optimization_barrier((activated, sent_sum))
    kept = both_cores(lower_kept(activated, down, (token_count, moved)))
    half_sums = []
    for h, (one, two) in enumerate(((1, 2), (2, 1))):
        summed = kept[h] + plane_hop(sent_sum[h], one).astype(F32)
        rows = summed.shape[0] // 2
        arrived = plane_hop(summed[rows:].astype(BF16), two).astype(F32)
        half_sums.append(summed[:rows] + arrived)
    plane_sum = jnp.concatenate(half_sums, axis=1).reshape(line, token_count, model_width)
    routed_sum = plane_sum[0]
    for k in range(1, line):
        routed_sum += line_hop(plane_sum[k].astype(BF16), k).astype(F32)

    tokens = chip * token_count + jnp.arange(token_count, dtype=jnp.int32)
    picked = (tokens[:, None] == jnp.arange(half_tokens, dtype=jnp.int32)[None, :]).astype(BF16)
    own_parts, _ = lax.optimization_barrier(([part for half in (first, second) for part, _ in half], sent_sum))
    own_rows = []
    for half, parts in ((first, own_parts[: len(first)]), (second, own_parts[len(first) :])):
        blocks = jnp.concatenate(
            [jnp.einsum("qt,krt->kqr", picked, part, preferred_element_type=F32) for part in parts]
        )
        offsets = [at for _, part_offsets in half for at in part_offsets]
        spots = jnp.stack(placed(offsets))
        own_rows.append(jnp.zeros_like(blocks).at[spots].set(blocks))
    own_hidden = jnp.concatenate(own_rows, axis=2).swapaxes(0, 1).reshape(token_count, model_width)
    return (own_hidden + routed_sum).astype(BF16)


def solution(mesh):
    in_specs = (
        P("dev", None, None),
        P("dev", "side", None),
        P("dev"),
        P("side", None, None),
        P("side", "dev"),
        P(("side", "dev"), None),
        P(),
        P(("side", "dev"), None),
        P(("side", "dev"), None),
        P("dev", None, None, "side"),
        P("dev", "side", None),
    )
    out_specs = P(("side", "dev"), None)
    return jax.shard_map(
        on_device, mesh=mesh, in_specs=in_specs, out_specs=out_specs, check_vma=False
    )
```

```python
import functools

import jax
import jax.numpy as jnp
from jax import lax
from jax.experimental import pallas as pl
from jax.experimental.pallas import tpu as pltpu
from jax.sharding import PartitionSpec as P

QKD = 192
F32 = jnp.float32
BF16 = jnp.bfloat16
VMEM_LIMIT = 48 * 2**20
LAST_VMEM_LIMIT = 51 * 2**20


def hop(value, axis, size, mask):
    return lax.ppermute(value, axis, [(i, i ^ mask) for i in range(size)])


def gather(block, split, groups, line_hop, plane_hop, beside, after):
    arrived = {0: block}
    for group in groups:
        for k in group:
            if k:
                arrived[k] = line_hop(block, k)
    halves = ([], [])
    for at, group in enumerate(groups):
        if at == 0 and len(group) > 1:
            block, arrived[group[1]] = lax.optimization_barrier((block, arrived[group[1]]))
            arrived[0] = block
        column = jnp.stack([arrived[k] for k in group])
        if at == len(groups) - 1:
            column, beside = lax.optimization_barrier((column, beside))
        split_column = split(column)
        nears = [plane_hop(half, one) for half, one in zip(split_column, (1, 2))]
        if at == len(groups) - 1:
            nears, after = lax.optimization_barrier((nears, after))
        for parts, half, near, (one, two) in zip(halves, split_column, nears, ((1, 2), (2, 1))):
            rest = plane_hop(jnp.concatenate([half, near]), two)
            parts.append((half, [(0, k) for k in group]))
            parts.append((near, [(one, k) for k in group]))
            parts.append((rest, [(p, k) for p in (two, 3) for k in group]))
    return halves, beside, after


def attend_kernel(
    length_ref, side_ref, query_ref, cache_ref, own_ref, other_ref, stats_ref, latents, *, scale
):
    group, heads, _ = query_ref.shape
    latent_width = own_ref.shape[2]
    slots = cache_ref.shape[2]
    half = heads // 2
    first = pl.program_id(0) * group
    side = side_ref[0]
    positions = side * slots + lax.broadcasted_iota(jnp.int32, (heads, slots), 1)
    lanes = lax.broadcasted_iota(jnp.int32, (heads, stats_ref.shape[2]), 1)
    everyone = range(group)
    usable = [positions < length_ref[first + at] for at in everyone]
    scores = [
        jnp.dot(query_ref[at], cache_ref[at], preferred_element_type=F32) * scale for at in everyone
    ]
    masked = [jnp.where(usable[at], scores[at], -1e30) for at in everyone]
    tops = [jnp.max(masked[at], axis=1, keepdims=True) for at in everyone]
    raised = [jnp.where(usable[at], jnp.exp(masked[at] - tops[at]), 0.0) for at in everyone]
    totals = [jnp.sum(raised[at], axis=1, keepdims=True) for at in everyone]
    sums = [
        lax.dot_general(
            raised[at].astype(BF16),
            cache_ref[at, :latent_width, :],
            (((1,), (1,)), ((), ())),
            preferred_element_type=F32,
        )
        for at in everyone
    ]
    for at in everyone:
        latents[at] = sums[at] / jnp.maximum(totals[at], 1e-30)
        stats_ref[at] = jnp.where(lanes == 0, tops[at], totals[at])
    for at in everyone:
        own_ref[at] = latents[at, pl.ds(pl.multiple_of(side * half, half), half), :].astype(BF16)
        other_ref[at] = latents[
            at, pl.ds(pl.multiple_of((1 - side) * half, half), half), :
        ].astype(BF16)


def attend(queries, cache_columns, lengths, side, latent_width):
    requests, heads, width = queries.shape
    slots = cache_columns.shape[2]
    group = 8
    return pl.pallas_call(
        functools.partial(attend_kernel, scale=QKD ** (-0.5)),
        grid_spec=pltpu.PrefetchScalarGridSpec(
            num_scalar_prefetch=2,
            grid=(requests // group,),
            in_specs=[
                pl.BlockSpec((group, heads, width), lambda r, lengths, side: (r, 0, 0)),
                pl.BlockSpec((group, width, slots), lambda r, lengths, side: (r, 0, 0)),
            ],
            out_specs=[
                pl.BlockSpec((group, heads // 2, latent_width), lambda r, lengths, side: (r, 0, 0)),
                pl.BlockSpec((group, heads // 2, latent_width), lambda r, lengths, side: (r, 0, 0)),
                pl.BlockSpec((group, heads, 128), lambda r, lengths, side: (r, 0, 0)),
            ],
            scratch_shapes=[pltpu.VMEM((group, heads, latent_width), F32)],
        ),
        out_shape=[
            jax.ShapeDtypeStruct((requests, heads // 2, latent_width), BF16),
            jax.ShapeDtypeStruct((requests, heads // 2, latent_width), BF16),
            jax.ShapeDtypeStruct((requests, heads, 128), F32),
        ],
        compiler_params=pltpu.CompilerParams(vmem_limit_bytes=48 * 2**20),
        cost_estimate=pl.CostEstimate(
            flops=4 * requests * heads * width * slots,
            bytes_accessed=2 * requests * width * (heads + slots),
            transcendentals=requests * heads * slots,
        ),
    )(lengths, side.reshape(1), queries, cache_columns)


def project_kernel(place_ref, *refs, counts, rows, depths, steps):
    groups = len(counts)
    parts = (refs[:groups], refs[groups : 2 * groups])
    map_ref, own_ref, send_ref, first, second, mapping, total, arrived, map_arrived = refs[2 * groups :]
    blocks = sum(counts)
    copies, map_copies = [], []
    for half, left in enumerate((first, second)):
        at = half * blocks
        for part, count in zip(parts[half], counts):
            for k in range(count):
                row = pl.multiple_of(place_ref[at] * rows, rows)
                copies.append(
                    pltpu.make_async_copy(part.at[k], left.at[pl.ds(row, rows)], arrived.at[at])
                )
                at += 1
    tile = mapping.shape[1] // steps
    for step in range(steps):
        columns = pl.ds(step * tile, tile)
        map_copies.append(
            pltpu.make_async_copy(
                map_ref.at[:, columns], mapping.at[:, columns], map_arrived.at[step]
            )
        )
    in_half = steps // 2
    for half in (0, 1):
        for copy in copies[half * blocks : (half + 1) * blocks]:
            copy.start()
        for copy in map_copies[half * in_half : (half + 1) * in_half]:
            copy.start()
    for step in range(steps):
        if step % in_half == 0:
            half = step // in_half
            for copy in copies[half * blocks : (half + 1) * blocks]:
                copy.wait()
        map_copies[step].wait()
        left = first if step * tile < depths else second
        column = step * tile if step * tile < depths else step * tile - depths
        term = lax.dot_general(
            left[:, column : column + tile],
            mapping[:, step * tile : (step + 1) * tile],
            (((1,), (1,)), ((), ())),
            preferred_element_type=F32,
        )
        if step:
            total[...] += term
        else:
            total[...] = term
    half_rows = total.shape[0] // 2
    side = place_ref[2 * blocks]
    own_ref[...] = total[pl.ds(pl.multiple_of(side * half_rows, half_rows), half_rows), :].T
    send_ref[...] = total[
        pl.ds(pl.multiple_of((1 - side) * half_rows, half_rows), half_rows), :
    ].T.astype(BF16)


def project(first, second, columns_map, place):
    width, depth = columns_map.shape
    rows = first[0].shape[1]
    counts = [part.shape[0] for part in first]
    total_rows = rows * sum(counts)
    steps = 4
    anywhere = pl.BlockSpec(memory_space=pl.ANY)
    whole = pl.BlockSpec(memory_space=pltpu.VMEM)
    return pl.pallas_call(
        functools.partial(
            project_kernel, counts=counts, rows=rows, depths=depth // 2, steps=steps
        ),
        in_specs=[pl.BlockSpec(memory_space=pltpu.SMEM)] + [anywhere] * (2 * len(counts) + 1),
        out_specs=[whole] * 2,
        out_shape=[
            jax.ShapeDtypeStruct((width, total_rows // 2), F32),
            jax.ShapeDtypeStruct((width, total_rows // 2), BF16),
        ],
        scratch_shapes=[
            pltpu.VMEM((total_rows, first[0].shape[2]), BF16),
            pltpu.VMEM((total_rows, second[0].shape[2]), BF16),
            pltpu.VMEM((width, depth), BF16),
            pltpu.VMEM((total_rows, width), F32),
            pltpu.SemaphoreType.DMA((2 * sum(counts),)),
            pltpu.SemaphoreType.DMA((steps,)),
        ],
        compiler_params=pltpu.CompilerParams(vmem_limit_bytes=60 * 2**20),
        cost_estimate=pl.CostEstimate(
            flops=2 * total_rows * depth * width,
            bytes_accessed=2 * (total_rows * depth + depth * width),
            transcendentals=0,
        ),
    )(place, *first, *second, columns_map)


def expert_kernel(place_ref, *refs, blocks, heights, halves, carried, sizes):
    count = len(blocks)
    own, other, refs = refs[:count], refs[count : 2 * count], refs[2 * count :]
    gain_refs, in_ref, refs = refs[:2], refs[2], refs[3:]
    sums_in, refs = refs[: 2 * carried], refs[2 * carried :]
    if sizes:
        gate_ref, down_ref, *refs = refs
        activated, outs, refs = refs[0], refs[1:5], refs[5:]
        total, squares, weights, rows, arrived, part_arrived = refs[:6]
        results, down, down_arrived, sent = refs[6:]
        width = down.shape[1] // 2
        down_copies = []
        for half in (0, 1):
            columns = pl.ds(half * width, width)
            down_copies.append(
                pltpu.make_async_copy(
                    down_ref.at[:, columns], down.at[:, columns], down_arrived.at[half]
                )
            )
    else:
        total, squares, weights, rows, arrived, part_arrived = refs
    lanes = rows.shape[1] // 2
    offsets = [sum(n * h for n, h in zip(blocks[:at], heights[:at])) for at in range(count + 1)]
    spots = []
    for entry in range(count):
        for k in range(blocks[entry]):
            row = offsets[entry] + k * heights[entry]
            spots.append((entry, k, row, heights[entry]))
    part_copies, weight_copies = [], []
    for at, (entry, k, row, height) in enumerate(spots):
        for side, ref in enumerate((own[entry], other[entry])):
            part_copies.append(
                pltpu.make_async_copy(
                    ref.at[k],
                    rows.at[pl.ds(row, height), pl.ds(side * lanes, lanes)],
                    part_arrived.at[2 * at + side],
                )
            )
        source = pl.multiple_of(place_ref[at], 8)
        weight_copies.append(
            pltpu.make_async_copy(
                in_ref.at[pl.ds(source, height)], weights.at[pl.ds(row, height)], arrived.at[at]
            )
        )
    for copy in part_copies + weight_copies:
        copy.start()
    if sizes:
        for copy in down_copies:
            copy.start()
    if sums_in:
        squares[...] = sums_in[1][...]
    else:
        squares[...] = jnp.zeros_like(squares)
    for at, (entry, k, row, height) in enumerate(spots):
        part_copies[2 * at].wait()
        part_copies[2 * at + 1].wait()
        wide = rows[row : row + height].astype(F32)
        squares[...] += jnp.sum((wide * wide).reshape(height // 8, 8, 2 * lanes), axis=0)
        lane = lax.broadcasted_iota(jnp.int32, gain_refs[halves[entry]].shape, 1)
        gain = jnp.where(lane == place_ref[len(spots) + at], gain_refs[halves[entry]][...], 0.0)
        gain = jnp.sum(gain, axis=1, keepdims=True)
        rows[row : row + height] = (wide * gain).astype(BF16)
    for entry in range(count):
        for at, spot in enumerate(spots):
            if spot[0] == entry:
                weight_copies[at].wait()
        term = lax.dot_general(
            rows[offsets[entry] : offsets[entry + 1]],
            weights[offsets[entry] : offsets[entry + 1]],
            (((0,), (0,)), ((), ())),
            preferred_element_type=F32,
        )
        if entry:
            total[...] += term
        elif sums_in:
            total[...] = sums_in[0][...] + term
        else:
            total[...] = term
    if not sizes:
        return

    units = total.shape[1] // 2
    mean = jnp.sum(squares[...].T, axis=1, keepdims=True) / in_ref.shape[0]
    level = lax.rsqrt(mean + 1e-06)
    gate_part = total[:, :units] * level
    up_part = total[:, units:] * level
    raised = gate_part / (1.0 + jnp.exp(-gate_part))
    total[:, :units] = raised * up_part * gate_ref[...]
    owner_rows, _ = sizes
    side_rows = total.shape[0] // 2
    order_at = 2 * len(spots)
    for first_row in (0, side_rows):
        for pair in range(side_rows // (2 * owner_rows)):
            pieces = []
            for j in (0, 1):
                row = first_row + place_ref[order_at + 2 * pair + j] * owner_rows
                row = pl.multiple_of(row, owner_rows)
                pieces.append(total[pl.ds(row, owner_rows), :units])
            row = first_row + 2 * pair * owner_rows
            activated[row : row + 2 * owner_rows, :] = jnp.concatenate(pieces).astype(BF16)
    lower(activated, down, results, outs, sent, down_copies, sizes, False)


def lower_kernel(activated_ref, down_ref, *refs, sizes, kept):
    outs, (results, down, arrived, sent) = refs[:4], refs[4:]
    copies = []
    width = down.shape[1] // 2
    for half in (0, 1):
        columns = pl.ds(half * width, width)
        copies.append(
            pltpu.make_async_copy(down_ref.at[:, columns], down.at[:, columns], arrived.at[half])
        )
        copies[-1].start()
    lower(activated_ref, down, results, outs, sent, copies, sizes, kept)


def lower(activated, down, results, outs, sent, arrivals, sizes, kept):
    _, moved = sizes
    width = down.shape[1] // 2
    tile = 512
    side_rows = activated.shape[0] // 2
    plane_rows = side_rows // 4
    copies = []
    for half in (0, 1):
        order = [at for at in range(4) if (at in moved[half]) != kept]
        rows = [
            activated[side * side_rows + at * plane_rows : side * side_rows + (at + 1) * plane_rows, :]
            for side in (1, 0)
            for at in order
        ]
        rows = jnp.concatenate(rows)
        arrivals[half].wait()
        for column in range(0, width, tile):
            results[half, :, column : column + tile] = jnp.dot(
                rows,
                down[:, half * width + column : half * width + column + tile],
                preferred_element_type=F32,
            ).astype(BF16)
        for at, side in enumerate((1, 0)):
            copies.append(
                pltpu.make_async_copy(
                    results.at[half, pl.ds(at * 2 * plane_rows, 2 * plane_rows)],
                    outs[2 * half + side],
                    sent.at[len(copies)],
                )
            )
            copies[-1].start()
    for copy in copies:
        copy.wait()


def lower_kept(activated, down, sizes):
    tokens, units = activated.shape
    anywhere = pl.BlockSpec(memory_space=pl.ANY)
    return pl.pallas_call(
        functools.partial(lower_kernel, sizes=sizes, kept=True),
        in_specs=[pl.BlockSpec(memory_space=pltpu.VMEM), anywhere],
        out_specs=[anywhere] * 4,
        out_shape=[jax.ShapeDtypeStruct((tokens // 4, down.shape[1] // 2), BF16)] * 4,
        scratch_shapes=[
            pltpu.VMEM((2, tokens // 2, down.shape[1] // 2), BF16),
            pltpu.VMEM(down.shape, BF16),
            pltpu.SemaphoreType.DMA((2,)),
            pltpu.SemaphoreType.DMA((4,)),
        ],
        compiler_params=pltpu.CompilerParams(vmem_limit_bytes=LAST_VMEM_LIMIT),
        cost_estimate=pl.CostEstimate(
            flops=tokens * units * down.shape[1],
            bytes_accessed=2 * down.shape[1] * (units + tokens // 2),
            transcendentals=0,
        ),
    )(activated, down)


def expert_rows(parts, other_parts, halves, gains, weights, place, carried, finish):
    model_width, double = weights.shape
    lanes = parts[0].shape[2]
    tokens = 2 * lanes
    blocks = [part.shape[0] for part in parts]
    heights = [part.shape[1] for part in parts]
    depth = sum(n * h for n, h in zip(blocks, heights))
    whole = pl.BlockSpec(memory_space=pltpu.VMEM)
    anywhere = pl.BlockSpec(memory_space=pl.ANY)
    sums = [jax.ShapeDtypeStruct((tokens, double), F32), jax.ShapeDtypeStruct((8, tokens), F32)]
    scratch = [
        pltpu.VMEM((depth, double), BF16),
        pltpu.VMEM((depth, tokens), BF16),
        pltpu.SemaphoreType.DMA((sum(blocks),)),
        pltpu.SemaphoreType.DMA((2 * sum(blocks),)),
    ]
    operands = [place, *parts, *other_parts, *gains, weights, *carried]
    in_specs = [pl.BlockSpec(memory_space=pltpu.SMEM)] + [anywhere] * (2 * len(parts))
    in_specs += [whole] * 2 + [anywhere] + [whole] * len(carried)
    sizes = None
    out_shape, out_specs = sums, [whole] * 2
    if finish is not None:
        gates, down, *sizes = finish
        operands += [gates, down]
        in_specs += [whole, anywhere]
        out_shape = [jax.ShapeDtypeStruct((tokens, double // 2), BF16)]
        out_shape += [jax.ShapeDtypeStruct((tokens // 4, model_width // 2), BF16)] * 4
        out_specs = [whole] + [anywhere] * 4
        scratch = [pltpu.VMEM(a.shape, F32) for a in sums] + scratch
        scratch += [
            pltpu.VMEM((2, tokens // 2, model_width // 2), BF16),
            pltpu.VMEM(down.shape, BF16),
            pltpu.SemaphoreType.DMA((2,)),
            pltpu.SemaphoreType.DMA((4,)),
        ]
    return pl.pallas_call(
        functools.partial(
            expert_kernel,
            blocks=blocks,
            heights=heights,
            halves=halves,
            carried=len(carried) // 2,
            sizes=sizes,
        ),
        in_specs=in_specs,
        out_specs=out_specs,
        out_shape=out_shape,
        scratch_shapes=scratch,
        compiler_params=pltpu.CompilerParams(
            vmem_limit_bytes=VMEM_LIMIT if finish is None else LAST_VMEM_LIMIT
        ),
        cost_estimate=pl.CostEstimate(
            flops=2 * tokens * depth * double,
            bytes_accessed=2 * depth * (double + tokens),
            transcendentals=0,
        ),
    )(*operands)


def on_device(
    queries,
    latent_cache,
    lengths,
    value_lift,
    output_map,
    residual,
    norm_gain,
    expert_ids,
    gate_values,
    expert_in,
    expert_down,
):
    request_count = queries.shape[0]
    latent_width = value_lift.shape[1]
    half_heads = value_lift.shape[0]
    value_width = value_lift.shape[2]
    token_count, model_width = residual.shape
    chips = lax.axis_size("dev")
    plane = 4
    line = chips // plane
    columns = output_map.shape[1]
    experts = chips // 2
    units = expert_down.shape[1]
    side = lax.axis_index("side")
    chip = lax.axis_index("dev")
    line_at, plane_at = chip // plane, chip % plane
    half_tokens = token_count * chips

    def line_hop(value, k):
        return hop(value, "dev", chips, k * plane)

    def plane_hop(value, k):
        return hop(value, "dev", chips, k)

    def swap(value):
        return hop(value, "side", 2, 1)

    def placed(offsets):
        return [(line_at ^ k_line) * plane + (plane_at ^ k_plane) for k_plane, k_line in offsets]

    chosen = expert_ids[:, :, None] == jnp.arange(experts, dtype=jnp.int32)[None, None, :]
    weights = jnp.sum(jnp.where(chosen, gate_values[:, :, None], 0.0), axis=1)
    weights_high = lax.reduce_precision(weights, 8, 7)
    weight_terms = jnp.concatenate([weights_high, weights - weights_high], axis=1).astype(BF16)
    weight_width = -(-token_count * 2 * experts // (request_count * 128)) * 128
    weight_block = jnp.pad(
        weight_terms.reshape(-1), (0, request_count * weight_width - weight_terms.size)
    ).reshape(request_count, weight_width)

    own_latent, sent_latent, stats = attend(
        queries, latent_cache.swapaxes(1, 2), lengths, side, latent_width
    )
    stats = stats[:, :, :2]

    def heads_of(value, which):
        return lax.dynamic_slice_in_dim(value, which * half_heads, half_heads, 1)

    other_latent = swap(sent_latent)
    other_stats = swap(heads_of(stats, 1 - side))
    own_stats = heads_of(stats, side)
    top = jnp.maximum(own_stats[:, :, 0], other_stats[:, :, 0])
    own_share = own_stats[:, :, 1] * jnp.exp(own_stats[:, :, 0] - top)
    other_share = other_stats[:, :, 1] * jnp.exp(other_stats[:, :, 0] - top)
    share_sum = own_share + other_share
    latent_out = (
        own_latent.astype(F32) * (own_share / share_sum)[:, :, None]
        + other_latent.astype(F32) * (other_share / share_sum)[:, :, None]
    ).astype(BF16)
    head_values = jnp.einsum("rhc,hcv->rhv", latent_out, value_lift, preferred_element_type=F32)
    head_values = head_values.astype(BF16).reshape(request_count, half_heads * value_width)

    groups = [list(range(line // 2)), list(range(line // 2, line))]

    half_depth = half_heads * value_width // 2
    first_width = half_depth + weight_width
    sent = jnp.concatenate(
        [head_values[:, :half_depth], weight_block, head_values[:, half_depth:]], axis=1
    )
    sent, residual, expert_in, norm_gain = lax.optimization_barrier(
        (sent, residual, expert_in, norm_gain)
    )

    (first, second), in_rows, residual = gather(
        sent,
        lambda column: (column[:, :, :first_width], column[:, :, first_width:]),
        groups,
        line_hop,
        plane_hop,
        expert_in.reshape(model_width, 2 * units),
        residual,
    )

    residual_blocks = residual.reshape(token_count, chips, columns).swapaxes(0, 1)
    residual_columns = lax.all_to_all(
        residual_blocks, "dev", split_axis=0, concat_axis=0, tiled=True
    )

    place = jnp.stack(
        [
            at
            for half in (first, second)
            for _, offsets in half
            for at in placed(offsets)
        ]
        + [side]
    ).astype(jnp.int32)
    first_parts, second_parts = [[part for part, _ in half] for half in (first, second)]
    own_columns, sent_columns = project(first_parts, second_parts, output_map.T, place)
    sent_columns, residual_columns = lax.optimization_barrier((sent_columns, residual_columns))
    residual_columns = residual_columns.reshape(half_tokens, columns).T
    attention = own_columns + swap(sent_columns).astype(F32)
    hidden = (residual_columns.astype(F32) + attention).astype(BF16)

    gathered = jnp.concatenate([part[:, :, half_depth:] for part, _ in first])
    gathered = gathered.reshape(chips, -1)[:, : token_count * 2 * experts]
    gathered = gathered.reshape(chips, token_count, 2, experts).astype(F32)
    gathered = lax.dynamic_index_in_dim(gathered, chip // 2, 3, keepdims=False).sum(axis=2)
    spots = place[:chips]
    own_gates = jnp.zeros((chips, token_count), F32).at[spots].set(gathered).reshape(-1, 1)
    gates = jnp.concatenate([own_gates, swap(own_gates)])

    first_rows = -(-columns // 32) * 16
    gains = norm_gain.astype(F32).reshape(chips, columns).T
    gains = [gains[:first_rows], gains[first_rows:]]
    hidden_groups = [list(range(line))]
    (first, second), gates, _ = gather(
        hidden,
        lambda column: (column[:, :first_rows], column[:, first_rows:]),
        hidden_groups,
        line_hop,
        plane_hop,
        gates,
        (),
    )
    down = expert_down[0]
    out_at = [(p, k) for p in range(plane) for k in range(line)]
    moved = ((1, 3), (2, 3))
    stages = [[0], [1], [2]]
    carried = ()
    for at, stage in enumerate(stages):
        last = at == len(stages) - 1
        parts, halves, spots = [], [], []
        for which in stage:
            for half, (part, offsets) in enumerate((first[which], second[which])):
                parts.append(part)
                halves.append(half)
                spots += [(spot, half) for spot in placed(offsets)]
        table = [spot * columns + half * first_rows for spot, half in spots]
        table += [spot for spot, _ in spots]
        if last:
            parts, carried = lax.optimization_barrier((parts, carried))
            table += placed((p, k) for p in range(plane) for k in range(line))
        carried = expert_rows(
            parts,
            [swap(part) for part in parts],
            halves,
            gains,
            in_rows,
            jnp.stack(table).astype(jnp.int32),
            carried,
            (gates, down, token_count, moved) if last else None,
        )

    def both_cores(partials):
        other = [swap(partials[2 * h + 1]).astype(F32) for h in (0, 1)]
        return [partials[2 * h].astype(F32) + other[h] for h in (0, 1)]

    activated, *partials = carried
    sent_sum = [part.astype(BF16) for part in both_cores(partials)]
    activated, _ = lax.optimization_barrier((activated, sent_sum))
    kept = both_cores(lower_kept(activated, down, (token_count, moved)))
    half_sums = []
    for h, (one, two) in enumerate(((1, 2), (2, 1))):
        summed = kept[h] + plane_hop(sent_sum[h], one).astype(F32)
        rows = summed.shape[0] // 2
        arrived = plane_hop(summed[rows:].astype(BF16), two).astype(F32)
        half_sums.append(summed[:rows] + arrived)
    plane_sum = jnp.concatenate(half_sums, axis=1).reshape(line, token_count, model_width)
    routed_sum = plane_sum[0]
    for k in range(1, line):
        routed_sum += line_hop(plane_sum[k].astype(BF16), k).astype(F32)

    tokens = chip * token_count + jnp.arange(token_count, dtype=jnp.int32)
    picked = (tokens[:, None] == jnp.arange(half_tokens, dtype=jnp.int32)[None, :]).astype(BF16)
    own_parts, _ = lax.optimization_barrier(([part for half in (first, second) for part, _ in half], sent_sum))
    own_rows = []
    for half, parts in ((first, own_parts[: len(first)]), (second, own_parts[len(first) :])):
        blocks = jnp.concatenate(
            [jnp.einsum("qt,krt->kqr", picked, part, preferred_element_type=F32) for part in parts]
        )
        offsets = [at for _, part_offsets in half for at in part_offsets]
        spots = jnp.stack(placed(offsets))
        own_rows.append(jnp.zeros_like(blocks).at[spots].set(blocks))
    own_hidden = jnp.concatenate(own_rows, axis=2).swapaxes(0, 1).reshape(token_count, model_width)
    return (own_hidden + routed_sum).astype(BF16)


def solution(mesh):
    in_specs = (
        P("dev", None, None),
        P("dev", "side", None),
        P("dev"),
        P("side", None, None),
        P("side", "dev"),
        P(("side", "dev"), None),
        P(),
        P(("side", "dev"), None),
        P(("side", "dev"), None),
        P("dev", None, None, "side"),
        P("dev", "side", None),
    )
    out_specs = P(("side", "dev"), None)
    return jax.shard_map(
        on_device, mesh=mesh, in_specs=in_specs, out_specs=out_specs, check_vma=False
    )
```

```python
import functools

import jax
import jax.numpy as jnp
from jax import lax
from jax.experimental import pallas as pl
from jax.experimental.pallas import tpu as pltpu
from jax.sharding import PartitionSpec as P

QKD = 192
F32 = jnp.float32
BF16 = jnp.bfloat16
VMEM_LIMIT = 48 * 2**20
LAST_VMEM_LIMIT = 51 * 2**20


def hop(value, axis, size, mask):
    return lax.ppermute(value, axis, [(i, i ^ mask) for i in range(size)])


def gather(block, split, groups, line_hop, plane_hop, beside, after):
    arrived = {0: block}
    for group in groups:
        for k in group:
            if k:
                arrived[k] = line_hop(block, k)
    halves = ([], [])
    for at, group in enumerate(groups):
        if at == 0 and len(group) > 1:
            block, arrived[group[1]] = lax.optimization_barrier((block, arrived[group[1]]))
            arrived[0] = block
        column = jnp.stack([arrived[k] for k in group])
        if at == len(groups) - 1:
            column, beside = lax.optimization_barrier((column, beside))
        split_column = split(column)
        nears = [plane_hop(half, one) for half, one in zip(split_column, (1, 2))]
        if at == len(groups) - 1:
            nears, after = lax.optimization_barrier((nears, after))
        for parts, half, near, (one, two) in zip(halves, split_column, nears, ((1, 2), (2, 1))):
            rest = plane_hop(jnp.concatenate([half, near]), two)
            parts.append((half, [(0, k) for k in group]))
            parts.append((near, [(one, k) for k in group]))
            parts.append((rest, [(p, k) for p in (two, 3) for k in group]))
    return halves, beside, after


def attend_kernel(
    length_ref, side_ref, query_ref, cache_ref, own_ref, other_ref, stats_ref, latents, *, scale
):
    group, heads, _ = query_ref.shape
    latent_width = own_ref.shape[2]
    slots = cache_ref.shape[2]
    half = heads // 2
    first = pl.program_id(0) * group
    side = side_ref[0]
    positions = side * slots + lax.broadcasted_iota(jnp.int32, (heads, slots), 1)
    lanes = lax.broadcasted_iota(jnp.int32, (heads, stats_ref.shape[2]), 1)
    everyone = range(group)
    usable = [positions < length_ref[first + at] for at in everyone]
    scores = [
        jnp.dot(query_ref[at], cache_ref[at], preferred_element_type=F32) * scale for at in everyone
    ]
    masked = [jnp.where(usable[at], scores[at], -1e30) for at in everyone]
    tops = [jnp.max(masked[at], axis=1, keepdims=True) for at in everyone]
    raised = [jnp.where(usable[at], jnp.exp(masked[at] - tops[at]), 0.0) for at in everyone]
    totals = [jnp.sum(raised[at], axis=1, keepdims=True) for at in everyone]
    sums = [
        lax.dot_general(
            raised[at].astype(BF16),
            cache_ref[at, :latent_width, :],
            (((1,), (1,)), ((), ())),
            preferred_element_type=F32,
        )
        for at in everyone
    ]
    for at in everyone:
        latents[at] = sums[at] / jnp.maximum(totals[at], 1e-30)
        stats_ref[at] = jnp.where(lanes == 0, tops[at], totals[at])
    for at in everyone:
        own_ref[at] = latents[at, pl.ds(pl.multiple_of(side * half, half), half), :].astype(BF16)
        other_ref[at] = latents[
            at, pl.ds(pl.multiple_of((1 - side) * half, half), half), :
        ].astype(BF16)


def attend(queries, cache_columns, lengths, side, latent_width):
    requests, heads, width = queries.shape
    slots = cache_columns.shape[2]
    group = 8
    return pl.pallas_call(
        functools.partial(attend_kernel, scale=QKD ** (-0.5)),
        grid_spec=pltpu.PrefetchScalarGridSpec(
            num_scalar_prefetch=2,
            grid=(requests // group,),
            in_specs=[
                pl.BlockSpec((group, heads, width), lambda r, lengths, side: (r, 0, 0)),
                pl.BlockSpec((group, width, slots), lambda r, lengths, side: (r, 0, 0)),
            ],
            out_specs=[
                pl.BlockSpec((group, heads // 2, latent_width), lambda r, lengths, side: (r, 0, 0)),
                pl.BlockSpec((group, heads // 2, latent_width), lambda r, lengths, side: (r, 0, 0)),
                pl.BlockSpec((group, heads, 128), lambda r, lengths, side: (r, 0, 0)),
            ],
            scratch_shapes=[pltpu.VMEM((group, heads, latent_width), F32)],
        ),
        out_shape=[
            jax.ShapeDtypeStruct((requests, heads // 2, latent_width), BF16),
            jax.ShapeDtypeStruct((requests, heads // 2, latent_width), BF16),
            jax.ShapeDtypeStruct((requests, heads, 128), F32),
        ],
        compiler_params=pltpu.CompilerParams(vmem_limit_bytes=48 * 2**20),
        cost_estimate=pl.CostEstimate(
            flops=4 * requests * heads * width * slots,
            bytes_accessed=2 * requests * width * (heads + slots),
            transcendentals=requests * heads * slots,
        ),
    )(lengths, side.reshape(1), queries, cache_columns)


def project_kernel(place_ref, *refs, counts, rows, depths, steps):
    groups = len(counts)
    parts = (refs[:groups], refs[groups : 2 * groups])
    map_ref, own_ref, send_ref, first, second, mapping, total, arrived, map_arrived = refs[2 * groups :]
    blocks = sum(counts)
    copies, map_copies = [], []
    for half, left in enumerate((first, second)):
        at = half * blocks
        for part, count in zip(parts[half], counts):
            for k in range(count):
                row = pl.multiple_of(place_ref[at] * rows, rows)
                copies.append(
                    pltpu.make_async_copy(part.at[k], left.at[pl.ds(row, rows)], arrived.at[at])
                )
                at += 1
    tile = mapping.shape[1] // steps
    for step in range(steps):
        columns = pl.ds(step * tile, tile)
        map_copies.append(
            pltpu.make_async_copy(
                map_ref.at[:, columns], mapping.at[:, columns], map_arrived.at[step]
            )
        )
    in_half = steps // 2
    for half in (0, 1):
        for copy in copies[half * blocks : (half + 1) * blocks]:
            copy.start()
        for copy in map_copies[half * in_half : (half + 1) * in_half]:
            copy.start()
    for step in range(steps):
        if step % in_half == 0:
            half = step // in_half
            for copy in copies[half * blocks : (half + 1) * blocks]:
                copy.wait()
        map_copies[step].wait()
        left = first if step * tile < depths else second
        column = step * tile if step * tile < depths else step * tile - depths
        term = lax.dot_general(
            left[:, column : column + tile],
            mapping[:, step * tile : (step + 1) * tile],
            (((1,), (1,)), ((), ())),
            preferred_element_type=F32,
        )
        if step:
            total[...] += term
        else:
            total[...] = term
    half_rows = total.shape[0] // 2
    side = place_ref[2 * blocks]
    own_ref[...] = total[pl.ds(pl.multiple_of(side * half_rows, half_rows), half_rows), :].T
    send_ref[...] = total[
        pl.ds(pl.multiple_of((1 - side) * half_rows, half_rows), half_rows), :
    ].T.astype(BF16)


def project(first, second, columns_map, place):
    width, depth = columns_map.shape
    rows = first[0].shape[1]
    counts = [part.shape[0] for part in first]
    total_rows = rows * sum(counts)
    steps = 4
    anywhere = pl.BlockSpec(memory_space=pl.ANY)
    whole = pl.BlockSpec(memory_space=pltpu.VMEM)
    return pl.pallas_call(
        functools.partial(
            project_kernel, counts=counts, rows=rows, depths=depth // 2, steps=steps
        ),
        in_specs=[pl.BlockSpec(memory_space=pltpu.SMEM)] + [anywhere] * (2 * len(counts) + 1),
        out_specs=[whole] * 2,
        out_shape=[
            jax.ShapeDtypeStruct((width, total_rows // 2), F32),
            jax.ShapeDtypeStruct((width, total_rows // 2), BF16),
        ],
        scratch_shapes=[
            pltpu.VMEM((total_rows, first[0].shape[2]), BF16),
            pltpu.VMEM((total_rows, second[0].shape[2]), BF16),
            pltpu.VMEM((width, depth), BF16),
            pltpu.VMEM((total_rows, width), F32),
            pltpu.SemaphoreType.DMA((2 * sum(counts),)),
            pltpu.SemaphoreType.DMA((steps,)),
        ],
        compiler_params=pltpu.CompilerParams(vmem_limit_bytes=50 * 2**20),
        cost_estimate=pl.CostEstimate(
            flops=2 * total_rows * depth * width,
            bytes_accessed=2 * (total_rows * depth + depth * width),
            transcendentals=0,
        ),
    )(place, *first, *second, columns_map)


def expert_kernel(place_ref, *refs, blocks, heights, halves, carried, sizes):
    count = len(blocks)
    own, other, refs = refs[:count], refs[count : 2 * count], refs[2 * count :]
    gain_refs, in_ref, refs = refs[:2], refs[2], refs[3:]
    sums_in, refs = refs[: 2 * carried], refs[2 * carried :]
    if sizes:
        gate_ref, down_ref, *refs = refs
        activated, outs, refs = refs[0], refs[1:5], refs[5:]
        total, squares, weights, rows, arrived, part_arrived = refs[:6]
        results, down, down_arrived, sent = refs[6:]
        width = down.shape[1] // 2
        down_copies = []
        for half in (0, 1):
            columns = pl.ds(half * width, width)
            down_copies.append(
                pltpu.make_async_copy(
                    down_ref.at[:, columns], down.at[:, columns], down_arrived.at[half]
                )
            )
    else:
        total, squares, weights, rows, arrived, part_arrived = refs
    lanes = rows.shape[1] // 2
    offsets = [sum(n * h for n, h in zip(blocks[:at], heights[:at])) for at in range(count + 1)]
    spots = []
    for entry in range(count):
        for k in range(blocks[entry]):
            row = offsets[entry] + k * heights[entry]
            spots.append((entry, k, row, heights[entry]))
    part_copies, weight_copies = [], []
    for at, (entry, k, row, height) in enumerate(spots):
        for side, ref in enumerate((own[entry], other[entry])):
            part_copies.append(
                pltpu.make_async_copy(
                    ref.at[k],
                    rows.at[pl.ds(row, height), pl.ds(side * lanes, lanes)],
                    part_arrived.at[2 * at + side],
                )
            )
        source = pl.multiple_of(place_ref[at], 8)
        weight_copies.append(
            pltpu.make_async_copy(
                in_ref.at[pl.ds(source, height)], weights.at[pl.ds(row, height)], arrived.at[at]
            )
        )
    for copy in part_copies + weight_copies:
        copy.start()
    if sizes:
        for copy in down_copies:
            copy.start()
    if sums_in:
        squares[...] = sums_in[1][...]
    else:
        squares[...] = jnp.zeros_like(squares)
    for at, (entry, k, row, height) in enumerate(spots):
        part_copies[2 * at].wait()
        part_copies[2 * at + 1].wait()
        wide = rows[row : row + height].astype(F32)
        squares[...] += jnp.sum((wide * wide).reshape(height // 8, 8, 2 * lanes), axis=0)
        lane = lax.broadcasted_iota(jnp.int32, gain_refs[halves[entry]].shape, 1)
        gain = jnp.where(lane == place_ref[len(spots) + at], gain_refs[halves[entry]][...], 0.0)
        gain = jnp.sum(gain, axis=1, keepdims=True)
        rows[row : row + height] = (wide * gain).astype(BF16)
    for entry in range(count):
        for at, spot in enumerate(spots):
            if spot[0] == entry:
                weight_copies[at].wait()
        term = lax.dot_general(
            rows[offsets[entry] : offsets[entry + 1]],
            weights[offsets[entry] : offsets[entry + 1]],
            (((0,), (0,)), ((), ())),
            preferred_element_type=F32,
        )
        if entry:
            total[...] += term
        elif sums_in:
            total[...] = sums_in[0][...] + term
        else:
            total[...] = term
    if not sizes:
        return

    units = total.shape[1] // 2
    mean = jnp.sum(squares[...].T, axis=1, keepdims=True) / in_ref.shape[0]
    level = lax.rsqrt(mean + 1e-06)
    gate_part = total[:, :units] * level
    up_part = total[:, units:] * level
    raised = gate_part / (1.0 + jnp.exp(-gate_part))
    total[:, :units] = raised * up_part * gate_ref[...]
    owner_rows, _ = sizes
    side_rows = total.shape[0] // 2
    order_at = 2 * len(spots)
    for first_row in (0, side_rows):
        for pair in range(side_rows // (2 * owner_rows)):
            pieces = []
            for j in (0, 1):
                row = first_row + place_ref[order_at + 2 * pair + j] * owner_rows
                row = pl.multiple_of(row, owner_rows)
                pieces.append(total[pl.ds(row, owner_rows), :units])
            row = first_row + 2 * pair * owner_rows
            activated[row : row + 2 * owner_rows, :] = jnp.concatenate(pieces).astype(BF16)
    lower(activated, down, results, outs, sent, down_copies, sizes, False)


def lower_kernel(activated_ref, down_ref, *refs, sizes, kept):
    outs, (results, down, arrived, sent) = refs[:4], refs[4:]
    copies = []
    width = down.shape[1] // 2
    for half in (0, 1):
        columns = pl.ds(half * width, width)
        copies.append(
            pltpu.make_async_copy(down_ref.at[:, columns], down.at[:, columns], arrived.at[half])
        )
        copies[-1].start()
    lower(activated_ref, down, results, outs, sent, copies, sizes, kept)


def lower(activated, down, results, outs, sent, arrivals, sizes, kept):
    _, moved = sizes
    width = down.shape[1] // 2
    tile = 512
    side_rows = activated.shape[0] // 2
    plane_rows = side_rows // 4
    copies = []
    for half in (0, 1):
        order = [at for at in range(4) if (at in moved[half]) != kept]
        rows = [
            activated[side * side_rows + at * plane_rows : side * side_rows + (at + 1) * plane_rows, :]
            for side in (1, 0)
            for at in order
        ]
        rows = jnp.concatenate(rows)
        arrivals[half].wait()
        for column in range(0, width, tile):
            results[half, :, column : column + tile] = jnp.dot(
                rows,
                down[:, half * width + column : half * width + column + tile],
                preferred_element_type=F32,
            ).astype(BF16)
        for at, side in enumerate((1, 0)):
            copies.append(
                pltpu.make_async_copy(
                    results.at[half, pl.ds(at * 2 * plane_rows, 2 * plane_rows)],
                    outs[2 * half + side],
                    sent.at[len(copies)],
                )
            )
            copies[-1].start()
    for copy in copies:
        copy.wait()


def lower_kept(activated, down, sizes):
    tokens, units = activated.shape
    anywhere = pl.BlockSpec(memory_space=pl.ANY)
    return pl.pallas_call(
        functools.partial(lower_kernel, sizes=sizes, kept=True),
        in_specs=[pl.BlockSpec(memory_space=pltpu.VMEM), anywhere],
        out_specs=[anywhere] * 4,
        out_shape=[jax.ShapeDtypeStruct((tokens // 4, down.shape[1] // 2), BF16)] * 4,
        scratch_shapes=[
            pltpu.VMEM((2, tokens // 2, down.shape[1] // 2), BF16),
            pltpu.VMEM(down.shape, BF16),
            pltpu.SemaphoreType.DMA((2,)),
            pltpu.SemaphoreType.DMA((4,)),
        ],
        compiler_params=pltpu.CompilerParams(vmem_limit_bytes=LAST_VMEM_LIMIT),
        cost_estimate=pl.CostEstimate(
            flops=tokens * units * down.shape[1],
            bytes_accessed=2 * down.shape[1] * (units + tokens // 2),
            transcendentals=0,
        ),
    )(activated, down)


def expert_rows(parts, other_parts, halves, gains, weights, place, carried, finish):
    model_width, double = weights.shape
    lanes = parts[0].shape[2]
    tokens = 2 * lanes
    blocks = [part.shape[0] for part in parts]
    heights = [part.shape[1] for part in parts]
    depth = sum(n * h for n, h in zip(blocks, heights))
    whole = pl.BlockSpec(memory_space=pltpu.VMEM)
    anywhere = pl.BlockSpec(memory_space=pl.ANY)
    sums = [jax.ShapeDtypeStruct((tokens, double), F32), jax.ShapeDtypeStruct((8, tokens), F32)]
    scratch = [
        pltpu.VMEM((depth, double), BF16),
        pltpu.VMEM((depth, tokens), BF16),
        pltpu.SemaphoreType.DMA((sum(blocks),)),
        pltpu.SemaphoreType.DMA((2 * sum(blocks),)),
    ]
    operands = [place, *parts, *other_parts, *gains, weights, *carried]
    in_specs = [pl.BlockSpec(memory_space=pltpu.SMEM)] + [anywhere] * (2 * len(parts))
    in_specs += [whole] * 2 + [anywhere] + [whole] * len(carried)
    sizes = None
    out_shape, out_specs = sums, [whole] * 2
    if finish is not None:
        gates, down, *sizes = finish
        operands += [gates, down]
        in_specs += [whole, anywhere]
        out_shape = [jax.ShapeDtypeStruct((tokens, double // 2), BF16)]
        out_shape += [jax.ShapeDtypeStruct((tokens // 4, model_width // 2), BF16)] * 4
        out_specs = [whole] + [anywhere] * 4
        scratch = [pltpu.VMEM(a.shape, F32) for a in sums] + scratch
        scratch += [
            pltpu.VMEM((2, tokens // 2, model_width // 2), BF16),
            pltpu.VMEM(down.shape, BF16),
            pltpu.SemaphoreType.DMA((2,)),
            pltpu.SemaphoreType.DMA((4,)),
        ]
    return pl.pallas_call(
        functools.partial(
            expert_kernel,
            blocks=blocks,
            heights=heights,
            halves=halves,
            carried=len(carried) // 2,
            sizes=sizes,
        ),
        in_specs=in_specs,
        out_specs=out_specs,
        out_shape=out_shape,
        scratch_shapes=scratch,
        compiler_params=pltpu.CompilerParams(
            vmem_limit_bytes=VMEM_LIMIT if finish is None else LAST_VMEM_LIMIT
        ),
        cost_estimate=pl.CostEstimate(
            flops=2 * tokens * depth * double,
            bytes_accessed=2 * depth * (double + tokens),
            transcendentals=0,
        ),
    )(*operands)


def on_device(
    queries,
    latent_cache,
    lengths,
    value_lift,
    output_map,
    residual,
    norm_gain,
    expert_ids,
    gate_values,
    expert_in,
    expert_down,
):
    request_count = queries.shape[0]
    latent_width = value_lift.shape[1]
    half_heads = value_lift.shape[0]
    value_width = value_lift.shape[2]
    token_count, model_width = residual.shape
    chips = lax.axis_size("dev")
    plane = 4
    line = chips // plane
    columns = output_map.shape[1]
    experts = chips // 2
    units = expert_down.shape[1]
    side = lax.axis_index("side")
    chip = lax.axis_index("dev")
    line_at, plane_at = chip // plane, chip % plane
    half_tokens = token_count * chips

    def line_hop(value, k):
        return hop(value, "dev", chips, k * plane)

    def plane_hop(value, k):
        return hop(value, "dev", chips, k)

    def swap(value):
        return hop(value, "side", 2, 1)

    def placed(offsets):
        return [(line_at ^ k_line) * plane + (plane_at ^ k_plane) for k_plane, k_line in offsets]

    chosen = expert_ids[:, :, None] == jnp.arange(experts, dtype=jnp.int32)[None, None, :]
    weights = jnp.sum(jnp.where(chosen, gate_values[:, :, None], 0.0), axis=1)
    weights_high = lax.reduce_precision(weights, 8, 7)
    weight_terms = jnp.concatenate([weights_high, weights - weights_high], axis=1).astype(BF16)
    weight_width = -(-token_count * 2 * experts // (request_count * 128)) * 128
    weight_block = jnp.pad(
        weight_terms.reshape(-1), (0, request_count * weight_width - weight_terms.size)
    ).reshape(request_count, weight_width)

    own_latent, sent_latent, stats = attend(
        queries, latent_cache.swapaxes(1, 2), lengths, side, latent_width
    )
    stats = stats[:, :, :2]

    def heads_of(value, which):
        return lax.dynamic_slice_in_dim(value, which * half_heads, half_heads, 1)

    other_latent = swap(sent_latent)
    other_stats = swap(heads_of(stats, 1 - side))
    own_stats = heads_of(stats, side)
    top = jnp.maximum(own_stats[:, :, 0], other_stats[:, :, 0])
    own_share = own_stats[:, :, 1] * jnp.exp(own_stats[:, :, 0] - top)
    other_share = other_stats[:, :, 1] * jnp.exp(other_stats[:, :, 0] - top)
    share_sum = own_share + other_share
    latent_out = (
        own_latent.astype(F32) * (own_share / share_sum)[:, :, None]
        + other_latent.astype(F32) * (other_share / share_sum)[:, :, None]
    ).astype(BF16)
    head_values = jnp.einsum("rhc,hcv->rhv", latent_out, value_lift, preferred_element_type=F32)
    head_values = head_values.astype(BF16).reshape(request_count, half_heads * value_width)

    groups = [list(range(line // 2)), list(range(line // 2, line))]

    half_depth = half_heads * value_width // 2
    first_width = half_depth + weight_width
    sent = jnp.concatenate(
        [head_values[:, :half_depth], weight_block, head_values[:, half_depth:]], axis=1
    )
    sent, residual, expert_in, norm_gain = lax.optimization_barrier(
        (sent, residual, expert_in, norm_gain)
    )

    (first, second), in_rows, residual = gather(
        sent,
        lambda column: (column[:, :, :first_width], column[:, :, first_width:]),
        groups,
        line_hop,
        plane_hop,
        expert_in.reshape(model_width, 2 * units),
        residual,
    )

    residual_blocks = residual.reshape(token_count, chips, columns).swapaxes(0, 1)
    residual_columns = lax.all_to_all(
        residual_blocks, "dev", split_axis=0, concat_axis=0, tiled=True
    )

    place = jnp.stack(
        [
            at
            for half in (first, second)
            for _, offsets in half
            for at in placed(offsets)
        ]
        + [side]
    ).astype(jnp.int32)
    first_parts, second_parts = [[part for part, _ in half] for half in (first, second)]
    own_columns, sent_columns = project(first_parts, second_parts, output_map.T, place)
    sent_columns, residual_columns = lax.optimization_barrier((sent_columns, residual_columns))
    residual_columns = residual_columns.reshape(half_tokens, columns).T
    attention = own_columns + swap(sent_columns).astype(F32)
    hidden = (residual_columns.astype(F32) + attention).astype(BF16)

    gathered = jnp.concatenate([part[:, :, half_depth:] for part, _ in first])
    gathered = gathered.reshape(chips, -1)[:, : token_count * 2 * experts]
    gathered = gathered.reshape(chips, token_count, 2, experts).astype(F32)
    gathered = lax.dynamic_index_in_dim(gathered, chip // 2, 3, keepdims=False).sum(axis=2)
    spots = place[:chips]
    own_gates = jnp.zeros((chips, token_count), F32).at[spots].set(gathered).reshape(-1, 1)
    gates = jnp.concatenate([own_gates, swap(own_gates)])

    first_rows = -(-columns // 32) * 16
    gains = norm_gain.astype(F32).reshape(chips, columns).T
    gains = [gains[:first_rows], gains[first_rows:]]
    hidden_groups = [list(range(line))]
    (first, second), gates, _ = gather(
        hidden,
        lambda column: (column[:, :first_rows], column[:, first_rows:]),
        hidden_groups,
        line_hop,
        plane_hop,
        gates,
        (),
    )
    down = expert_down[0]
    out_at = [(p, k) for p in range(plane) for k in range(line)]
    moved = ((1, 3), (2, 3))
    stages = [[0], [1], [2]]
    carried = ()
    for at, stage in enumerate(stages):
        last = at == len(stages) - 1
        parts, halves, spots = [], [], []
        for which in stage:
            for half, (part, offsets) in enumerate((first[which], second[which])):
                parts.append(part)
                halves.append(half)
                spots += [(spot, half) for spot in placed(offsets)]
        table = [spot * columns + half * first_rows for spot, half in spots]
        table += [spot for spot, _ in spots]
        if last:
            parts, carried = lax.optimization_barrier((parts, carried))
            table += placed((p, k) for p in range(plane) for k in range(line))
        carried = expert_rows(
            parts,
            [swap(part) for part in parts],
            halves,
            gains,
            in_rows,
            jnp.stack(table).astype(jnp.int32),
            carried,
            (gates, down, token_count, moved) if last else None,
        )

    def both_cores(partials):
        other = [swap(partials[2 * h + 1]).astype(F32) for h in (0, 1)]
        return [partials[2 * h].astype(F32) + other[h] for h in (0, 1)]

    activated, *partials = carried
    sent_sum = [part.astype(BF16) for part in both_cores(partials)]
    activated, _ = lax.optimization_barrier((activated, sent_sum))
    kept = both_cores(lower_kept(activated, down, (token_count, moved)))
    half_sums = []
    for h, (one, two) in enumerate(((1, 2), (2, 1))):
        summed = kept[h] + plane_hop(sent_sum[h], one).astype(F32)
        rows = summed.shape[0] // 2
        arrived = plane_hop(summed[rows:].astype(BF16), two).astype(F32)
        half_sums.append(summed[:rows] + arrived)
    plane_sum = jnp.concatenate(half_sums, axis=1).reshape(line, token_count, model_width)
    routed_sum = plane_sum[0]
    for k in range(1, line):
        routed_sum += line_hop(plane_sum[k].astype(BF16), k).astype(F32)

    tokens = chip * token_count + jnp.arange(token_count, dtype=jnp.int32)
    picked = (tokens[:, None] == jnp.arange(half_tokens, dtype=jnp.int32)[None, :]).astype(BF16)
    own_parts, _ = lax.optimization_barrier(([part for half in (first, second) for part, _ in half], sent_sum))
    own_rows = []
    for half, parts in ((first, own_parts[: len(first)]), (second, own_parts[len(first) :])):
        blocks = jnp.concatenate(
            [jnp.einsum("qt,krt->kqr", picked, part, preferred_element_type=F32) for part in parts]
        )
        offsets = [at for _, part_offsets in half for at in part_offsets]
        spots = jnp.stack(placed(offsets))
        own_rows.append(jnp.zeros_like(blocks).at[spots].set(blocks))
    own_hidden = jnp.concatenate(own_rows, axis=2).swapaxes(0, 1).reshape(token_count, model_width)
    return (own_hidden + routed_sum).astype(BF16)


def solution(mesh):
    in_specs = (
        P("dev", None, None),
        P("dev", "side", None),
        P("dev"),
        P("side", None, None),
        P("side", "dev"),
        P(("side", "dev"), None),
        P(),
        P(("side", "dev"), None),
        P(("side", "dev"), None),
        P("dev", None, None, "side"),
        P("dev", "side", None),
    )
    out_specs = P(("side", "dev"), None)
    return jax.shard_map(
        on_device, mesh=mesh, in_specs=in_specs, out_specs=out_specs, check_vma=False
    )
```
